256 devices in a mesh: gx: 16 (over x, y), gz: 8 (over z), gy: 2 (over core).
Axes of the slice: x: 4, y: 4, z: 8, core: 2. Of those that a mesh axis runs over, the one named last changes fastest.
Arguments:
- blocks: bfloat16 [16, 8, 4, 96, 4096], P('gx', 'gz', 'gy'), may hold values from -6 to 6
- block_count: int32 [16, 8, 2], P('gx', 'gz', 'gy'), may hold values from 1 to 2, as said below
- neighbours: int32 [16, 8, 4, 26], P('gx', 'gz', 'gy'), may hold values from -1 to 15, as said below
- conv_weight: bfloat16 [48, 2592], replicated, may hold values from -0.125 to 0.125
- conv_bias: float32 [48], replicated, may hold values from -3 to 3
- head_weight: bfloat16 [48, 48], replicated, may hold values from -0.875 to 0.875
- head_bias: float32 [48], replicated, may hold values from -3 to 3
Outputs:
- features: bfloat16 [16, 8, 4, 48, 4096], P('gx', 'gz', 'gy')
The draws below stay inside these ranges and needn't reach their ends.
Inputs may be any that keep to these rules, and one draw needn't show every extreme that they name: Each device's foreground blocks fill its first block_count slots; some device fills all 2. `neighbours`: -1 means no foreground block at that offset. Otherwise the value is u + 2 c: used slot u of the device reached from this one by the offset's steps along the axes whose bits are set in c (bit 0 x, bit 1 y, bit 2 z); bits are set only on axes where the offset is nonzero, and c = 0 names this device. Unused slots hold -1 everywhere. Each device's blocks sit at distinct positions of its own region of 2 x 2 x 4 block positions, and the links follow that geometry. The most is reached in every draw.
All inputs are finite; a program needn't handle non-finite values.
Results may differ from the reference program's by a relative error of at most 0.0046.
Values may be sent and summed in bfloat16 or wider, within the bound.
No kernel may reach another device: no remote copies, remote signals or barrier semaphores. Data moves between devices by JAX's collectives and lax.ppermute only.
A program may use at most 128 MiB of HBM per device.

```python
import jax
import jax.numpy as jnp
from jax import lax

CIN = 96
COUT = 48
EDGE = 16
VOX = 4096
SLOTS = 2
RX = 2
RY = 2
RZ = 4
N_GX = 16
N_GZ = 8
N_GY = 2


def permute_region(subkey):
    return jax.random.permutation(subkey, RX * RY * RZ)


def place_value(row, index, value):
    where_now = jnp.argmax((row == value).astype(jnp.int32)).astype(jnp.int32)
    current = row[index]
    return row.at[where_now].set(current).at[index].set(value)


def shared_layout(key):
    ndevices = N_GX * N_GZ * N_GY
    base = jax.random.fold_in(key, 4242)
    key_one, key_two, key_three, key_four = jax.random.split(base, 4)
    factor_one = jax.random.randint(key_one, (ndevices,), 0, SLOTS)
    factor_two = jax.random.randint(key_two, (ndevices,), 0, SLOTS)
    filled = 1 + factor_one * factor_two // max(SLOTS - 1, 1)
    chosen = jax.random.randint(key_three, (), 0, ndevices)
    corner_dev = (1 * N_GZ + 1) * N_GY + 1
    device_ids = jnp.arange(ndevices)
    filled = jnp.where((device_ids == chosen) | (device_ids == corner_dev), SLOTS, filled).astype(jnp.int32)
    ordering = jax.vmap(permute_region)(jax.random.split(key_four, ndevices)).astype(jnp.int32)
    first_row = place_value(ordering[0], 0, RX * RY * RZ - 1)
    ordering = ordering.at[0].set(first_row)
    corner_row = place_value(ordering[corner_dev], SLOTS - 1, 0)
    ordering = ordering.at[corner_dev].set(corner_row)
    inverse = jnp.argsort(ordering, axis=1).astype(jnp.int32)
    slot_of = jnp.where(inverse < filled[:, None], inverse, -1)
    device = jnp.arange(ndevices, dtype=jnp.int32)
    coord_y = jnp.broadcast_to((device % N_GY)[:, None], (ndevices, SLOTS))
    coord_z = jnp.broadcast_to((device // N_GY % N_GZ)[:, None], (ndevices, SLOTS))
    coord_x = jnp.broadcast_to((device // (N_GY * N_GZ))[:, None], (ndevices, SLOTS))
    position_id = ordering[:, :SLOTS]
    local_z = position_id % RZ
    local_y = position_id // RZ % RY
    local_x = position_id // (RZ * RY)
    used = jnp.arange(SLOTS)[None, :] < filled[:, None]
    region_sizes = [RX, RY, RZ]
    device_sizes = [N_GX, N_GY, N_GZ]
    columns = []
    for step_x in (-1, 0, 1):
        for step_y in (-1, 0, 1):
            for step_z in (-1, 0, 1):
                offsets = (step_x, step_y, step_z)
                if offsets == (0, 0, 0):
                    continue
                locals_now = [local_x, local_y, local_z]
                devices_now = [coord_x, coord_y, coord_z]
                present = used
                code = jnp.zeros_like(local_x)
                for axis_id in range(3):
                    if offsets[axis_id] == 0:
                        continue
                    stepped = locals_now[axis_id] + offsets[axis_id]
                    inside = (stepped >= 0) & (stepped < region_sizes[axis_id])
                    locals_now[axis_id] = stepped % region_sizes[axis_id]
                    devices_now[axis_id] = devices_now[axis_id] + jnp.where(inside, 0, offsets[axis_id])
                    code = code + jnp.where(inside, 0, 2 ** axis_id)
                    present = present & (devices_now[axis_id] >= 0) & (devices_now[axis_id] < device_sizes[axis_id])
                target_dev = (devices_now[0] * N_GZ + devices_now[2]) * N_GY + devices_now[1]
                target_dev = jnp.clip(target_dev, 0, ndevices - 1)
                target_pos = (locals_now[0] * RY + locals_now[1]) * RZ + locals_now[2]
                neighbour_slot = slot_of[target_dev, target_pos]
                encoded = jnp.where(present & (neighbour_slot >= 0), neighbour_slot + SLOTS * code, -1)
                columns.append(encoded)
    face_links = jnp.stack(columns, -1).astype(jnp.int32)
    return (filled.reshape(N_GX, N_GZ, N_GY), face_links.reshape(N_GX, N_GZ, N_GY * SLOTS, 26))


def draw_block_count(key, part):
    return shared_layout(key)[0]


def draw_neighbours(key, part):
    return shared_layout(key)[1]


def levels(key, extent, shards, smallest, largest):
    level = 1.0
    for axis_at, parts in shards:
        heights = jax.random.uniform(jax.random.fold_in(jax.random.fold_in(key, 6), axis_at), (parts,), jnp.float32, smallest / len(shards), largest / len(shards))
        level = level * jnp.repeat(jnp.exp(heights), extent[axis_at] // parts).reshape((-1,) + (1,) * (len(extent) - 1 - axis_at))
    return level


def centred(rng, dims, deviation, bound, shards=(), kind=jnp.bfloat16):
    drawn = jax.random.normal(rng, dims, jnp.float32) * deviation
    if len(shards) > 0:
        drawn = levels(rng, dims, shards, -0.22, 0.18) * drawn
    return jnp.clip(drawn, min=-bound, max=bound).astype(kind)


def setup_inputs(seed: int = 0) -> dict:
    streams_of = jax.random.split(jax.random.key(seed), 8)
    return {
        "blocks": centred(streams_of[0], (N_GX, N_GZ, N_GY * SLOTS, CIN, VOX), 1.0, 6.0, ((0, 16), (1, 8), (2, 2))),
        "block_count": draw_block_count(jax.random.fold_in(streams_of[7], 71), 0),
        "neighbours": draw_neighbours(jax.random.fold_in(streams_of[7], 71), 0),
        "conv_weight": centred(streams_of[3], (COUT, 27 * CIN), (27 * CIN) ** -0.5, 0.125),
        "conv_bias": centred(streams_of[4], (COUT,), 0.5, 3.0, (), jnp.float32),
        "head_weight": centred(streams_of[5], (COUT, COUT), COUT ** -0.5, 0.875),
        "head_bias": centred(streams_of[6], (COUT,), 0.5, 3.0, (), jnp.float32),
    }


def offset_list():
    return [(step_x, step_y, step_z) for step_x in (-1, 0, 1) for step_y in (-1, 0, 1) for step_z in (-1, 0, 1)]


def edge_piece(volume, offsets, first_axis):
    piece = volume
    for axis_id in range(3):
        dim = first_axis + axis_id
        length = piece.shape[dim]
        if offsets[axis_id] == -1:
            piece = lax.slice_in_dim(piece, length - 1, length, axis=dim)
        elif offsets[axis_id] == 1:
            piece = lax.slice_in_dim(piece, 0, 1, axis=dim)
    return piece


def assemble(pieces, first_axis):
    layers_x = []
    for step_x in (-1, 0, 1):
        layers_y = []
        for step_y in (-1, 0, 1):
            layers_y.append(jnp.concatenate([pieces[(step_x, step_y, step_z)] for step_z in (-1, 0, 1)], first_axis + 2))
        layers_x.append(jnp.concatenate(layers_y, first_axis + 1))
    return jnp.concatenate(layers_x, first_axis)


def convolve_padded(padded, conv_weight, conv_bias, head_weight, head_bias):
    channels = padded.shape[0]
    edge = padded.shape[1] - 2
    total = jnp.zeros((conv_weight.shape[0], edge * edge * edge), jnp.float32)
    for tap, offsets in enumerate(offset_list()):
        view = padded[:, 1 + offsets[0]:1 + offsets[0] + edge, 1 + offsets[1]:1 + offsets[1] + edge,
                      1 + offsets[2]:1 + offsets[2] + edge]
        total = total + jnp.dot(conv_weight[:, tap * channels:(tap + 1) * channels], view.reshape(channels, -1),
                                preferred_element_type=jnp.float32)
    hidden = jnp.maximum(total + conv_bias[:, None], 0.0).astype(jnp.bfloat16)
    mixed = jnp.dot(head_weight, hidden, preferred_element_type=jnp.float32) + head_bias[:, None]
    return mixed.astype(jnp.bfloat16)


def reference(blocks, block_count, neighbours, conv_weight, conv_bias, head_weight, head_bias):
    flat_blocks = blocks.reshape(-1, CIN, EDGE, EDGE, EDGE)
    face_links = neighbours.reshape(-1, 26)
    filled = block_count.reshape(-1)
    block_total = flat_blocks.shape[0]

    def compute_one(position):
        device = position // SLOTS
        slot_id = position % SLOTS
        coord_y = device % N_GY
        coord_z = (device // N_GY) % N_GZ
        coord_x = device // (N_GY * N_GZ)

        def active():
            volume = lax.dynamic_index_in_dim(flat_blocks, position, 0, keepdims=False)
            pieces = {(0, 0, 0): volume}
            link_index = 0
            for offsets in offset_list():
                if offsets == (0, 0, 0):
                    continue
                encoded = face_links[position, link_index]
                link_index += 1
                clean = jnp.maximum(encoded, 0)
                code = clean // SLOTS
                source_slot = clean % SLOTS
                target = [coord_x, coord_y, coord_z]
                for axis_id in range(3):
                    crossed = (code // (2 ** axis_id)) % 2
                    target[axis_id] = target[axis_id] + offsets[axis_id] * crossed
                source_dev = (target[0] * N_GZ + target[2]) * N_GY + target[1]
                source = jnp.clip(source_dev * SLOTS + source_slot, 0, block_total - 1).astype(jnp.int32)
                neighbour = lax.dynamic_index_in_dim(flat_blocks, source, 0, keepdims=False)
                face_piece = edge_piece(neighbour, offsets, 1)
                pieces[offsets] = jnp.where(encoded >= 0, face_piece, jnp.zeros_like(face_piece))
            padded = assemble(pieces, 1)
            return convolve_padded(padded, conv_weight, conv_bias, head_weight, head_bias)

        def vacant():
            return jnp.zeros((COUT, VOX), jnp.bfloat16)

        return lax.cond(slot_id < filled[device], active, vacant)

    results = lax.map(compute_one, jnp.arange(block_total, dtype=jnp.int32))
    return results.reshape(N_GX, N_GZ, N_GY * SLOTS, COUT, VOX)
```

```python
import jax
import jax.numpy as jnp
from jax import lax
from jax.experimental import pallas as pl
from jax.experimental.pallas import tpu as pltpu
from jax.sharding import PartitionSpec as P

CIN = 96
COUT = 48
EDGE = 16
PLANE = 256
VOX = 4096
SLOTS = 2
TAPS = 9
BF = jnp.bfloat16
F32 = jnp.float32

OWN_X = 0
FAR_X = 4
FAR_Y = 8
OWN_Y = 10
OWN_Z = 14
FAR_Z = 18
EDGE_Z = 22
EDGE_Y = 24
TURN_Z = 28
SOURCES = 32


def params(mib):
    return pltpu.CompilerParams(vmem_limit_bytes=mib * 2**20)


def lanes(rows, width):
    return lax.broadcasted_iota(jnp.int32, (rows, width), 1)


def last(side):
    return EDGE - 1 if side == 0 else 0


def roll(value, shift):
    width = value.shape[1]
    if isinstance(shift, int):
        shift = shift % width
        if shift == 0:
            return value
    return pltpu.roll(value, shift, 1)


def interior(block, wall, columns, write):
    lane = lanes(CIN, PLANE)
    z_of = lane % EDGE
    z_first, z_last = z_of == 0, z_of == EDGE - 1
    y_first, y_last = lane < EDGE, lane >= PLANE - EDGE
    zero = jnp.zeros((CIN, PLANE), BF)
    before = current = None
    for x in range(EDGE):
        centre = block(x)
        z_less = jnp.where(z_first, zero, roll(centre, 1))
        z_more = jnp.where(z_last, zero, roll(centre, -1))
        buffer = x % 2
        for tap_z, value in enumerate((z_less, centre, z_more)):
            for tap_y in range(3):
                if tap_y == 0:
                    shifted = jnp.where(y_first, zero, roll(value, EDGE))
                elif tap_y == 1:
                    shifted = value
                else:
                    shifted = jnp.where(y_last, zero, roll(value, -EDGE))
                start = (tap_y * 3 + tap_z) * CIN
                columns[buffer, start : start + CIN, :] = shifted
        part = jnp.dot(wall[...], columns[buffer], preferred_element_type=F32)
        if x > 0:
            write(x - 1, before + part[2 * COUT :])
            before = current + part[COUT : 2 * COUT]
        else:
            before = part[COUT : 2 * COUT]
        current = part[:COUT]
    write(EDGE - 1, before)


def write_plane(acc):
    def write(x, value):
        acc[:, x * PLANE : (x + 1) * PLANE] = value

    return write


def pack_and_convolve(blocks, weight, faces_y, faces_z, acc, wall, columns):
    for tap_x in range(3):
        wall[tap_x * COUT : (tap_x + 1) * COUT, :] = weight[
            :, tap_x * TAPS * CIN : (tap_x + 1) * TAPS * CIN
        ]
    lane = lanes(CIN, PLANE)
    half_lane = lanes(CIN, 128)
    for slot in range(SLOTS):
        for side in range(2):
            plane_z = jnp.zeros((CIN, PLANE), BF)
            halves = [jnp.zeros((CIN, 128), BF), jnp.zeros((CIN, 128), BF)]
            for x in range(EDGE):
                centre = blocks[slot, :, x * PLANE : (x + 1) * PLANE]
                plane_z = jnp.where(lane % EDGE == x, roll(centre, x - last(side)), plane_z)
                half = centre[:, 128:] if side == 0 else centre[:, :128]
                at = (x % 8) * EDGE
                moved = roll(half, at - (112 if side == 0 else 0))
                halves[x // 8] = jnp.where(half_lane // EDGE == x % 8, moved, halves[x // 8])
            faces_z[side * 2 + slot] = plane_z
            faces_y[side * 2 + slot, :, :128] = halves[0]
            faces_y[side * 2 + slot, :, 128:] = halves[1]
    interior(
        lambda x: blocks[0, :, x * PLANE : (x + 1) * PLANE], wall, columns, write_plane(acc)
    )


def convolve_second(blocks, wall, tie, acc, columns):
    interior(
        lambda x: blocks[0, :, x * PLANE : (x + 1) * PLANE], wall, columns, write_plane(acc)
    )


def pack_for_y(place, faces_y, far_a, far_b, out):
    odd_x, at_y = place[0] == 1, place[2]
    for slot in range(SLOTS):
        out[slot, :, :PLANE] = faces_y[at_y * 2 + slot]
        start = pl.multiple_of((1 - at_y) * 128, 128)
        a = far_a[slot, :, pl.ds(start, 128)]
        b = far_b[slot, :, pl.ds(start, 128)]
        out[slot, :, PLANE : PLANE + 128] = jnp.where(odd_x, a, b)
        out[slot, :, PLANE + 128 :] = jnp.where(odd_x, b, a)


def pack_for_z(place, faces_z, far_a, far_b, far_y, out_a, out_b):
    odd_x, odd_z, at_y = place[0] == 1, place[1] == 1, place[2]
    lane = lanes(CIN, PLANE)
    half_lane = lanes(CIN, 128)
    row = at_y * 112
    packs = []
    for side in range(2):
        z = last(side)
        pack = jnp.zeros((CIN, PLANE), BF)
        corner = jnp.zeros((CIN, 128), BF)
        for slot in range(SLOTS):
            a, b = far_a[slot], far_b[slot]
            pair = (jnp.where(odd_x, a, b), jnp.where(odd_x, b, a))
            for d in range(2):
                k = d * 2 + slot
                pack = jnp.where(lane % EDGE == k, roll(pair[d], k - z), pack)
                edge = far_y[slot, :, PLANE + d * 128 : PLANE + (d + 1) * 128]
                moved = pltpu.roll(edge, (6 + k - z - row) % 128, 1)
                corner = jnp.where(half_lane == 6 + k, moved, corner)
            k = 4 + slot
            pack = jnp.where(lane % EDGE == k, roll(far_y[slot, :, :PLANE], k - z), pack)
        low = jnp.where((half_lane >= 6) & (half_lane < 10), corner, pack[:, :128])
        packs.append((low, pack[:, 128:]))
    first, second = packs
    for part in range(2):
        at = slice(part * 128, (part + 1) * 128)
        out_a[2, :, at] = jnp.where(odd_z, second[part], first[part])
        out_b[2, :, at] = jnp.where(odd_z, first[part], second[part])
    for slot in range(SLOTS):
        out_a[slot] = faces_z[place[1] * 2 + slot]
        out_b[slot] = faces_z[(1 - place[1]) * 2 + slot]


def pick(code, choices):
    result = choices[-1][1]
    for known, value in reversed(choices[:-1]):
        result = jnp.where(code == known, value, result)
    return result


def finish(
    place, links, count, acc_a, acc_b, own_a, own_b, far_a, far_b, faces_y, far_y, faces_z,
    got_a, got_b, wall, bias, head, head_bias, turn, out, table, columns, extra
):
    odd_x, odd_z = place[0] == 1, place[1] == 1
    lane = lanes(CIN, PLANE)
    z_of = lane % EDGE
    z_first, z_last = z_of == 0, z_of == EDGE - 1
    y_first, y_last = lane < EDGE, lane >= PLANE - EDGE
    half_lane = lanes(CIN, 128)
    zero = jnp.zeros((CIN, PLANE), BF)
    half_zero = jnp.zeros((CIN, 128), BF)
    for slot in range(SLOTS):
        a, b = own_a[slot], own_b[slot]
        table[OWN_X + slot] = jnp.where(odd_x, b, a)
        table[OWN_X + 2 + slot] = jnp.where(odd_x, a, b)
        a, b = far_a[slot], far_b[slot]
        table[FAR_X + slot] = jnp.where(odd_x, a, b)
        table[FAR_X + 2 + slot] = jnp.where(odd_x, b, a)
        table[FAR_Y + slot] = far_y[slot, :, :PLANE]
        a, b = got_a[slot], got_b[slot]
        table[FAR_Z + slot] = jnp.where(odd_z, a, b)
        table[FAR_Z + 2 + slot] = jnp.where(odd_z, b, a)
        for d in range(2):
            table[OWN_Y + d * 2 + slot] = faces_y[d * 2 + slot]
            table[OWN_Z + d * 2 + slot] = faces_z[d * 2 + slot]
            table[EDGE_Y + d * 2 + slot, :, :128] = far_y[
                slot, :, PLANE + d * 128 : PLANE + (d + 1) * 128
            ]
            table[EDGE_Y + d * 2 + slot, :, 128:] = half_zero
    a, b = got_a[2], got_b[2]
    table[EDGE_Z] = jnp.where(odd_z, a, b)
    table[EDGE_Z + 1] = jnp.where(odd_z, b, a)
    for k in range(4):
        table[TURN_Z + k] = jnp.dot(
            table[FAR_Z + k], turn[...], preferred_element_type=F32
        ).astype(BF)

    def link(slot, dx, dy, dz):
        index = (dx + 1) * 9 + (dy + 1) * 3 + dz + 1
        value = links[slot, index if index < 13 else index - 1]
        clean = jnp.maximum(value, 0)
        return value >= 0, clean // 2, clean % 2

    def whole(present, index):
        return jnp.where(present, table[index], zero)

    def column(present, index, source, side):
        target = 0 if side == 0 else EDGE - 1
        moved = pltpu.roll(table[index], (target - source + PLANE) % PLANE, 1)
        return jnp.where(present, moved, zero)

    def short(present, index, source, target):
        start = pl.multiple_of((source // 128) * 128, 128)
        value = table[index, :, pl.ds(start, 128)]
        moved = pltpu.roll(value, (target - source % 128 + 128) % 128, 1)
        return jnp.where(present, moved, half_zero)

    def sign(side):
        return -1 if side == 0 else 1

    accs = (acc_a, acc_b)
    lane_o = lanes(COUT, PLANE)
    half_o = lanes(COUT, 128)
    none = jnp.zeros((COUT, PLANE), F32)
    for slot in range(SLOTS):
        acc = accs[slot]
        for d in range(2):
            present, code, u = link(slot, sign(d), 0, 0)
            centre = whole(present, code * 4 + d * 2 + u)
            sides = []
            for f in range(2):
                present, code, u = link(slot, sign(d), 0, sign(f))
                index = pick(
                    code,
                    (
                        (0, d * 2 + u),
                        (1, FAR_X + d * 2 + u),
                        (4, FAR_Z + f * 2 + u),
                        (5, EDGE_Z + f),
                    ),
                )
                source = pick(code, ((0, last(f)), (1, last(f)), (4, last(d)), (5, d * 2 + u)))
                sides.append(column(present, index, source, f))
            z_less = jnp.where(z_first, sides[0], roll(centre, 1))
            z_more = jnp.where(z_last, sides[1], roll(centre, -1))
            rows = []
            for e in range(2):
                present, code, u = link(slot, sign(d), sign(e), 0)
                index = pick(
                    code,
                    (
                        (0, d * 2 + u),
                        (1, FAR_X + d * 2 + u),
                        (2, FAR_Y + u),
                        (3, EDGE_Y + d * 2 + u),
                    ),
                )
                far = 112 if e == 0 else 0
                source = pick(
                    code,
                    ((0, last(e) * EDGE), (1, last(e) * EDGE), (2, last(d) * EDGE), (3, far)),
                )
                row = short(present, index, source, 0)
                for f in range(2):
                    present, code, u = link(slot, sign(d), sign(e), sign(f))
                    index = pick(
                        code,
                        (
                            (0, d * 2 + u),
                            (1, FAR_X + d * 2 + u),
                            (2, FAR_Y + u),
                            (3, EDGE_Y + d * 2 + u),
                            (4, FAR_Z + f * 2 + u),
                            (5, EDGE_Z + f),
                        ),
                    )
                    source = pick(
                        code,
                        (
                            (0, last(e) * EDGE + last(f)),
                            (1, last(e) * EDGE + last(f)),
                            (2, last(d) * EDGE + last(f)),
                            (3, far + last(f)),
                            (4, last(e) * EDGE + last(d)),
                            (5, last(e) * EDGE + d * 2 + u),
                            (6, last(d) * EDGE + 4 + u),
                            (7, 6 + d * 2 + u),
                        ),
                    )
                    target = 127 if f == 0 else EDGE
                    row = jnp.where(half_lane == target, short(present, index, source, target), row)
                rows.append(row)
            for tap_z, value in enumerate((z_less, centre, z_more)):
                low, high = roll(rows[0], 1 - tap_z), roll(rows[1], 1 - tap_z)
                for tap_y in range(3):
                    start = (tap_y * 3 + tap_z) * CIN
                    if tap_y == 1:
                        columns[d, start : start + CIN, :] = value
                    elif tap_y == 0:
                        shifted = roll(value, EDGE)
                        columns[d, start : start + CIN, :128] = jnp.where(
                            half_lane < EDGE, low, shifted[:, :128]
                        )
                        columns[d, start : start + CIN, 128:] = shifted[:, 128:]
                    else:
                        shifted = roll(value, -EDGE)
                        columns[d, start : start + CIN, :128] = shifted[:, :128]
                        columns[d, start : start + CIN, 128:] = jnp.where(
                            half_lane >= 112, roll(high, 112), shifted[:, 128:]
                        )
            x = 0 if d == 0 else EDGE - 1
            at = slice(x * PLANE, (x + 1) * PLANE)
            taps = wall[2 * d * COUT : (2 * d + 1) * COUT, :]
            extra[:, at] = acc[:, at] + jnp.dot(taps, columns[d], preferred_element_type=F32)
        sheets_y = []
        for e in range(2):
            present, code, u = link(slot, 0, sign(e), 0)
            centre = whole(present, pick(code, ((0, OWN_Y + e * 2 + u), (2, FAR_Y + u))))
            sides = []
            for f in range(2):
                present, code, u = link(slot, 0, sign(e), sign(f))
                index = pick(
                    code,
                    (
                        (0, OWN_Y + e * 2 + u),
                        (2, FAR_Y + u),
                        (4, TURN_Z + f * 2 + u),
                        (6, EDGE_Z + f),
                    ),
                )
                source = pick(code, ((0, last(f)), (2, last(f)), (4, last(e)), (6, 4 + u)))
                sides.append(column(present, index, source, f))
            columns[e, :CIN, :] = jnp.where(z_first, sides[0], roll(centre, 1))
            columns[e, CIN : 2 * CIN, :] = centre
            columns[e, 2 * CIN : 3 * CIN, :] = jnp.where(z_last, sides[1], roll(centre, -1))
            taps = wall[:, 2 * e * 3 * CIN : (2 * e + 1) * 3 * CIN]
            part = jnp.dot(taps, columns[e, : 3 * CIN, :], preferred_element_type=F32)
            sheet = part[COUT : 2 * COUT]
            sheet = sheet + jnp.where(lane_o < EDGE, none, roll(part[:COUT], EDGE))
            sheet = sheet + jnp.where(
                lane_o >= PLANE - EDGE, none, roll(part[2 * COUT :], -EDGE)
            )
            sheets_y.append(sheet)
        sheets_z = []
        for f in range(2):
            present, code, u = link(slot, 0, 0, sign(f))
            centre = whole(present, pick(code, ((0, OWN_Z + f * 2 + u), (4, FAR_Z + f * 2 + u))))
            part = jnp.zeros((3 * COUT, PLANE), F32)
            for tap_y in range(3):
                if tap_y == 0:
                    value = jnp.where(y_first, zero, roll(centre, EDGE))
                elif tap_y == 1:
                    value = centre
                else:
                    value = jnp.where(y_last, zero, roll(centre, -EDGE))
                columns[f, tap_y * CIN : (tap_y + 1) * CIN, :] = value
            taps = jnp.concatenate(
                [
                    wall[:, (tap_y * 3 + 2 * f) * CIN : (tap_y * 3 + 2 * f + 1) * CIN]
                    for tap_y in range(3)
                ],
                1,
            )
            part = jnp.dot(taps, columns[f, : 3 * CIN, :], preferred_element_type=F32)
            sheet = part[COUT : 2 * COUT]
            sheet = sheet + jnp.where(lane_o % EDGE == 0, none, roll(part[:COUT], 1))
            sheet = sheet + jnp.where(
                lane_o % EDGE == EDGE - 1, none, roll(part[2 * COUT :], -1)
            )
            sheets_z.append(sheet)
        used = slot < count[0]
        half_none = jnp.zeros((COUT, 128), F32)
        for x in range(EDGE):
            at = slice(x * PLANE, (x + 1) * PLANE)
            total = extra[:, at] if x in (0, EDGE - 1) else acc[:, at]
            total = total + jnp.where(lane_o % EDGE == 0, roll(sheets_z[0], -x), none)
            total = total + jnp.where(
                lane_o % EDGE == EDGE - 1, roll(sheets_z[1], EDGE - 1 - x), none
            )
            from_half = slice((x // 8) * 128, (x // 8 + 1) * 128)
            low = roll(sheets_y[0][:, from_half], -(x % 8) * EDGE)
            high = roll(sheets_y[1][:, from_half], 112 - (x % 8) * EDGE)
            low = total[:, :128] + jnp.where(half_o < EDGE, low, half_none)
            high = total[:, 128:] + jnp.where(half_o >= 112, high, half_none)
            for part, value in enumerate((low, high)):
                hidden = jnp.maximum(value + bias[...], 0.0).astype(BF)
                mixed = jnp.dot(head[...], hidden, preferred_element_type=F32) + head_bias[...]
                out[slot, :, x * PLANE + part * 128 : x * PLANE + (part + 1) * 128] = jnp.where(
                    used, mixed, half_none
                ).astype(BF)


SMEM = pl.BlockSpec(memory_space=pltpu.SMEM)
VMEM = pl.BlockSpec(memory_space=pltpu.VMEM)


def shape(dims, kind=BF):
    return jax.ShapeDtypeStruct(dims, kind)


def swap(first, second, axis):
    length = lax.axis_size(axis)
    even = [(i, i ^ 1) for i in range(length)]
    odd = [(i, ((i + 1) ^ 1) - 1) for i in range(1, length - 1)]
    return lax.ppermute(first, axis, even), lax.ppermute(second, axis, odd)


def body(blocks, block_count, neighbours, conv_weight, conv_bias, head_weight, head_bias):
    volumes = blocks.reshape(SLOTS, CIN, VOX)
    count = block_count.reshape(1)
    links = neighbours.reshape(SLOTS, 26)
    odd_x = lax.axis_index("gx") % 2
    odd_z = lax.axis_index("gz") % 2
    place = jnp.stack([odd_x, odd_z, lax.axis_index("gy")]).astype(jnp.int32)
    far_end = VOX - PLANE
    own_a = lax.dynamic_slice_in_dim(volumes, (1 - odd_x) * far_end, PLANE, 2)
    own_b = lax.dynamic_slice_in_dim(volumes, odd_x * far_end, PLANE, 2)
    far_a, far_b = swap(own_a, own_b, "gx")
    buffer = pltpu.VMEM((2, TAPS * CIN, PLANE), BF)
    faces_y, faces_z, acc_a, wall = pl.pallas_call(
        pack_and_convolve,
        out_shape=(
            shape((4, CIN, PLANE)),
            shape((4, CIN, PLANE)),
            shape((COUT, VOX), F32),
            shape((3 * COUT, TAPS * CIN)),
        ),
        in_specs=[VMEM, VMEM],
        out_specs=(VMEM, VMEM, VMEM, VMEM),
        scratch_shapes=[buffer],
        compiler_params=params(16),
        cost_estimate=pl.CostEstimate(
            flops=2 * COUT * 27 * CIN * VOX, bytes_accessed=4 * 2**20, transcendentals=0
        ),
    )(volumes, conv_weight)
    sent_y = pl.pallas_call(
        pack_for_y,
        out_shape=shape((SLOTS, CIN, 2 * PLANE)),
        in_specs=[SMEM, VMEM, VMEM, VMEM],
        out_specs=VMEM,
        compiler_params=params(8),
    )(place, faces_y, far_a, far_b)
    far_y = lax.ppermute(sent_y, "gy", [(0, 1), (1, 0)])
    sent_a, sent_b = pl.pallas_call(
        pack_for_z,
        out_shape=(shape((3, CIN, PLANE)), shape((3, CIN, PLANE))),
        in_specs=[SMEM, VMEM, VMEM, VMEM, VMEM],
        out_specs=(VMEM, VMEM),
        compiler_params=params(8),
    )(place, faces_z, far_a, far_b, far_y)
    got_a, got_b = swap(sent_a, sent_b, "gz")
    acc_b = pl.pallas_call(
        convolve_second,
        grid=(1,),
        out_shape=shape((COUT, VOX), F32),
        in_specs=[
            pl.BlockSpec((1, CIN, VOX), lambda i: (1, 0, 0)),
            VMEM,
            pl.BlockSpec(memory_space=pl.ANY),
        ],
        out_specs=VMEM,
        scratch_shapes=[buffer],
        compiler_params=params(16),
        cost_estimate=pl.CostEstimate(
            flops=2 * COUT * 27 * CIN * VOX, bytes_accessed=2 * 2**20, transcendentals=0
        ),
    )(volumes, wall, sent_a)
    index = jnp.arange(PLANE)
    turn = (index[:, None] == (index % EDGE * EDGE + index // EDGE)[None, :]).astype(BF)
    outputs = pl.pallas_call(
        finish,
        out_shape=shape((SLOTS, COUT, VOX)),
        in_specs=[SMEM] * 3 + [VMEM] * 16,
        out_specs=VMEM,
        scratch_shapes=[
            pltpu.VMEM((SOURCES, CIN, PLANE), BF),
            buffer,
            pltpu.VMEM((COUT, VOX), F32),
        ],
        compiler_params=params(24),
    )(
        place, links, count, acc_a, acc_b, own_a, own_b, far_a, far_b, faces_y, far_y, faces_z,
        got_a, got_b, wall, conv_bias.reshape(COUT, 1), head_weight,
        head_bias.reshape(COUT, 1), turn,
    )
    return outputs.reshape(1, 1, SLOTS, COUT, VOX)


def solution(mesh):
    placed = (
        P("gx", "gz", "gy", None, None),
        P("gx", "gz", "gy"),
        P("gx", "gz", "gy", None),
        P(),
        P(),
        P(),
        P(),
    )
    return jax.shard_map(
        body, mesh=mesh, in_specs=placed, out_specs=P("gx", "gz", "gy", None, None), check_vma=False
    )
```

```python
import jax
import jax.numpy as jnp
from jax import lax
from jax.experimental import pallas as pl
from jax.experimental.pallas import tpu as pltpu
from jax.sharding import PartitionSpec as P

CIN = 96
COUT = 48
EDGE = 16
PLANE = 256
VOX = 4096
SLOTS = 2
TAPS = 9
BF = jnp.bfloat16
F32 = jnp.float32

OWN_X, FAR_X, FAR_Y, OWN_Y, EDGE_Y, NEAR_SOURCES = 0, 4, 8, 10, 14, 18
FAR_Z, EDGE_Z, TURN_Z, Z_SOURCES = 0, 4, 6, 8
SPLIT = 5
CHUNK = 4


def params(mib):
    return pltpu.CompilerParams(vmem_limit_bytes=mib * 2**20)


def lanes(rows, width):
    return lax.broadcasted_iota(jnp.int32, (rows, width), 1)


def last(side):
    return EDGE - 1 if side == 0 else 0


def roll(value, shift):
    width = value.shape[1]
    if isinstance(shift, int):
        shift = shift % width
        if shift == 0:
            return value
    return pltpu.roll(value, shift, 1)


def place():
    return lax.axis_index("gx") % 2, lax.axis_index("gz") % 2, lax.axis_index("gy")


def interior(block, wall, columns, write, first, stop, carry=None):
    lane = lanes(CIN, PLANE)
    z_of = lane % EDGE
    z_first, z_last = z_of == 0, z_of == EDGE - 1
    y_first, y_last = lane < EDGE, lane >= PLANE - EDGE
    zero = jnp.zeros((CIN, PLANE), BF)
    before, current = carry if carry is not None else (None, None)
    for x in range(first, stop):
        centre = block(x)
        z_less = jnp.where(z_first, zero, roll(centre, 1))
        z_more = jnp.where(z_last, zero, roll(centre, -1))
        buffer = x % 2
        for tap_z, value in enumerate((z_less, centre, z_more)):
            for tap_y in range(3):
                if tap_y == 0:
                    shifted = jnp.where(y_first, zero, roll(value, EDGE))
                elif tap_y == 1:
                    shifted = value
                else:
                    shifted = jnp.where(y_last, zero, roll(value, -EDGE))
                start = (tap_y * 3 + tap_z) * CIN
                columns[buffer, start : start + CIN, :] = shifted
        part = jnp.dot(wall[...], columns[buffer], preferred_element_type=F32)
        if x > 0:
            write(x - 1, before + part[2 * COUT :])
            before = current + part[COUT : 2 * COUT]
        else:
            before = part[COUT : 2 * COUT]
        current = part[:COUT]
    if stop == EDGE:
        write(EDGE - 1, before)
    return before, current


def write_plane(acc):
    def write(x, value):
        acc[:, x * PLANE : (x + 1) * PLANE] = value

    return write


def plane_of(block):
    return lambda x: block[:, x * PLANE : (x + 1) * PLANE]


def pack_and_convolve(blocks, weight, held, faces_y, faces_z, acc, wall, columns, first, weights, sems, weight_sem):
    width = VOX // CHUNK
    copies = []
    for slot in range(SLOTS):
        for part in range(CHUNK):
            at = pl.ds(part * width, width)
            copies.append(
                pltpu.make_async_copy(
                    blocks.at[slot, :, at], (first, held)[slot].at[:, at], sems.at[slot * CHUNK + part]
                )
            )
    weight_copy = pltpu.make_async_copy(weight, weights, weight_sem)
    copies[0].start()
    weight_copy.start()
    for copy in copies[1:]:
        copy.start()
    lane = lanes(CIN, PLANE)
    half_lane = lanes(CIN, 128)
    for slot in range(SLOTS):
        planes_z = [jnp.zeros((CIN, PLANE), BF)] * 2
        halves = [[jnp.zeros((CIN, 128), BF)] * 2 for _ in range(2)]
        for x in range(EDGE):
            if x % (EDGE // CHUNK) == 0:
                copies[slot * CHUNK + x // (EDGE // CHUNK)].wait()
            centre = (first, held)[slot][:, x * PLANE : (x + 1) * PLANE]
            for side in range(2):
                planes_z[side] = jnp.where(
                    lane % EDGE == x, roll(centre, x - last(side)), planes_z[side]
                )
                half = centre[:, 128:] if side == 0 else centre[:, :128]
                at = (x % 8) * EDGE
                moved = roll(half, at - (112 if side == 0 else 0))
                halves[side][x // 8] = jnp.where(
                    half_lane // EDGE == x % 8, moved, halves[side][x // 8]
                )
        for side in range(2):
            faces_z[side * 2 + slot] = planes_z[side]
            faces_y[side * 2 + slot, :, :128] = halves[side][0]
            faces_y[side * 2 + slot, :, 128:] = halves[side][1]
        if slot == 0:
            weight_copy.wait()
            for tap_x in range(3):
                wall[tap_x * COUT : (tap_x + 1) * COUT, :] = weights[
                    :, tap_x * TAPS * CIN : (tap_x + 1) * TAPS * CIN
                ]
            interior(plane_of(first), wall, columns, write_plane(acc), 0, EDGE)


def begin_second(held, wall, tie, acc, carry, columns):
    before, current = interior(plane_of(held), wall, columns, write_plane(acc), 0, SPLIT)
    carry[0], carry[1] = before, current


def pack_for_y(faces_y, far_a, far_b, out):
    parity, _, at_y = place()
    odd_x = parity == 1
    for slot in range(SLOTS):
        out[slot, :, :PLANE] = faces_y[at_y * 2 + slot]
        start = pl.multiple_of((1 - at_y) * 128, 128)
        a = far_a[slot, :, pl.ds(start, 128)]
        b = far_b[slot, :, pl.ds(start, 128)]
        out[slot, :, PLANE : PLANE + 128] = jnp.where(odd_x, a, b)
        out[slot, :, PLANE + 128 :] = jnp.where(odd_x, b, a)


def pack_for_z(faces_z, far_a, far_b, far_y, out_a, out_b):
    parity_x, parity_z, at_y = place()
    odd_x, odd_z = parity_x == 1, parity_z == 1
    lane = lanes(CIN, PLANE)
    half_lane = lanes(CIN, 128)
    row = at_y * 112
    packs = []
    for side in range(2):
        z = last(side)
        pack = jnp.zeros((CIN, PLANE), BF)
        corner = jnp.zeros((CIN, 128), BF)
        for slot in range(SLOTS):
            a, b = far_a[slot], far_b[slot]
            pair = (jnp.where(odd_x, a, b), jnp.where(odd_x, b, a))
            for d in range(2):
                k = d * 2 + slot
                pack = jnp.where(lane % EDGE == k, roll(pair[d], k - z), pack)
                edge = far_y[slot, :, PLANE + d * 128 : PLANE + (d + 1) * 128]
                moved = pltpu.roll(edge, (6 + k - z - row + 128) % 128, 1)
                corner = jnp.where(half_lane == 6 + k, moved, corner)
            k = 4 + slot
            pack = jnp.where(lane % EDGE == k, roll(far_y[slot, :, :PLANE], k - z), pack)
        low = jnp.where((half_lane >= 6) & (half_lane < 10), corner, pack[:, :128])
        packs.append((low, pack[:, 128:]))
    first, second = packs
    for part in range(2):
        at = slice(part * 128, (part + 1) * 128)
        out_a[2, :, at] = jnp.where(odd_z, second[part], first[part])
        out_b[2, :, at] = jnp.where(odd_z, first[part], second[part])
    for slot in range(SLOTS):
        out_a[slot] = faces_z[parity_z * 2 + slot]
        out_b[slot] = faces_z[(1 - parity_z) * 2 + slot]


def pick(code, choices):
    result = choices[-1][1]
    for known, value in reversed(choices[:-1]):
        result = jnp.where(code == known, value, result)
    return result


def sign(side):
    return -1 if side == 0 else 1


def link(links, slot, dx, dy, dz):
    index = (dx + 1) * 9 + (dy + 1) * 3 + dz + 1
    value = links[slot, index if index < 13 else index - 1]
    clean = jnp.maximum(value, 0)
    return value >= 0, clean // 2, clean % 2


def whole(table, present, index):
    return jnp.where(present, table[index], jnp.zeros((CIN, PLANE), BF))


def column(table, present, index, source, side):
    target = 0 if side == 0 else EDGE - 1
    moved = pltpu.roll(table[index], (target - source + PLANE) % PLANE, 1)
    return jnp.where(present, moved, jnp.zeros((CIN, PLANE), BF))


def short(table, present, index, source, target):
    start = pl.multiple_of((source // 128) * 128, 128)
    value = table[index, :, pl.ds(start, 128)]
    moved = pltpu.roll(value, (target - source % 128 + 128) % 128, 1)
    return jnp.where(present, moved, jnp.zeros((CIN, 128), BF))


def put_corner(row, side, value):
    return jnp.where(lanes(CIN, 128) == (127 if side == 0 else EDGE), value, row)


def fill_columns(columns, buffer, centre, sides, rows):
    lane = lanes(CIN, PLANE)
    half_lane = lanes(CIN, 128)
    less = jnp.where(lane % EDGE == 0, sides[0], roll(centre, 1))
    more = jnp.where(lane % EDGE == EDGE - 1, sides[1], roll(centre, -1))
    for minor, value in enumerate((less, centre, more)):
        low, high = roll(rows[0], 1 - minor), roll(rows[1], 113 - minor)
        for major in range(3):
            start = (major * 3 + minor) * CIN
            at = slice(start, start + CIN)
            if major == 1:
                columns[buffer, at, :] = value
            elif major == 0:
                shifted = roll(value, EDGE)
                columns[buffer, at, :128] = jnp.where(half_lane < EDGE, low, shifted[:, :128])
                columns[buffer, at, 128:] = shifted[:, 128:]
            else:
                shifted = roll(value, -EDGE)
                columns[buffer, at, :128] = shifted[:, :128]
                columns[buffer, at, 128:] = jnp.where(half_lane >= 112, high, shifted[:, 128:])


def finish_second(
    links, held, wall, tie, carry, part_acc, own_a, own_b, far_a, far_b, faces_y, far_y, faces_z,
    acc, walls_z, sheets_x, sheets_y, sheets_z, columns, table
):
    parity_x, _, _ = place()
    odd_x = parity_x == 1
    for x in range(SPLIT - 1):
        at = slice(x * PLANE, (x + 1) * PLANE)
        acc[:, at] = part_acc[:, at]
    interior(
        plane_of(held), wall, columns, write_plane(acc), SPLIT, EDGE, (carry[0], carry[1])
    )
    for f in range(2):
        for tap_y in range(3):
            for tap_x in range(3):
                start = (tap_y * 3 + tap_x) * CIN
                source = (tap_y * 3 + 2 * f) * CIN
                walls_z[f, :, start : start + CIN] = wall[
                    tap_x * COUT : (tap_x + 1) * COUT, source : source + CIN
                ]
    for slot in range(SLOTS):
        a, b = own_a[slot], own_b[slot]
        table[OWN_X + slot] = jnp.where(odd_x, b, a)
        table[OWN_X + 2 + slot] = jnp.where(odd_x, a, b)
        a, b = far_a[slot], far_b[slot]
        table[FAR_X + slot] = jnp.where(odd_x, a, b)
        table[FAR_X + 2 + slot] = jnp.where(odd_x, b, a)
        table[FAR_Y + slot] = far_y[slot, :, :PLANE]
        for d in range(2):
            table[OWN_Y + d * 2 + slot] = faces_y[d * 2 + slot]
            table[EDGE_Y + d * 2 + slot, :, :128] = far_y[
                slot, :, PLANE + d * 128 : PLANE + (d + 1) * 128
            ]
            table[EDGE_Y + d * 2 + slot, :, 128:] = jnp.zeros((CIN, 128), BF)

    lane = lanes(CIN, PLANE)
    y_first, y_last = lane < EDGE, lane >= PLANE - EDGE
    zero = jnp.zeros((CIN, PLANE), BF)
    lane_o = lanes(COUT, PLANE)
    none = jnp.zeros((COUT, PLANE), F32)
    for slot in range(SLOTS):
        for d in range(2):
            present, code, u = link(links, slot, sign(d), 0, 0)
            k = d * 2 + u
            centre = whole(table, present, jnp.minimum(code, 1) * 4 + k)
            sides = []
            for f in range(2):
                present, code, u = link(links, slot, sign(d), 0, sign(f))
                index = jnp.minimum(code, 1) * 4 + d * 2 + u
                sides.append(column(table, present & (code < 4), index, last(f), f))
            rows = []
            for e in range(2):
                far = 112 if e == 0 else 0

                def index_of(code, u):
                    return pick(
                        code,
                        (
                            (0, OWN_X + d * 2 + u),
                            (1, FAR_X + d * 2 + u),
                            (2, FAR_Y + u),
                            (3, EDGE_Y + d * 2 + u),
                        ),
                    )

                def start_of(code):
                    return pick(
                        code,
                        ((0, last(e) * EDGE), (1, last(e) * EDGE), (2, last(d) * EDGE), (3, far)),
                    )

                present, code, u = link(links, slot, sign(d), sign(e), 0)
                row = short(table, present, index_of(code, u), start_of(code), 0)
                for f in range(2):
                    present, code, u = link(links, slot, sign(d), sign(e), sign(f))
                    target = 127 if f == 0 else EDGE
                    value = short(
                        table,
                        present & (code < 4),
                        index_of(code, u),
                        start_of(code) + last(f),
                        target,
                    )
                    row = put_corner(row, f, value)
                rows.append(row)
            fill_columns(columns, d, centre, sides, rows)
            taps = wall[2 * d * COUT : (2 * d + 1) * COUT, :]
            sheets_x[slot * 2 + d] = jnp.dot(taps, columns[d], preferred_element_type=F32)
        for e in range(2):
            present, code, u = link(links, slot, 0, sign(e), 0)
            centre = whole(
                table, present, jnp.where(code == 0, OWN_Y + e * 2 + u, FAR_Y + u)
            )
            sides = []
            for f in range(2):
                present, code, u = link(links, slot, 0, sign(e), sign(f))
                index = jnp.where(code == 0, OWN_Y + e * 2 + u, FAR_Y + u)
                sides.append(column(table, present & (code < 4), index, last(f), f))
            columns[e, :CIN, :] = jnp.where(lane % EDGE == 0, sides[0], roll(centre, 1))
            columns[e, CIN : 2 * CIN, :] = centre
            columns[e, 2 * CIN : 3 * CIN, :] = jnp.where(
                lane % EDGE == EDGE - 1, sides[1], roll(centre, -1)
            )
            taps = wall[:, 2 * e * 3 * CIN : (2 * e + 1) * 3 * CIN]
            part = jnp.dot(taps, columns[e, : 3 * CIN, :], preferred_element_type=F32)
            sheet = part[COUT : 2 * COUT]
            sheet = sheet + jnp.where(lane_o < EDGE, none, roll(part[:COUT], EDGE))
            sheet = sheet + jnp.where(
                lane_o >= PLANE - EDGE, none, roll(part[2 * COUT :], -EDGE)
            )
            sheets_y[slot * 2 + e] = sheet
        for f in range(2):
            present, code, u = link(links, slot, 0, 0, sign(f))
            centre = jnp.where(present & (code < 4), faces_z[f * 2 + u], zero)
            columns[f, :CIN, :] = jnp.where(y_first, zero, roll(centre, EDGE))
            columns[f, CIN : 2 * CIN, :] = centre
            columns[f, 2 * CIN : 3 * CIN, :] = jnp.where(y_last, zero, roll(centre, -EDGE))
            taps = jnp.concatenate(
                [
                    wall[:, (tap_y * 3 + 2 * f) * CIN : (tap_y * 3 + 2 * f + 1) * CIN]
                    for tap_y in range(3)
                ],
                1,
            )
            part = jnp.dot(taps, columns[f, : 3 * CIN, :], preferred_element_type=F32)
            sheet = part[COUT : 2 * COUT]
            sheet = sheet + jnp.where(lane_o % EDGE == 0, none, roll(part[:COUT], 1))
            sheet = sheet + jnp.where(
                lane_o % EDGE == EDGE - 1, none, roll(part[2 * COUT :], -1)
            )
            sheets_z[slot * 2 + f] = sheet


def finish(
    links, count, acc_a, acc_b, sheets_x, sheets_y, near_z, got_a, got_b, walls_z, bias, head,
    head_bias, turn, out, columns, table
):
    _, parity_z, _ = place()
    odd_z = parity_z == 1
    for slot in range(SLOTS):
        a, b = got_a[slot], got_b[slot]
        table[FAR_Z + slot] = jnp.where(odd_z, a, b)
        table[FAR_Z + 2 + slot] = jnp.where(odd_z, b, a)
    a, b = got_a[2], got_b[2]
    for f, value in enumerate((jnp.where(odd_z, a, b), jnp.where(odd_z, b, a))):
        table[EDGE_Z + f] = value
        table[TURN_Z + f] = jnp.dot(value, turn[...], preferred_element_type=F32).astype(BF)
    accs = (acc_a, acc_b)
    lane_o = lanes(COUT, PLANE)
    half_o = lanes(COUT, 128)
    none = jnp.zeros((COUT, PLANE), F32)
    half_none = jnp.zeros((COUT, 128), F32)
    for slot in range(SLOTS):
        acc = accs[slot]
        sheets_z = []
        for f in range(2):
            present, code, u = link(links, slot, 0, 0, sign(f))
            centre = whole(table, present & (code >= 4), FAR_Z + f * 2 + u)
            sides = []
            for d in range(2):
                present, code, u = link(links, slot, sign(d), 0, sign(f))
                index = jnp.where(code == 4, FAR_Z + f * 2 + u, EDGE_Z + f)
                source = jnp.where(code == 4, last(d), d * 2 + u)
                sides.append(column(table, present & (code >= 4), index, source, d))
            rows = []
            for e in range(2):
                present, code, u = link(links, slot, 0, sign(e), sign(f))
                index = jnp.where(code == 4, FAR_Z + f * 2 + u, TURN_Z + f)
                source = jnp.where(code == 4, last(e) * EDGE, (4 + u) * EDGE)
                row = short(table, present & (code >= 4), index, source, 0)
                for d in range(2):
                    present, code, u = link(links, slot, sign(d), sign(e), sign(f))
                    index = jnp.where(code == 4, FAR_Z + f * 2 + u, EDGE_Z + f)
                    source = pick(
                        code,
                        (
                            (4, last(e) * EDGE + last(d)),
                            (5, last(e) * EDGE + d * 2 + u),
                            (6, last(d) * EDGE + 4 + u),
                            (7, 6 + d * 2 + u),
                        ),
                    )
                    target = 127 if d == 0 else EDGE
                    value = short(table, present & (code >= 4), index, source, target)
                    row = put_corner(row, d, value)
                rows.append(row)
            fill_columns(columns, f, centre, sides, rows)
            sheets_z.append(
                near_z[slot * 2 + f]
                + jnp.dot(walls_z[f], columns[f], preferred_element_type=F32)
            )
        used = slot < count[0]
        for x in range(EDGE):
            total = acc[:, x * PLANE : (x + 1) * PLANE]
            if x == 0:
                total = total + sheets_x[slot * 2]
            elif x == EDGE - 1:
                total = total + sheets_x[slot * 2 + 1]
            total = total + jnp.where(lane_o % EDGE == 0, roll(sheets_z[0], -x), none)
            total = total + jnp.where(
                lane_o % EDGE == EDGE - 1, roll(sheets_z[1], EDGE - 1 - x), none
            )
            from_half = slice((x // 8) * 128, (x // 8 + 1) * 128)
            low = roll(sheets_y[slot * 2, :, from_half], -(x % 8) * EDGE)
            high = roll(sheets_y[slot * 2 + 1, :, from_half], 112 - (x % 8) * EDGE)
            low = total[:, :128] + jnp.where(half_o < EDGE, low, half_none)
            high = total[:, 128:] + jnp.where(half_o >= 112, high, half_none)
            for part, value in enumerate((low, high)):
                hidden = jnp.maximum(value + bias[...], 0.0).astype(BF)
                mixed = jnp.dot(head[...], hidden, preferred_element_type=F32) + head_bias[...]
                out[slot, :, x * PLANE + part * 128 : x * PLANE + (part + 1) * 128] = jnp.where(
                    used, mixed, half_none
                ).astype(BF)


SMEM = pl.BlockSpec(memory_space=pltpu.SMEM)
VMEM = pl.BlockSpec(memory_space=pltpu.VMEM)
HBM = pl.BlockSpec(memory_space=pltpu.HBM)
ANY = pl.BlockSpec(memory_space=pl.ANY)


def shape(dims, kind=BF):
    return jax.ShapeDtypeStruct(dims, kind)


def in_hbm(value):
    return pltpu.with_memory_space_constraint(value, pltpu.HBM)


def swap(first, second, axis):
    length = lax.axis_size(axis)
    even = [(i, i ^ 1) for i in range(length)]
    odd = [(i, ((i + 1) ^ 1) - 1) for i in range(1, length - 1)]
    return lax.ppermute(first, axis, even), lax.ppermute(second, axis, odd)


def body(blocks, block_count, neighbours, conv_weight, conv_bias, head_weight, head_bias):
    volumes = blocks.reshape(SLOTS, CIN, VOX)
    count = block_count.reshape(1)
    links = neighbours.reshape(SLOTS, 26)
    odd_x = lax.axis_index("gx") % 2
    far_end = VOX - PLANE
    own_a = lax.dynamic_slice_in_dim(volumes, (1 - odd_x) * far_end, PLANE, 2)
    own_b = lax.dynamic_slice_in_dim(volumes, odd_x * far_end, PLANE, 2)
    far_a, far_b = swap(own_a, own_b, "gx")
    buffer = pltpu.VMEM((2, TAPS * CIN, PLANE), BF)
    block_flops = 2 * COUT * 27 * CIN * VOX
    held, faces_y, faces_z, acc_a, wall = pl.pallas_call(
        pack_and_convolve,
        out_shape=(
            shape((CIN, VOX)),
            shape((4, CIN, PLANE)),
            shape((4, CIN, PLANE)),
            shape((COUT, VOX), F32),
            shape((3 * COUT, TAPS * CIN)),
        ),
        in_specs=[HBM, HBM],
        out_specs=(VMEM, VMEM, VMEM, VMEM, VMEM),
        scratch_shapes=[
            buffer,
            pltpu.VMEM((CIN, VOX), BF),
            pltpu.VMEM((COUT, 27 * CIN), BF),
            pltpu.SemaphoreType.DMA((SLOTS * CHUNK,)),
            pltpu.SemaphoreType.DMA,
        ],
        compiler_params=params(16),
        cost_estimate=pl.CostEstimate(
            flops=2 * block_flops, bytes_accessed=4 * 2**20, transcendentals=0
        ),
    )(in_hbm(volumes), in_hbm(conv_weight))
    sent_y = pl.pallas_call(
        pack_for_y,
        out_shape=shape((SLOTS, CIN, 2 * PLANE)),
        in_specs=[VMEM, VMEM, VMEM],
        out_specs=VMEM,
        compiler_params=params(8),
    )(faces_y, far_a, far_b)
    far_y = lax.ppermute(sent_y, "gy", [(0, 1), (1, 0)])
    part_acc, carry = pl.pallas_call(
        begin_second,
        out_shape=(shape((COUT, (SPLIT - 1) * PLANE), F32), shape((2, COUT, PLANE), F32)),
        in_specs=[VMEM, VMEM, ANY],
        out_specs=(VMEM, VMEM),
        scratch_shapes=[buffer],
        compiler_params=params(16),
        cost_estimate=pl.CostEstimate(
            flops=block_flops, bytes_accessed=2**20, transcendentals=0
        ),
    )(held, wall, sent_y)
    sent_a, sent_b = pl.pallas_call(
        pack_for_z,
        out_shape=(shape((3, CIN, PLANE)), shape((3, CIN, PLANE))),
        in_specs=[VMEM, VMEM, VMEM, VMEM],
        out_specs=(VMEM, VMEM),
        compiler_params=params(8),
    )(faces_z, far_a, far_b, far_y)
    got_a, got_b = swap(sent_a, sent_b, "gz")
    sheet = shape((4, COUT, PLANE), F32)
    acc_b, walls_z, sheets_x, sheets_y, near_z = pl.pallas_call(
        finish_second,
        out_shape=(
            shape((COUT, VOX), F32), shape((2, COUT, TAPS * CIN)), sheet, sheet, sheet
        ),
        in_specs=[SMEM, VMEM, VMEM, ANY] + [VMEM] * 9,
        out_specs=(VMEM,) * 5,
        scratch_shapes=[buffer, pltpu.VMEM((NEAR_SOURCES, CIN, PLANE), BF)],
        compiler_params=params(16),
        cost_estimate=pl.CostEstimate(
            flops=2 * block_flops, bytes_accessed=2 * 2**20, transcendentals=0
        ),
    )(
        links, held, wall, sent_a, carry, part_acc, own_a, own_b, far_a, far_b, faces_y, far_y,
        faces_z,
    )
    index = jnp.arange(PLANE)
    turn = (index[:, None] == (index % EDGE * EDGE + index // EDGE)[None, :]).astype(BF)
    outputs = pl.pallas_call(
        finish,
        out_shape=shape((SLOTS, COUT, VOX)),
        in_specs=[SMEM] * 2 + [VMEM] * 12,
        out_specs=VMEM,
        scratch_shapes=[buffer, pltpu.VMEM((Z_SOURCES, CIN, PLANE), BF)],
        compiler_params=params(16),
    )(
        links, count, acc_a, acc_b, sheets_x, sheets_y, near_z, got_a, got_b, walls_z,
        conv_bias.reshape(COUT, 1), head_weight, head_bias.reshape(COUT, 1), turn,
    )
    return outputs.reshape(1, 1, SLOTS, COUT, VOX)


def solution(mesh):
    placed = (
        P("gx", "gz", "gy", None, None),
        P("gx", "gz", "gy"),
        P("gx", "gz", "gy", None),
        P(),
        P(),
        P(),
        P(),
    )
    return jax.shard_map(
        body, mesh=mesh, in_specs=placed, out_specs=P("gx", "gz", "gy", None, None), check_vma=False
    )
```

```python
import jax
import jax.numpy as jnp
from jax import lax
from jax.experimental import pallas as pl
from jax.experimental.pallas import tpu as pltpu
from jax.sharding import PartitionSpec as P

CIN = 96
COUT = 48
EDGE = 16
PLANE = 256
VOX = 4096
SLOTS = 2
TAPS = 9
BF = jnp.bfloat16
F32 = jnp.float32

OWN_X, FAR_X, FAR_Y, OWN_Y, EDGE_Y, NEAR_SOURCES = 0, 4, 8, 10, 14, 18
FAR_Z, EDGE_Z, TURN_Z, Z_SOURCES = 0, 4, 6, 8
SPLIT = 5
CHUNK = 4


def params(mib):
    return pltpu.CompilerParams(vmem_limit_bytes=mib * 2**20)


def lanes(rows, width):
    return lax.broadcasted_iota(jnp.int32, (rows, width), 1)


def last(side):
    return EDGE - 1 if side == 0 else 0


def roll(value, shift):
    width = value.shape[1]
    if isinstance(shift, int):
        shift = shift % width
        if shift == 0:
            return value
    return pltpu.roll(value, shift, 1)


def place():
    return lax.axis_index("gx") % 2, lax.axis_index("gz") % 2, lax.axis_index("gy")


def interior(block, wall, columns, write, first, stop, carry=None):
    lane = lanes(CIN, PLANE)
    z_of = lane % EDGE
    z_first, z_last = z_of == 0, z_of == EDGE - 1
    y_first, y_last = lane < EDGE, lane >= PLANE - EDGE
    zero = jnp.zeros((CIN, PLANE), BF)
    before, current = carry if carry is not None else (None, None)
    for x in range(first, stop):
        centre = block(x)
        z_less = jnp.where(z_first, zero, roll(centre, 1))
        z_more = jnp.where(z_last, zero, roll(centre, -1))
        buffer = x % 2
        for tap_z, value in enumerate((z_less, centre, z_more)):
            for tap_y in range(3):
                if tap_y == 0:
                    shifted = jnp.where(y_first, zero, roll(value, EDGE))
                elif tap_y == 1:
                    shifted = value
                else:
                    shifted = jnp.where(y_last, zero, roll(value, -EDGE))
                start = (tap_y * 3 + tap_z) * CIN
                columns[buffer, start : start + CIN, :] = shifted
        part = jnp.dot(wall[...], columns[buffer], preferred_element_type=F32)
        if x > 0:
            write(x - 1, before + part[2 * COUT :])
            before = current + part[COUT : 2 * COUT]
        else:
            before = part[COUT : 2 * COUT]
        current = part[:COUT]
    if stop == EDGE:
        write(EDGE - 1, before)
    return before, current


def write_plane(acc):
    def write(x, value):
        acc[:, x * PLANE : (x + 1) * PLANE] = value

    return write


def plane_of(block):
    return lambda x: block[:, x * PLANE : (x + 1) * PLANE]


def pack_and_convolve(blocks, weight, held, faces_y, faces_z, acc, wall, columns, first, weights, sems, weight_sem):
    width = VOX // CHUNK
    copies = []
    for slot in range(SLOTS):
        for part in range(CHUNK):
            at = pl.ds(part * width, width)
            copies.append(
                pltpu.make_async_copy(
                    blocks.at[slot, :, at], (first, held)[slot].at[:, at], sems.at[slot * CHUNK + part]
                )
            )
    weight_copy = pltpu.make_async_copy(weight, weights, weight_sem)
    copies[0].start()
    weight_copy.start()
    for copy in copies[1:]:
        copy.start()
    lane = lanes(CIN, PLANE)
    half_lane = lanes(CIN, 128)
    for slot in range(SLOTS):
        planes_z = [jnp.zeros((CIN, PLANE), BF)] * 2
        halves = [[jnp.zeros((CIN, 128), BF)] * 2 for _ in range(2)]
        for x in range(EDGE):
            if x % (EDGE // CHUNK) == 0:
                copies[slot * CHUNK + x // (EDGE // CHUNK)].wait()
            centre = (first, held)[slot][:, x * PLANE : (x + 1) * PLANE]
            for side in range(2):
                planes_z[side] = jnp.where(
                    lane % EDGE == x, roll(centre, x - last(side)), planes_z[side]
                )
                half = centre[:, 128:] if side == 0 else centre[:, :128]
                at = (x % 8) * EDGE
                moved = roll(half, at - (112 if side == 0 else 0))
                halves[side][x // 8] = jnp.where(
                    half_lane // EDGE == x % 8, moved, halves[side][x // 8]
                )
        for side in range(2):
            faces_z[side * 2 + slot] = planes_z[side]
            faces_y[side * 2 + slot, :, :128] = halves[side][0]
            faces_y[side * 2 + slot, :, 128:] = halves[side][1]
        if slot == 0:
            weight_copy.wait()
            for tap_x in range(3):
                wall[tap_x * COUT : (tap_x + 1) * COUT, :] = weights[
                    :, tap_x * TAPS * CIN : (tap_x + 1) * TAPS * CIN
                ]
            interior(plane_of(first), wall, columns, write_plane(acc), 0, EDGE)


def begin_second(held, wall, tie, acc, carry, columns):
    before, current = interior(plane_of(held), wall, columns, write_plane(acc), 0, SPLIT)
    carry[0], carry[1] = before, current


def pack_for_y(faces_y, far_a, far_b, out):
    parity, _, at_y = place()
    odd_x = parity == 1
    for slot in range(SLOTS):
        out[slot, :, :PLANE] = faces_y[at_y * 2 + slot]
        start = pl.multiple_of((1 - at_y) * 128, 128)
        a = far_a[slot, :, pl.ds(start, 128)]
        b = far_b[slot, :, pl.ds(start, 128)]
        out[slot, :, PLANE : PLANE + 128] = jnp.where(odd_x, a, b)
        out[slot, :, PLANE + 128 :] = jnp.where(odd_x, b, a)


def pack_for_z(faces_z, far_a, far_b, far_y, out_a, out_b):
    parity_x, parity_z, at_y = place()
    odd_x, odd_z = parity_x == 1, parity_z == 1
    lane = lanes(CIN, PLANE)
    half_lane = lanes(CIN, 128)
    row = at_y * 112
    packs = []
    for side in range(2):
        z = last(side)
        pack = jnp.zeros((CIN, PLANE), BF)
        corner = jnp.zeros((CIN, 128), BF)
        for slot in range(SLOTS):
            a, b = far_a[slot], far_b[slot]
            pair = (jnp.where(odd_x, a, b), jnp.where(odd_x, b, a))
            for d in range(2):
                k = d * 2 + slot
                pack = jnp.where(lane % EDGE == k, roll(pair[d], k - z), pack)
                edge = far_y[slot, :, PLANE + d * 128 : PLANE + (d + 1) * 128]
                moved = pltpu.roll(edge, (6 + k - z - row + 128) % 128, 1)
                corner = jnp.where(half_lane == 6 + k, moved, corner)
            k = 4 + slot
            pack = jnp.where(lane % EDGE == k, roll(far_y[slot, :, :PLANE], k - z), pack)
        low = jnp.where((half_lane >= 6) & (half_lane < 10), corner, pack[:, :128])
        packs.append((low, pack[:, 128:]))
    first, second = packs
    for part in range(2):
        at = slice(part * 128, (part + 1) * 128)
        out_a[2, :, at] = jnp.where(odd_z, second[part], first[part])
        out_b[2, :, at] = jnp.where(odd_z, first[part], second[part])
    for slot in range(SLOTS):
        out_a[slot] = faces_z[parity_z * 2 + slot]
        out_b[slot] = faces_z[(1 - parity_z) * 2 + slot]


def pick(code, choices):
    result = choices[-1][1]
    for known, value in reversed(choices[:-1]):
        result = jnp.where(code == known, value, result)
    return result


def sign(side):
    return -1 if side == 0 else 1


def link(links, slot, dx, dy, dz):
    index = (dx + 1) * 9 + (dy + 1) * 3 + dz + 1
    value = links[slot, index if index < 13 else index - 1]
    clean = jnp.maximum(value, 0)
    return value >= 0, clean // 2, clean % 2


def whole(table, present, index):
    return jnp.where(present, table[index], jnp.zeros((CIN, PLANE), BF))


def column(table, present, index, source, side):
    target = 0 if side == 0 else EDGE - 1
    moved = pltpu.roll(table[index], (target - source + PLANE) % PLANE, 1)
    return jnp.where(present, moved, jnp.zeros((CIN, PLANE), BF))


def short(table, present, index, source, target):
    start = pl.multiple_of((source // 128) * 128, 128)
    value = table[index, :, pl.ds(start, 128)]
    moved = pltpu.roll(value, (target - source % 128 + 128) % 128, 1)
    return jnp.where(present, moved, jnp.zeros((CIN, 128), BF))


def put_corner(row, side, value):
    return jnp.where(lanes(CIN, 128) == (127 if side == 0 else EDGE), value, row)


def fill_columns(columns, buffer, centre, sides, rows):
    lane = lanes(CIN, PLANE)
    half_lane = lanes(CIN, 128)
    less = jnp.where(lane % EDGE == 0, sides[0], roll(centre, 1))
    more = jnp.where(lane % EDGE == EDGE - 1, sides[1], roll(centre, -1))
    for minor, value in enumerate((less, centre, more)):
        low, high = roll(rows[0], 1 - minor), roll(rows[1], 113 - minor)
        for major in range(3):
            start = (major * 3 + minor) * CIN
            at = slice(start, start + CIN)
            if major == 1:
                columns[buffer, at, :] = value
            elif major == 0:
                shifted = roll(value, EDGE)
                columns[buffer, at, :128] = jnp.where(half_lane < EDGE, low, shifted[:, :128])
                columns[buffer, at, 128:] = shifted[:, 128:]
            else:
                shifted = roll(value, -EDGE)
                columns[buffer, at, :128] = shifted[:, :128]
                columns[buffer, at, 128:] = jnp.where(half_lane >= 112, high, shifted[:, 128:])


def any_of(terms):
    result = terms[0]
    for term in terms[1:]:
        result = result | term
    return result


def near(links, slot, dx, dy, dz):
    present, code, _ = link(links, slot, dx, dy, dz)
    return present & (code < 4)


def add_rows(acc, sheet, side):
    half_o = lanes(COUT, 128)
    none = jnp.zeros((COUT, 128), F32)
    for x in range(EDGE):
        part = sheet[:, (x // 8) * 128 : (x // 8 + 1) * 128]
        if side == 0:
            moved = jnp.where(half_o < EDGE, roll(part, -(x % 8) * EDGE), none)
            at = slice(x * PLANE, x * PLANE + 128)
        else:
            moved = jnp.where(half_o >= 112, roll(part, 112 - (x % 8) * EDGE), none)
            at = slice(x * PLANE + 128, (x + 1) * PLANE)
        acc[:, at] = acc[:, at] + moved


def spread(sheet, side, x):
    lane_o = lanes(COUT, PLANE)
    moved = roll(sheet, last(1 - side) - x)
    return jnp.where(lane_o % EDGE == last(1 - side), moved, jnp.zeros((COUT, PLANE), F32))


def near_x(links, table, wall, columns, acc, slot, d):
    present, code, u = link(links, slot, sign(d), 0, 0)
    centre = whole(table, present, jnp.minimum(code, 1) * 4 + d * 2 + u)
    sides = []
    for f in range(2):
        present, code, u = link(links, slot, sign(d), 0, sign(f))
        index = jnp.minimum(code, 1) * 4 + d * 2 + u
        sides.append(column(table, present & (code < 4), index, last(f), f))
    rows = []
    for e in range(2):
        far = 112 if e == 0 else 0

        def index_of(code, u):
            return pick(
                code,
                (
                    (0, OWN_X + d * 2 + u),
                    (1, FAR_X + d * 2 + u),
                    (2, FAR_Y + u),
                    (3, EDGE_Y + d * 2 + u),
                ),
            )

        def start_of(code):
            return pick(
                code, ((0, last(e) * EDGE), (1, last(e) * EDGE), (2, last(d) * EDGE), (3, far))
            )

        present, code, u = link(links, slot, sign(d), sign(e), 0)
        row = short(table, present, index_of(code, u), start_of(code), 0)
        for f in range(2):
            present, code, u = link(links, slot, sign(d), sign(e), sign(f))
            target = 127 if f == 0 else EDGE
            source = start_of(code) + last(f)
            value = short(table, present & (code < 4), index_of(code, u), source, target)
            row = put_corner(row, f, value)
        rows.append(row)
    fill_columns(columns, d, centre, sides, rows)
    taps = wall[2 * d * COUT : (2 * d + 1) * COUT, :]
    x = last(1 - d)
    at = slice(x * PLANE, (x + 1) * PLANE)
    acc[:, at] = acc[:, at] + jnp.dot(taps, columns[d], preferred_element_type=F32)


def near_y(links, table, wall, columns, acc, slot, e):
    lane = lanes(CIN, PLANE)
    lane_o = lanes(COUT, PLANE)
    none = jnp.zeros((COUT, PLANE), F32)
    present, code, u = link(links, slot, 0, sign(e), 0)
    centre = whole(table, present, jnp.where(code == 0, OWN_Y + e * 2 + u, FAR_Y + u))
    sides = []
    for f in range(2):
        present, code, u = link(links, slot, 0, sign(e), sign(f))
        index = jnp.where(code == 0, OWN_Y + e * 2 + u, FAR_Y + u)
        sides.append(column(table, present & (code < 4), index, last(f), f))
    columns[e, :CIN, :] = jnp.where(lane % EDGE == 0, sides[0], roll(centre, 1))
    columns[e, CIN : 2 * CIN, :] = centre
    columns[e, 2 * CIN : 3 * CIN, :] = jnp.where(lane % EDGE == EDGE - 1, sides[1], roll(centre, -1))
    taps = wall[:, 2 * e * 3 * CIN : (2 * e + 1) * 3 * CIN]
    part = jnp.dot(taps, columns[e, : 3 * CIN, :], preferred_element_type=F32)
    sheet = part[COUT : 2 * COUT]
    sheet = sheet + jnp.where(lane_o < EDGE, none, roll(part[:COUT], EDGE))
    sheet = sheet + jnp.where(lane_o >= PLANE - EDGE, none, roll(part[2 * COUT :], -EDGE))
    add_rows(acc, sheet, e)


def near_z(links, faces_z, wall, columns, acc, slot, f):
    lane = lanes(CIN, PLANE)
    zero = jnp.zeros((CIN, PLANE), BF)
    lane_o = lanes(COUT, PLANE)
    none = jnp.zeros((COUT, PLANE), F32)
    _, _, u = link(links, slot, 0, 0, sign(f))
    centre = faces_z[f * 2 + u]
    columns[f, :CIN, :] = jnp.where(lane < EDGE, zero, roll(centre, EDGE))
    columns[f, CIN : 2 * CIN, :] = centre
    columns[f, 2 * CIN : 3 * CIN, :] = jnp.where(lane >= PLANE - EDGE, zero, roll(centre, -EDGE))
    taps = jnp.concatenate(
        [
            wall[:, (tap_y * 3 + 2 * f) * CIN : (tap_y * 3 + 2 * f + 1) * CIN]
            for tap_y in range(3)
        ],
        1,
    )
    part = jnp.dot(taps, columns[f, : 3 * CIN, :], preferred_element_type=F32)
    sheet = part[COUT : 2 * COUT]
    sheet = sheet + jnp.where(lane_o % EDGE == 0, none, roll(part[:COUT], 1))
    sheet = sheet + jnp.where(lane_o % EDGE == EDGE - 1, none, roll(part[2 * COUT :], -1))
    for x in range(EDGE):
        at = slice(x * PLANE, (x + 1) * PLANE)
        acc[:, at] = acc[:, at] + spread(sheet, f, x)


def finish_second(
    links_in, held, wall, tie, carry, part_acc, acc_in, own_a, own_b, far_a, far_b, faces_y,
    far_y, faces_z, acc_a, acc_b, walls_z, columns, table, links, sem
):
    fetch = pltpu.make_async_copy(links_in, links, sem)
    fetch.start()
    parity_x, _, _ = place()
    odd_x = parity_x == 1
    for slot in range(SLOTS):
        a, b = own_a[slot], own_b[slot]
        table[OWN_X + slot] = jnp.where(odd_x, b, a)
        table[OWN_X + 2 + slot] = jnp.where(odd_x, a, b)
        a, b = far_a[slot], far_b[slot]
        table[FAR_X + slot] = jnp.where(odd_x, a, b)
        table[FAR_X + 2 + slot] = jnp.where(odd_x, b, a)
        table[FAR_Y + slot] = far_y[slot, :, :PLANE]
        for d in range(2):
            table[OWN_Y + d * 2 + slot] = faces_y[d * 2 + slot]
            table[EDGE_Y + d * 2 + slot, :, :128] = far_y[
                slot, :, PLANE + d * 128 : PLANE + (d + 1) * 128
            ]
            table[EDGE_Y + d * 2 + slot, :, 128:] = jnp.zeros((CIN, 128), BF)
    for x in range(EDGE):
        at = slice(x * PLANE, (x + 1) * PLANE)
        acc_a[:, at] = acc_in[:, at]
        if x < SPLIT - 1:
            acc_b[:, at] = part_acc[:, at]
    interior(plane_of(held), wall, columns, write_plane(acc_b), SPLIT, EDGE, (carry[0], carry[1]))
    for f in range(2):
        for tap_y in range(3):
            for tap_x in range(3):
                start = (tap_y * 3 + tap_x) * CIN
                source = (tap_y * 3 + 2 * f) * CIN
                walls_z[f, :, start : start + CIN] = wall[
                    tap_x * COUT : (tap_x + 1) * COUT, source : source + CIN
                ]
    fetch.wait()
    accs = (acc_a, acc_b)
    steps = (-1, 0, 1)
    for slot in range(SLOTS):
        acc = accs[slot]
        for d in range(2):
            wanted = any_of(
                [near(links, slot, sign(d), dy, dz) for dy in steps for dz in steps]
            )

            @pl.when(wanted)
            def _():
                near_x(links, table, wall, columns, acc, slot, d)

        for e in range(2):

            @pl.when(any_of([near(links, slot, 0, sign(e), dz) for dz in steps]))
            def _():
                near_y(links, table, wall, columns, acc, slot, e)

        for f in range(2):

            @pl.when(near(links, slot, 0, 0, sign(f)))
            def _():
                near_z(links, faces_z, wall, columns, acc, slot, f)


def far_z(links, table, walls_z, columns, slot, f):
    present, code, u = link(links, slot, 0, 0, sign(f))
    centre = whole(table, present & (code >= 4), FAR_Z + f * 2 + u)
    sides = []
    for d in range(2):
        present, code, u = link(links, slot, sign(d), 0, sign(f))
        index = jnp.where(code == 4, FAR_Z + f * 2 + u, EDGE_Z + f)
        source = jnp.where(code == 4, last(d), d * 2 + u)
        sides.append(column(table, present & (code >= 4), index, source, d))
    rows = []
    for e in range(2):
        present, code, u = link(links, slot, 0, sign(e), sign(f))
        index = jnp.where(code == 4, FAR_Z + f * 2 + u, TURN_Z + f)
        source = jnp.where(code == 4, last(e) * EDGE, (4 + u) * EDGE)
        row = short(table, present & (code >= 4), index, source, 0)
        for d in range(2):
            present, code, u = link(links, slot, sign(d), sign(e), sign(f))
            index = jnp.where(code == 4, FAR_Z + f * 2 + u, EDGE_Z + f)
            source = pick(
                code,
                (
                    (4, last(e) * EDGE + last(d)),
                    (5, last(e) * EDGE + d * 2 + u),
                    (6, last(d) * EDGE + 4 + u),
                    (7, 6 + d * 2 + u),
                ),
            )
            target = 127 if d == 0 else EDGE
            value = short(table, present & (code >= 4), index, source, target)
            row = put_corner(row, d, value)
        rows.append(row)
    fill_columns(columns, f, centre, sides, rows)
    return jnp.dot(walls_z[f], columns[f], preferred_element_type=F32)


def upright(row):
    size = row.shape[1]
    across = lax.broadcasted_iota(jnp.int32, (size, size), 1)
    down = lax.broadcasted_iota(jnp.int32, (size, size), 0)
    wide = jnp.where(across == down, jnp.broadcast_to(row, (size, size)), 0.0)
    return jnp.sum(wide, axis=1, keepdims=True)


def finish(
    links_in, count_in, acc_a, acc_b, got_a, got_b, walls_z, bias_row, head, head_bias_row, turn,
    out, columns, table, sheets, links, count, sems
):
    fetch_links = pltpu.make_async_copy(links_in, links, sems.at[0])
    fetch_count = pltpu.make_async_copy(count_in, count, sems.at[1])
    fetch_links.start()
    fetch_count.start()
    _, parity_z, _ = place()
    odd_z = parity_z == 1
    bias, head_bias = upright(bias_row[...]), upright(head_bias_row[...])
    weights = head[...]
    for slot in range(SLOTS):
        a, b = got_a[slot], got_b[slot]
        table[FAR_Z + slot] = jnp.where(odd_z, a, b)
        table[FAR_Z + 2 + slot] = jnp.where(odd_z, b, a)
    a, b = got_a[2], got_b[2]
    for f, value in enumerate((jnp.where(odd_z, a, b), jnp.where(odd_z, b, a))):
        table[EDGE_Z + f] = value
        table[TURN_Z + f] = jnp.dot(value, turn[...], preferred_element_type=F32).astype(BF)
    fetch_links.wait()
    fetch_count.wait()
    accs = (acc_a, acc_b)
    steps = (-1, 0, 1)

    def emit(slot, total, x):
        hidden = jnp.maximum(total + bias, 0.0).astype(BF)
        mixed = jnp.dot(weights, hidden, preferred_element_type=F32) + head_bias
        out[slot, :, x * PLANE : (x + 1) * PLANE] = mixed.astype(BF)

    for slot in range(SLOTS):
        acc = accs[slot]
        wanted = []
        for f in range(2):
            terms = []
            for dx in steps:
                for dy in steps:
                    present, code, _ = link(links, slot, dx, dy, sign(f))
                    terms.append(present & (code >= 4))
            wanted.append(any_of(terms))
        used = slot < count[0, 0, 0]
        both = wanted[0] | wanted[1]

        @pl.when(used & both)
        def _():
            for f in range(2):

                @pl.when(wanted[f])
                def _():
                    sheets[f] = far_z(links, table, walls_z, columns, slot, f)

                @pl.when(jnp.logical_not(wanted[f]))
                def _():
                    sheets[f] = jnp.zeros((COUT, PLANE), F32)

            for x in range(EDGE):
                total = acc[:, x * PLANE : (x + 1) * PLANE]
                total = total + spread(sheets[0], 0, x) + spread(sheets[1], 1, x)
                emit(slot, total, x)

        @pl.when(used & jnp.logical_not(both))
        def _():
            for x in range(EDGE):
                emit(slot, acc[:, x * PLANE : (x + 1) * PLANE], x)

        @pl.when(jnp.logical_not(used))
        def _():
            for x in range(EDGE):
                out[slot, :, x * PLANE : (x + 1) * PLANE] = jnp.zeros((COUT, PLANE), BF)


VMEM = pl.BlockSpec(memory_space=pltpu.VMEM)
HBM = pl.BlockSpec(memory_space=pltpu.HBM)
ANY = pl.BlockSpec(memory_space=pl.ANY)


def shape(dims, kind=BF):
    return jax.ShapeDtypeStruct(dims, kind)


def in_hbm(value):
    return pltpu.with_memory_space_constraint(value, pltpu.HBM)


def swap(first, second, axis):
    length = lax.axis_size(axis)
    even = [(i, i ^ 1) for i in range(length)]
    odd = [(i, ((i + 1) ^ 1) - 1) for i in range(1, length - 1)]
    return lax.ppermute(first, axis, even), lax.ppermute(second, axis, odd)


def body(blocks, block_count, neighbours, conv_weight, conv_bias, head_weight, head_bias):
    volumes = blocks.reshape(SLOTS, CIN, VOX)
    links = neighbours.reshape(SLOTS, 26)
    odd_x = lax.axis_index("gx") % 2
    far_end = VOX - PLANE
    own_a = lax.dynamic_slice_in_dim(volumes, (1 - odd_x) * far_end, PLANE, 2)
    own_b = lax.dynamic_slice_in_dim(volumes, odd_x * far_end, PLANE, 2)
    far_a, far_b = swap(own_a, own_b, "gx")
    buffer = pltpu.VMEM((2, TAPS * CIN, PLANE), BF)
    block_flops = 2 * COUT * 27 * CIN * VOX
    held, faces_y, faces_z, acc_a, wall = pl.pallas_call(
        pack_and_convolve,
        out_shape=(
            shape((CIN, VOX)),
            shape((4, CIN, PLANE)),
            shape((4, CIN, PLANE)),
            shape((COUT, VOX), F32),
            shape((3 * COUT, TAPS * CIN)),
        ),
        in_specs=[HBM, HBM],
        out_specs=(VMEM, VMEM, VMEM, VMEM, VMEM),
        scratch_shapes=[
            buffer,
            pltpu.VMEM((CIN, VOX), BF),
            pltpu.VMEM((COUT, 27 * CIN), BF),
            pltpu.SemaphoreType.DMA((SLOTS * CHUNK,)),
            pltpu.SemaphoreType.DMA,
        ],
        compiler_params=params(16),
        cost_estimate=pl.CostEstimate(
            flops=2 * block_flops, bytes_accessed=4 * 2**20, transcendentals=0
        ),
    )(in_hbm(volumes), in_hbm(conv_weight))
    sent_y = pl.pallas_call(
        pack_for_y,
        out_shape=shape((SLOTS, CIN, 2 * PLANE)),
        in_specs=[VMEM, VMEM, VMEM],
        out_specs=VMEM,
        compiler_params=params(8),
    )(faces_y, far_a, far_b)
    far_y = lax.ppermute(sent_y, "gy", [(0, 1), (1, 0)])
    part_acc, carry = pl.pallas_call(
        begin_second,
        out_shape=(shape((COUT, (SPLIT - 1) * PLANE), F32), shape((2, COUT, PLANE), F32)),
        in_specs=[VMEM, VMEM, ANY],
        out_specs=(VMEM, VMEM),
        scratch_shapes=[buffer],
        compiler_params=params(16),
        cost_estimate=pl.CostEstimate(
            flops=block_flops, bytes_accessed=2**20, transcendentals=0
        ),
    )(held, wall, sent_y)
    sent_a, sent_b = pl.pallas_call(
        pack_for_z,
        out_shape=(shape((3, CIN, PLANE)), shape((3, CIN, PLANE))),
        in_specs=[VMEM, VMEM, VMEM, VMEM],
        out_specs=(VMEM, VMEM),
        compiler_params=params(8),
    )(faces_z, far_a, far_b, far_y)
    got_a, got_b = swap(sent_a, sent_b, "gz")
    smem_links = pltpu.SMEM((SLOTS, 26), jnp.int32)
    acc_a, acc_b, walls_z = pl.pallas_call(
        finish_second,
        out_shape=(
            shape((COUT, VOX), F32), shape((COUT, VOX), F32), shape((2, COUT, TAPS * CIN))
        ),
        in_specs=[ANY, VMEM, VMEM, ANY] + [VMEM] * 10,
        out_specs=(VMEM,) * 3,
        scratch_shapes=[
            buffer,
            pltpu.VMEM((NEAR_SOURCES, CIN, PLANE), BF),
            smem_links,
            pltpu.SemaphoreType.DMA,
        ],
        compiler_params=params(16),
        cost_estimate=pl.CostEstimate(
            flops=2 * block_flops, bytes_accessed=2 * 2**20, transcendentals=0
        ),
    )(
        links, held, wall, sent_a, carry, part_acc, acc_a, own_a, own_b, far_a, far_b, faces_y,
        far_y, faces_z,
    )
    index = jnp.arange(PLANE)
    turn = (index[:, None] == (index % EDGE * EDGE + index // EDGE)[None, :]).astype(BF)
    outputs = pl.pallas_call(
        finish,
        out_shape=shape((SLOTS, COUT, VOX)),
        in_specs=[ANY] * 2 + [VMEM] * 9,
        out_specs=VMEM,
        scratch_shapes=[
            buffer,
            pltpu.VMEM((Z_SOURCES, CIN, PLANE), BF),
            pltpu.VMEM((2, COUT, PLANE), F32),
            smem_links,
            pltpu.SMEM((1, 1, 1), jnp.int32),
            pltpu.SemaphoreType.DMA((2,)),
        ],
        compiler_params=params(16),
    )(
        links, block_count, acc_a, acc_b, got_a, got_b, walls_z, conv_bias.reshape(1, COUT),
        head_weight, head_bias.reshape(1, COUT), turn,
    )
    return outputs.reshape(1, 1, SLOTS, COUT, VOX)


def solution(mesh):
    placed = (
        P("gx", "gz", "gy", None, None),
        P("gx", "gz", "gy"),
        P("gx", "gz", "gy", None),
        P(),
        P(),
        P(),
        P(),
    )
    return jax.shard_map(
        body, mesh=mesh, in_specs=placed, out_specs=P("gx", "gz", "gy", None, None), check_vma=False
    )
```

```python
import jax
import jax.numpy as jnp
from jax import lax
from jax.experimental import pallas as pl
from jax.experimental.pallas import tpu as pltpu
from jax.sharding import PartitionSpec as P

CIN = 96
COUT = 48
EDGE = 16
PLANE = 256
VOX = 4096
SLOTS = 2
TAPS = 9
BF = jnp.bfloat16
F32 = jnp.float32

OWN_X, FAR_X, FAR_Y, OWN_Y, EDGE_Y, NEAR_SOURCES = 0, 4, 8, 10, 14, 18
FAR_Z, EDGE_Z, TURN_Z, Z_SOURCES = 0, 4, 6, 8
SPLIT = 5
CHUNK = 4


def params(mib):
    return pltpu.CompilerParams(vmem_limit_bytes=mib * 2**20)


def lanes(rows, width):
    return lax.broadcasted_iota(jnp.int32, (rows, width), 1)


def last(side):
    return EDGE - 1 if side == 0 else 0


def roll(value, shift):
    width = value.shape[1]
    if isinstance(shift, int):
        shift = shift % width
        if shift == 0:
            return value
    return pltpu.roll(value, shift, 1)


def place():
    return lax.axis_index("gx") % 2, lax.axis_index("gz") % 2, lax.axis_index("gy")


def interior(block, wall, columns, write, first, stop, carry=None):
    lane = lanes(CIN, PLANE)
    z_of = lane % EDGE
    z_first, z_last = z_of == 0, z_of == EDGE - 1
    y_first, y_last = lane < EDGE, lane >= PLANE - EDGE
    zero = jnp.zeros((CIN, PLANE), BF)
    before, current = carry if carry is not None else (None, None)
    for x in range(first, stop):
        centre = block(x)
        z_less = jnp.where(z_first, zero, roll(centre, 1))
        z_more = jnp.where(z_last, zero, roll(centre, -1))
        buffer = x % 2
        for tap_z, value in enumerate((z_less, centre, z_more)):
            for tap_y in range(3):
                if tap_y == 0:
                    shifted = jnp.where(y_first, zero, roll(value, EDGE))
                elif tap_y == 1:
                    shifted = value
                else:
                    shifted = jnp.where(y_last, zero, roll(value, -EDGE))
                start = (tap_y * 3 + tap_z) * CIN
                columns[buffer, start : start + CIN, :] = shifted
        part = jnp.dot(wall[...], columns[buffer], preferred_element_type=F32)
        if x > 0:
            write(x - 1, before + part[2 * COUT :])
            before = current + part[COUT : 2 * COUT]
        else:
            before = part[COUT : 2 * COUT]
        current = part[:COUT]
    if stop == EDGE:
        write(EDGE - 1, before)
    return before, current


def write_plane(acc):
    def write(x, value):
        acc[:, x * PLANE : (x + 1) * PLANE] = value

    return write


def plane_of(block):
    return lambda x: block[:, x * PLANE : (x + 1) * PLANE]


def pack_and_convolve(blocks, weight, held, faces_y, faces_z, acc, wall, columns, first, weights, sems, weight_sem):
    width = VOX // CHUNK
    copies = []
    for slot in range(SLOTS):
        for part in range(CHUNK):
            at = pl.ds(part * width, width)
            copies.append(
                pltpu.make_async_copy(
                    blocks.at[slot, :, at], (first, held)[slot].at[:, at], sems.at[slot * CHUNK + part]
                )
            )
    weight_copy = pltpu.make_async_copy(weight, weights, weight_sem)
    copies[0].start()
    weight_copy.start()
    for copy in copies[1:]:
        copy.start()
    lane = lanes(CIN, PLANE)
    half_lane = lanes(CIN, 128)
    for slot in range(SLOTS):
        planes_z = [jnp.zeros((CIN, PLANE), BF)] * 2
        halves = [[jnp.zeros((CIN, 128), BF)] * 2 for _ in range(2)]
        for x in range(EDGE):
            if x % (EDGE // CHUNK) == 0:
                copies[slot * CHUNK + x // (EDGE // CHUNK)].wait()
            centre = (first, held)[slot][:, x * PLANE : (x + 1) * PLANE]
            for side in range(2):
                planes_z[side] = jnp.where(
                    lane % EDGE == x, roll(centre, x - last(side)), planes_z[side]
                )
                half = centre[:, 128:] if side == 0 else centre[:, :128]
                at = (x % 8) * EDGE
                moved = roll(half, at - (112 if side == 0 else 0))
                halves[side][x // 8] = jnp.where(
                    half_lane // EDGE == x % 8, moved, halves[side][x // 8]
                )
        for side in range(2):
            faces_z[side * 2 + slot] = planes_z[side]
            faces_y[side * 2 + slot, :, :128] = halves[side][0]
            faces_y[side * 2 + slot, :, 128:] = halves[side][1]
        if slot == 0:
            weight_copy.wait()
            for tap_x in range(3):
                wall[tap_x * COUT : (tap_x + 1) * COUT, :] = weights[
                    :, tap_x * TAPS * CIN : (tap_x + 1) * TAPS * CIN
                ]
            interior(plane_of(first), wall, columns, write_plane(acc), 0, EDGE)


def begin_second(held, wall, tie, acc, carry, columns):
    before, current = interior(plane_of(held), wall, columns, write_plane(acc), 0, SPLIT)
    carry[0], carry[1] = before, current


def pack_for_y(faces_y, far_a, far_b, out):
    parity, _, at_y = place()
    odd_x = parity == 1
    for slot in range(SLOTS):
        out[slot, :, :PLANE] = faces_y[at_y * 2 + slot]
        start = pl.multiple_of((1 - at_y) * 128, 128)
        a = far_a[slot, :, pl.ds(start, 128)]
        b = far_b[slot, :, pl.ds(start, 128)]
        out[slot, :, PLANE : PLANE + 128] = jnp.where(odd_x, a, b)
        out[slot, :, PLANE + 128 :] = jnp.where(odd_x, b, a)


def pack_for_z(faces_z, far_a, far_b, far_y, out_a, out_b):
    parity_x, parity_z, at_y = place()
    odd_x, odd_z = parity_x == 1, parity_z == 1
    lane = lanes(CIN, PLANE)
    half_lane = lanes(CIN, 128)
    row = at_y * 112
    packs = []
    for side in range(2):
        z = last(side)
        pack = jnp.zeros((CIN, PLANE), BF)
        corner = jnp.zeros((CIN, 128), BF)
        for slot in range(SLOTS):
            a, b = far_a[slot], far_b[slot]
            pair = (jnp.where(odd_x, a, b), jnp.where(odd_x, b, a))
            for d in range(2):
                k = d * 2 + slot
                pack = jnp.where(lane % EDGE == k, roll(pair[d], k - z), pack)
                edge = far_y[slot, :, PLANE + d * 128 : PLANE + (d + 1) * 128]
                moved = pltpu.roll(edge, (6 + k - z - row + 128) % 128, 1)
                corner = jnp.where(half_lane == 6 + k, moved, corner)
            k = 4 + slot
            pack = jnp.where(lane % EDGE == k, roll(far_y[slot, :, :PLANE], k - z), pack)
        low = jnp.where((half_lane >= 6) & (half_lane < 10), corner, pack[:, :128])
        packs.append((low, pack[:, 128:]))
    first, second = packs
    for part in range(2):
        at = slice(part * 128, (part + 1) * 128)
        out_a[2, :, at] = jnp.where(odd_z, second[part], first[part])
        out_b[2, :, at] = jnp.where(odd_z, first[part], second[part])
    for slot in range(SLOTS):
        out_a[slot] = faces_z[parity_z * 2 + slot]
        out_b[slot] = faces_z[(1 - parity_z) * 2 + slot]


def pick(code, choices):
    result = choices[-1][1]
    for known, value in reversed(choices[:-1]):
        result = jnp.where(code == known, value, result)
    return result


def sign(side):
    return -1 if side == 0 else 1


def link(links, slot, dx, dy, dz):
    index = (dx + 1) * 9 + (dy + 1) * 3 + dz + 1
    value = links[slot, index if index < 13 else index - 1]
    clean = jnp.maximum(value, 0)
    return value >= 0, clean // 2, clean % 2


def whole(table, present, index):
    return jnp.where(present, table[index], jnp.zeros((CIN, PLANE), BF))


def column(table, present, index, source, side):
    target = 0 if side == 0 else EDGE - 1
    moved = pltpu.roll(table[index], (target - source + PLANE) % PLANE, 1)
    return jnp.where(present, moved, jnp.zeros((CIN, PLANE), BF))


def short(table, present, index, source, target):
    start = pl.multiple_of((source // 128) * 128, 128)
    value = table[index, :, pl.ds(start, 128)]
    moved = pltpu.roll(value, (target - source % 128 + 128) % 128, 1)
    return jnp.where(present, moved, jnp.zeros((CIN, 128), BF))


def put_corner(row, side, value):
    return jnp.where(lanes(CIN, 128) == (127 if side == 0 else EDGE), value, row)


def fill_columns(columns, buffer, centre, sides, rows):
    lane = lanes(CIN, PLANE)
    half_lane = lanes(CIN, 128)
    less = jnp.where(lane % EDGE == 0, sides[0], roll(centre, 1))
    more = jnp.where(lane % EDGE == EDGE - 1, sides[1], roll(centre, -1))
    for minor, value in enumerate((less, centre, more)):
        low, high = roll(rows[0], 1 - minor), roll(rows[1], 113 - minor)
        for major in range(3):
            start = (major * 3 + minor) * CIN
            at = slice(start, start + CIN)
            if major == 1:
                columns[buffer, at, :] = value
            elif major == 0:
                shifted = roll(value, EDGE)
                columns[buffer, at, :128] = jnp.where(half_lane < EDGE, low, shifted[:, :128])
                columns[buffer, at, 128:] = shifted[:, 128:]
            else:
                shifted = roll(value, -EDGE)
                columns[buffer, at, :128] = shifted[:, :128]
                columns[buffer, at, 128:] = jnp.where(half_lane >= 112, high, shifted[:, 128:])


def any_of(terms):
    result = terms[0]
    for term in terms[1:]:
        result = result | term
    return result


def near(links, slot, dx, dy, dz):
    present, code, _ = link(links, slot, dx, dy, dz)
    return present & (code < 4)


def add_rows(acc, sheet, side):
    half_o = lanes(COUT, 128)
    none = jnp.zeros((COUT, 128), F32)
    for x in range(EDGE):
        part = sheet[:, (x // 8) * 128 : (x // 8 + 1) * 128]
        if side == 0:
            moved = jnp.where(half_o < EDGE, roll(part, -(x % 8) * EDGE), none)
            at = slice(x * PLANE, x * PLANE + 128)
        else:
            moved = jnp.where(half_o >= 112, roll(part, 112 - (x % 8) * EDGE), none)
            at = slice(x * PLANE + 128, (x + 1) * PLANE)
        acc[:, at] = acc[:, at] + moved


def spread(sheet, side, x):
    lane_o = lanes(COUT, PLANE)
    moved = roll(sheet, last(1 - side) - x)
    return jnp.where(lane_o % EDGE == last(1 - side), moved, jnp.zeros((COUT, PLANE), F32))


def near_x(links, table, wall, columns, acc, slot, d):
    present, code, u = link(links, slot, sign(d), 0, 0)
    centre = whole(table, present, jnp.minimum(code, 1) * 4 + d * 2 + u)
    sides = []
    for f in range(2):
        present, code, u = link(links, slot, sign(d), 0, sign(f))
        index = jnp.minimum(code, 1) * 4 + d * 2 + u
        sides.append(column(table, present & (code < 4), index, last(f), f))
    rows = []
    for e in range(2):
        far = 112 if e == 0 else 0

        def index_of(code, u):
            return pick(
                code,
                (
                    (0, OWN_X + d * 2 + u),
                    (1, FAR_X + d * 2 + u),
                    (2, FAR_Y + u),
                    (3, EDGE_Y + d * 2 + u),
                ),
            )

        def start_of(code):
            return pick(
                code, ((0, last(e) * EDGE), (1, last(e) * EDGE), (2, last(d) * EDGE), (3, far))
            )

        present, code, u = link(links, slot, sign(d), sign(e), 0)
        row = short(table, present, index_of(code, u), start_of(code), 0)
        for f in range(2):
            present, code, u = link(links, slot, sign(d), sign(e), sign(f))
            target = 127 if f == 0 else EDGE
            source = start_of(code) + last(f)
            value = short(table, present & (code < 4), index_of(code, u), source, target)
            row = put_corner(row, f, value)
        rows.append(row)
    fill_columns(columns, d, centre, sides, rows)
    taps = wall[2 * d * COUT : (2 * d + 1) * COUT, :]
    x = last(1 - d)
    at = slice(x * PLANE, (x + 1) * PLANE)
    acc[:, at] = acc[:, at] + jnp.dot(taps, columns[d], preferred_element_type=F32)


def near_y(links, table, wall, columns, acc, slot, e):
    lane = lanes(CIN, PLANE)
    lane_o = lanes(COUT, PLANE)
    none = jnp.zeros((COUT, PLANE), F32)
    present, code, u = link(links, slot, 0, sign(e), 0)
    centre = whole(table, present, jnp.where(code == 0, OWN_Y + e * 2 + u, FAR_Y + u))
    sides = []
    for f in range(2):
        present, code, u = link(links, slot, 0, sign(e), sign(f))
        index = jnp.where(code == 0, OWN_Y + e * 2 + u, FAR_Y + u)
        sides.append(column(table, present & (code < 4), index, last(f), f))
    columns[e, :CIN, :] = jnp.where(lane % EDGE == 0, sides[0], roll(centre, 1))
    columns[e, CIN : 2 * CIN, :] = centre
    columns[e, 2 * CIN : 3 * CIN, :] = jnp.where(lane % EDGE == EDGE - 1, sides[1], roll(centre, -1))
    taps = wall[:, 2 * e * 3 * CIN : (2 * e + 1) * 3 * CIN]
    part = jnp.dot(taps, columns[e, : 3 * CIN, :], preferred_element_type=F32)
    sheet = part[COUT : 2 * COUT]
    sheet = sheet + jnp.where(lane_o < EDGE, none, roll(part[:COUT], EDGE))
    sheet = sheet + jnp.where(lane_o >= PLANE - EDGE, none, roll(part[2 * COUT :], -EDGE))
    add_rows(acc, sheet, e)


def near_z(links, faces_z, wall, columns, acc, slot, f):
    lane = lanes(CIN, PLANE)
    zero = jnp.zeros((CIN, PLANE), BF)
    lane_o = lanes(COUT, PLANE)
    none = jnp.zeros((COUT, PLANE), F32)
    _, _, u = link(links, slot, 0, 0, sign(f))
    centre = faces_z[f * 2 + u]
    columns[f, :CIN, :] = jnp.where(lane < EDGE, zero, roll(centre, EDGE))
    columns[f, CIN : 2 * CIN, :] = centre
    columns[f, 2 * CIN : 3 * CIN, :] = jnp.where(lane >= PLANE - EDGE, zero, roll(centre, -EDGE))
    taps = jnp.concatenate(
        [
            wall[:, (tap_y * 3 + 2 * f) * CIN : (tap_y * 3 + 2 * f + 1) * CIN]
            for tap_y in range(3)
        ],
        1,
    )
    part = jnp.dot(taps, columns[f, : 3 * CIN, :], preferred_element_type=F32)
    sheet = part[COUT : 2 * COUT]
    sheet = sheet + jnp.where(lane_o % EDGE == 0, none, roll(part[:COUT], 1))
    sheet = sheet + jnp.where(lane_o % EDGE == EDGE - 1, none, roll(part[2 * COUT :], -1))
    for x in range(EDGE):
        at = slice(x * PLANE, (x + 1) * PLANE)
        acc[:, at] = acc[:, at] + spread(sheet, f, x)


def finish_second(
    links_in, held, wall, tie, carry, part_acc, acc_in, own_a, own_b, far_a, far_b, faces_y,
    far_y, faces_z, acc_a, acc_b, walls_z, columns, table, links, sem
):
    fetch = pltpu.make_async_copy(links_in, links, sem)
    fetch.start()
    parity_x, _, _ = place()
    odd_x = parity_x == 1
    for slot in range(SLOTS):
        a, b = own_a[slot], own_b[slot]
        table[OWN_X + slot] = jnp.where(odd_x, b, a)
        table[OWN_X + 2 + slot] = jnp.where(odd_x, a, b)
        a, b = far_a[slot], far_b[slot]
        table[FAR_X + slot] = jnp.where(odd_x, a, b)
        table[FAR_X + 2 + slot] = jnp.where(odd_x, b, a)
        table[FAR_Y + slot] = far_y[slot, :, :PLANE]
        for d in range(2):
            table[OWN_Y + d * 2 + slot] = faces_y[d * 2 + slot]
            table[EDGE_Y + d * 2 + slot, :, :128] = far_y[
                slot, :, PLANE + d * 128 : PLANE + (d + 1) * 128
            ]
            table[EDGE_Y + d * 2 + slot, :, 128:] = jnp.zeros((CIN, 128), BF)
    for x in range(EDGE):
        at = slice(x * PLANE, (x + 1) * PLANE)
        acc_a[:, at] = acc_in[:, at]
        if x < SPLIT - 1:
            acc_b[:, at] = part_acc[:, at]
    interior(plane_of(held), wall, columns, write_plane(acc_b), SPLIT, EDGE, (carry[0], carry[1]))
    for f in range(2):
        for tap_y in range(3):
            for tap_x in range(3):
                start = (tap_y * 3 + tap_x) * CIN
                source = (tap_y * 3 + 2 * f) * CIN
                walls_z[f, :, start : start + CIN] = wall[
                    tap_x * COUT : (tap_x + 1) * COUT, source : source + CIN
                ]
    fetch.wait()
    accs = (acc_a, acc_b)
    steps = (-1, 0, 1)
    for slot in range(SLOTS):
        acc = accs[slot]
        for d in range(2):
            wanted = any_of(
                [near(links, slot, sign(d), dy, dz) for dy in steps for dz in steps]
            )

            @pl.when(wanted)
            def _():
                near_x(links, table, wall, columns, acc, slot, d)

        for e in range(2):

            @pl.when(any_of([near(links, slot, 0, sign(e), dz) for dz in steps]))
            def _():
                near_y(links, table, wall, columns, acc, slot, e)

        for f in range(2):

            @pl.when(near(links, slot, 0, 0, sign(f)))
            def _():
                near_z(links, faces_z, wall, columns, acc, slot, f)


def far_z(links, table, walls_z, columns, slot, f):
    present, code, u = link(links, slot, 0, 0, sign(f))
    centre = whole(table, present & (code >= 4), FAR_Z + f * 2 + u)
    sides = []
    for d in range(2):
        present, code, u = link(links, slot, sign(d), 0, sign(f))
        index = jnp.where(code == 4, FAR_Z + f * 2 + u, EDGE_Z + f)
        source = jnp.where(code == 4, last(d), d * 2 + u)
        sides.append(column(table, present & (code >= 4), index, source, d))
    rows = []
    for e in range(2):
        present, code, u = link(links, slot, 0, sign(e), sign(f))
        index = jnp.where(code == 4, FAR_Z + f * 2 + u, TURN_Z + f)
        source = jnp.where(code == 4, last(e) * EDGE, (4 + u) * EDGE)
        row = short(table, present & (code >= 4), index, source, 0)
        for d in range(2):
            present, code, u = link(links, slot, sign(d), sign(e), sign(f))
            index = jnp.where(code == 4, FAR_Z + f * 2 + u, EDGE_Z + f)
            source = pick(
                code,
                (
                    (4, last(e) * EDGE + last(d)),
                    (5, last(e) * EDGE + d * 2 + u),
                    (6, last(d) * EDGE + 4 + u),
                    (7, 6 + d * 2 + u),
                ),
            )
            target = 127 if d == 0 else EDGE
            value = short(table, present & (code >= 4), index, source, target)
            row = put_corner(row, d, value)
        rows.append(row)
    fill_columns(columns, f, centre, sides, rows)
    return jnp.dot(walls_z[f], columns[f], preferred_element_type=F32)


def upright(row):
    size = row.shape[1]
    across = lax.broadcasted_iota(jnp.int32, (size, size), 1)
    down = lax.broadcasted_iota(jnp.int32, (size, size), 0)
    wide = jnp.where(across == down, jnp.broadcast_to(row, (size, size)), 0.0)
    return jnp.sum(wide, axis=1, keepdims=True)


def finish(
    links_in, count_in, acc_a, acc_b, got_a, got_b, walls_z, bias_row, head, head_bias_row, turn,
    out, columns, table, sheets, links, count, sems
):
    fetch_links = pltpu.make_async_copy(links_in, links, sems.at[0])
    fetch_count = pltpu.make_async_copy(count_in, count, sems.at[1])
    fetch_links.start()
    fetch_count.start()
    _, parity_z, _ = place()
    odd_z = parity_z == 1
    bias, head_bias = upright(bias_row[...]), upright(head_bias_row[...])
    weights = head[...]
    for slot in range(SLOTS):
        a, b = got_a[slot], got_b[slot]
        table[FAR_Z + slot] = jnp.where(odd_z, a, b)
        table[FAR_Z + 2 + slot] = jnp.where(odd_z, b, a)
    a, b = got_a[2], got_b[2]
    for f, value in enumerate((jnp.where(odd_z, a, b), jnp.where(odd_z, b, a))):
        table[EDGE_Z + f] = value
        table[TURN_Z + f] = jnp.dot(value, turn[...], preferred_element_type=F32).astype(BF)
    fetch_links.wait()
    fetch_count.wait()
    accs = (acc_a, acc_b)
    steps = (-1, 0, 1)

    def emit(slot, total, x):
        hidden = jnp.maximum(total + bias, 0.0).astype(BF)
        mixed = jnp.dot(weights, hidden, preferred_element_type=F32) + head_bias
        out[slot, :, x * PLANE : (x + 1) * PLANE] = mixed.astype(BF)

    for slot in range(SLOTS):
        acc = accs[slot]
        wanted = []
        for f in range(2):
            terms = []
            for dx in steps:
                for dy in steps:
                    present, code, _ = link(links, slot, dx, dy, sign(f))
                    terms.append(present & (code >= 4))
            wanted.append(any_of(terms))
        used = slot < count[0, 0, 0]
        both = wanted[0] | wanted[1]

        @pl.when(used & both)
        def _():
            for f in range(2):

                @pl.when(wanted[f])
                def _():
                    sheets[f] = far_z(links, table, walls_z, columns, slot, f)

                @pl.when(jnp.logical_not(wanted[f]))
                def _():
                    sheets[f] = jnp.zeros((COUT, PLANE), F32)

            for x in range(EDGE):
                total = acc[:, x * PLANE : (x + 1) * PLANE]
                total = total + spread(sheets[0], 0, x) + spread(sheets[1], 1, x)
                emit(slot, total, x)

        @pl.when(used & jnp.logical_not(both))
        def _():
            for x in range(EDGE):
                emit(slot, acc[:, x * PLANE : (x + 1) * PLANE], x)

        @pl.when(jnp.logical_not(used))
        def _():
            for x in range(EDGE):
                out[slot, :, x * PLANE : (x + 1) * PLANE] = jnp.zeros((COUT, PLANE), BF)


VMEM = pl.BlockSpec(memory_space=pltpu.VMEM)
HBM = pl.BlockSpec(memory_space=pltpu.HBM)
ANY = pl.BlockSpec(memory_space=pl.ANY)


def shape(dims, kind=BF):
    return jax.ShapeDtypeStruct(dims, kind)


def in_hbm(value):
    return pltpu.with_memory_space_constraint(value, pltpu.HBM)


def swap(first, second, axis):
    length = lax.axis_size(axis)
    even = [(i, i ^ 1) for i in range(length)]
    odd = []
    for i in range(length):
        partner = ((i + 1) ^ 1) - 1
        for core in range(2):
            if 0 <= partner < length:
                odd.append((i * 2 + core, partner * 2 + core))
            else:
                odd.append((i * 2 + core, i * 2 + 1 - core))
    return lax.ppermute(first, axis, even), lax.ppermute(second, (axis, "gy"), odd)


def body(blocks, block_count, neighbours, conv_weight, conv_bias, head_weight, head_bias):
    volumes = blocks.reshape(SLOTS, CIN, VOX)
    links = neighbours.reshape(SLOTS, 26)
    odd_x = lax.axis_index("gx") % 2
    far_end = VOX - PLANE
    own_a = lax.dynamic_slice_in_dim(volumes, (1 - odd_x) * far_end, PLANE, 2)
    own_b = lax.dynamic_slice_in_dim(volumes, odd_x * far_end, PLANE, 2)
    far_a, far_b = swap(own_a, own_b, "gx")
    buffer = pltpu.VMEM((2, TAPS * CIN, PLANE), BF)
    block_flops = 2 * COUT * 27 * CIN * VOX
    held, faces_y, faces_z, acc_a, wall = pl.pallas_call(
        pack_and_convolve,
        out_shape=(
            shape((CIN, VOX)),
            shape((4, CIN, PLANE)),
            shape((4, CIN, PLANE)),
            shape((COUT, VOX), F32),
            shape((3 * COUT, TAPS * CIN)),
        ),
        in_specs=[HBM, HBM],
        out_specs=(VMEM, VMEM, VMEM, VMEM, VMEM),
        scratch_shapes=[
            buffer,
            pltpu.VMEM((CIN, VOX), BF),
            pltpu.VMEM((COUT, 27 * CIN), BF),
            pltpu.SemaphoreType.DMA((SLOTS * CHUNK,)),
            pltpu.SemaphoreType.DMA,
        ],
        compiler_params=params(16),
        cost_estimate=pl.CostEstimate(
            flops=2 * block_flops, bytes_accessed=4 * 2**20, transcendentals=0
        ),
    )(in_hbm(volumes), in_hbm(conv_weight))
    sent_y = pl.pallas_call(
        pack_for_y,
        out_shape=shape((SLOTS, CIN, 2 * PLANE)),
        in_specs=[VMEM, VMEM, VMEM],
        out_specs=VMEM,
        compiler_params=params(8),
    )(faces_y, far_a, far_b)
    far_y = lax.ppermute(sent_y, "gy", [(0, 1), (1, 0)])
    part_acc, carry = pl.pallas_call(
        begin_second,
        out_shape=(shape((COUT, (SPLIT - 1) * PLANE), F32), shape((2, COUT, PLANE), F32)),
        in_specs=[VMEM, VMEM, ANY],
        out_specs=(VMEM, VMEM),
        scratch_shapes=[buffer],
        compiler_params=params(16),
        cost_estimate=pl.CostEstimate(
            flops=block_flops, bytes_accessed=2**20, transcendentals=0
        ),
    )(held, wall, sent_y)
    sent_a, sent_b = pl.pallas_call(
        pack_for_z,
        out_shape=(shape((3, CIN, PLANE)), shape((3, CIN, PLANE))),
        in_specs=[VMEM, VMEM, VMEM, VMEM],
        out_specs=(VMEM, VMEM),
        compiler_params=params(8),
    )(faces_z, far_a, far_b, far_y)
    got_a, got_b = swap(sent_a, sent_b, "gz")
    smem_links = pltpu.SMEM((SLOTS, 26), jnp.int32)
    acc_a, acc_b, walls_z = pl.pallas_call(
        finish_second,
        out_shape=(
            shape((COUT, VOX), F32), shape((COUT, VOX), F32), shape((2, COUT, TAPS * CIN))
        ),
        in_specs=[ANY, VMEM, VMEM, ANY] + [VMEM] * 10,
        out_specs=(VMEM,) * 3,
        scratch_shapes=[
            buffer,
            pltpu.VMEM((NEAR_SOURCES, CIN, PLANE), BF),
            smem_links,
            pltpu.SemaphoreType.DMA,
        ],
        compiler_params=params(16),
        cost_estimate=pl.CostEstimate(
            flops=2 * block_flops, bytes_accessed=2 * 2**20, transcendentals=0
        ),
    )(
        links, held, wall, sent_a, carry, part_acc, acc_a, own_a, own_b, far_a, far_b, faces_y,
        far_y, faces_z,
    )
    index = jnp.arange(PLANE)
    turn = (index[:, None] == (index % EDGE * EDGE + index // EDGE)[None, :]).astype(BF)
    outputs = pl.pallas_call(
        finish,
        out_shape=shape((SLOTS, COUT, VOX)),
        in_specs=[ANY] * 2 + [VMEM] * 9,
        out_specs=VMEM,
        scratch_shapes=[
            buffer,
            pltpu.VMEM((Z_SOURCES, CIN, PLANE), BF),
            pltpu.VMEM((2, COUT, PLANE), F32),
            smem_links,
            pltpu.SMEM((1, 1, 1), jnp.int32),
            pltpu.SemaphoreType.DMA((2,)),
        ],
        compiler_params=params(16),
    )(
        links, block_count, acc_a, acc_b, got_a, got_b, walls_z, conv_bias.reshape(1, COUT),
        head_weight, head_bias.reshape(1, COUT), turn,
    )
    return outputs.reshape(1, 1, SLOTS, COUT, VOX)


def solution(mesh):
    placed = (
        P("gx", "gz", "gy", None, None),
        P("gx", "gz", "gy"),
        P("gx", "gz", "gy", None),
        P(),
        P(),
        P(),
        P(),
    )
    return jax.shard_map(
        body, mesh=mesh, in_specs=placed, out_specs=P("gx", "gz", "gy", None, None), check_vma=False
    )
```

```python
import jax
import jax.numpy as jnp
from jax import lax
from jax.experimental import pallas as pl
from jax.experimental.pallas import tpu as pltpu
from jax.sharding import PartitionSpec as P

CIN = 96
COUT = 48
EDGE = 16
PLANE = 256
VOX = 4096
SLOTS = 2
TAPS = 9
BF = jnp.bfloat16
F32 = jnp.float32

OWN_X, FAR_X, FAR_Y, OWN_Y, EDGE_Y, NEAR_SOURCES = 0, 4, 8, 10, 14, 18
FAR_Z, EDGE_Z, TURN_Z, Z_SOURCES = 0, 4, 6, 8
Z_WIDTH = SLOTS * PLANE + 128
SPLIT = 11
CHUNK = 4


def params(mib):
    return pltpu.CompilerParams(vmem_limit_bytes=mib * 2**20)


def lanes(rows, width):
    return lax.broadcasted_iota(jnp.int32, (rows, width), 1)


def last(side):
    return EDGE - 1 if side == 0 else 0


def roll(value, shift):
    width = value.shape[1]
    if isinstance(shift, int):
        shift = shift % width
        if shift == 0:
            return value
    return pltpu.roll(value, shift, 1)


def place():
    return lax.axis_index("gx") % 2, lax.axis_index("gz") % 2, lax.axis_index("gy")


def interior(block, wall, columns, write, first, stop, carry=None):
    lane = lanes(CIN, PLANE)
    z_of = lane % EDGE
    z_first, z_last = z_of == 0, z_of == EDGE - 1
    y_first, y_last = lane < EDGE, lane >= PLANE - EDGE
    zero = jnp.zeros((CIN, PLANE), BF)
    before, current = carry if carry is not None else (None, None)
    for x in range(first, stop):
        centre = block(x)
        z_less = jnp.where(z_first, zero, roll(centre, 1))
        z_more = jnp.where(z_last, zero, roll(centre, -1))
        buffer = x % 2
        for tap_z, value in enumerate((z_less, centre, z_more)):
            for tap_y in range(3):
                if tap_y == 0:
                    shifted = jnp.where(y_first, zero, roll(value, EDGE))
                elif tap_y == 1:
                    shifted = value
                else:
                    shifted = jnp.where(y_last, zero, roll(value, -EDGE))
                start = (tap_y * 3 + tap_z) * CIN
                columns[buffer, start : start + CIN, :] = shifted
        part = jnp.dot(wall[...], columns[buffer], preferred_element_type=F32)
        if x > 0:
            write(x - 1, before + part[2 * COUT :])
            before = current + part[COUT : 2 * COUT]
        else:
            before = part[COUT : 2 * COUT]
        current = part[:COUT]
    if stop == EDGE:
        write(EDGE - 1, before)
    return before, current


def write_plane(acc):
    def write(x, value):
        acc[:, x * PLANE : (x + 1) * PLANE] = value

    return write


def plane_of(block):
    return lambda x: block[:, x * PLANE : (x + 1) * PLANE]


def pack_and_convolve(blocks, weight, held, faces_y, faces_z, acc, carry, rest, wall, columns, first, weights, sems, weight_sem):
    width = VOX // CHUNK
    copies = []
    for slot in range(SLOTS):
        for part in range(CHUNK):
            at = pl.ds(part * width, width)
            copies.append(
                pltpu.make_async_copy(
                    blocks.at[slot, :, at], (first, held)[slot].at[:, at], sems.at[slot * CHUNK + part]
                )
            )
    weight_copy = pltpu.make_async_copy(weight, weights, weight_sem)
    copies[0].start()
    weight_copy.start()
    for copy in copies[1:]:
        copy.start()
    lane = lanes(CIN, PLANE)
    half_lane = lanes(CIN, 128)
    for slot in range(SLOTS):
        planes_z = [jnp.zeros((CIN, PLANE), BF)] * 2
        halves = [[jnp.zeros((CIN, 128), BF)] * 2 for _ in range(2)]
        for x in range(EDGE):
            if x % (EDGE // CHUNK) == 0:
                copies[slot * CHUNK + x // (EDGE // CHUNK)].wait()
            centre = (first, held)[slot][:, x * PLANE : (x + 1) * PLANE]
            moved = roll(centre, x)
            planes_z[0] = jnp.where(lane % EDGE == (x + EDGE - 1) % EDGE, moved, planes_z[0])
            planes_z[1] = jnp.where(lane % EDGE == x, moved, planes_z[1])
            ends = jnp.where(half_lane < 64, centre[:, :128], centre[:, 128:])
            moved = roll(ends, (x % 8) * EDGE)
            part = x // 8
            halves[0][part] = jnp.where(half_lane // EDGE == (x + 7) % 8, moved, halves[0][part])
            halves[1][part] = jnp.where(half_lane // EDGE == x % 8, moved, halves[1][part])
        faces_z[slot] = roll(planes_z[0], 1 - EDGE)
        faces_z[2 + slot] = planes_z[1]
        for part in range(2):
            at = slice(part * 128, (part + 1) * 128)
            faces_y[slot, :, at] = roll(halves[0][part], EDGE)
            faces_y[2 + slot, :, at] = halves[1][part]
        if slot == 0:
            weight_copy.wait()
            for tap_x in range(3):
                wall[tap_x * COUT : (tap_x + 1) * COUT, :] = weights[
                    :, tap_x * TAPS * CIN : (tap_x + 1) * TAPS * CIN
                ]
            before, current = interior(
                plane_of(first), wall, columns, write_plane(acc), 0, SPLIT
            )
            carry[0], carry[1] = before, current
            rest[...] = first[:, SPLIT * PLANE :]


def end_first(rest, wall, carry, tie, acc, columns):
    def block(x):
        return rest[:, (x - SPLIT) * PLANE : (x - SPLIT + 1) * PLANE]

    def write(x, value):
        x = x - (SPLIT - 1)
        acc[:, x * PLANE : (x + 1) * PLANE] = value

    interior(block, wall, columns, write, SPLIT, EDGE, (carry[0], carry[1]))


def pack_for_y(faces_y, far_a, far_b, out):
    parity, _, at_y = place()
    odd_x = parity == 1
    for slot in range(SLOTS):
        out[slot, :, :PLANE] = faces_y[at_y * 2 + slot]
        start = pl.multiple_of((1 - at_y) * 128, 128)
        a = far_a[slot, :, pl.ds(start, 128)]
        b = far_b[slot, :, pl.ds(start, 128)]
        out[slot, :, PLANE : PLANE + 128] = jnp.where(odd_x, a, b)
        out[slot, :, PLANE + 128 :] = jnp.where(odd_x, b, a)


def corner_lane(k):
    return k // 2 * EDGE + 6 + k % 2


def pack_for_z(faces_z, far_a, far_b, far_y, out_a, out_b):
    parity_x, parity_z, at_y = place()
    odd_x, odd_z = parity_x == 1, parity_z == 1
    lane = lanes(CIN, PLANE)
    half_lane = lanes(CIN, 128)
    row = at_y * 112
    packs = []
    for side in range(2):
        z = last(side)
        pack = jnp.zeros((CIN, PLANE), BF)
        corner = jnp.zeros((CIN, 128), BF)
        for slot in range(SLOTS):
            a, b = far_a[slot], far_b[slot]
            pair = (jnp.where(odd_x, a, b), jnp.where(odd_x, b, a))
            for d in range(2):
                k = d * 2 + slot
                pack = jnp.where(lane % EDGE == k, roll(pair[d], k - z), pack)
                edge = far_y[slot, :, PLANE + d * 128 : PLANE + (d + 1) * 128]
                target = corner_lane(k)
                moved = pltpu.roll(edge, (target - z - row + 128) % 128, 1)
                corner = jnp.where(half_lane == target, moved, corner)
            k = 4 + slot
            pack = jnp.where(lane % EDGE == k, roll(far_y[slot, :, :PLANE], k - z), pack)
        slim = jnp.where(half_lane % EDGE < 8, pack[:, :128], roll(pack[:, 128:], 8))
        packs.append(jnp.where((half_lane % 8 >= 6) & (half_lane % EDGE < 8), corner, slim))
    first, second = packs
    out_a[:, SLOTS * PLANE :] = jnp.where(odd_z, second, first)
    out_b[:, SLOTS * PLANE :] = jnp.where(odd_z, first, second)
    for slot in range(SLOTS):
        at = slice(slot * PLANE, (slot + 1) * PLANE)
        out_a[:, at] = faces_z[parity_z * 2 + slot]
        out_b[:, at] = faces_z[(1 - parity_z) * 2 + slot]


def pick(code, choices):
    result = choices[-1][1]
    for known, value in reversed(choices[:-1]):
        result = jnp.where(code == known, value, result)
    return result


def sign(side):
    return -1 if side == 0 else 1


def link(links, slot, dx, dy, dz):
    index = (dx + 1) * 9 + (dy + 1) * 3 + dz + 1
    value = links[slot, index if index < 13 else index - 1]
    clean = jnp.maximum(value, 0)
    return value >= 0, clean // 2, clean % 2


def whole(table, present, index):
    return jnp.where(present, table[index], jnp.zeros((CIN, PLANE), BF))


def column(table, present, index, source, side):
    target = 0 if side == 0 else EDGE - 1
    moved = pltpu.roll(table[index], (target - source + PLANE) % PLANE, 1)
    return jnp.where(present, moved, jnp.zeros((CIN, PLANE), BF))


def short(table, present, index, source, target):
    start = pl.multiple_of((source // 128) * 128, 128)
    value = table[index, :, pl.ds(start, 128)]
    moved = pltpu.roll(value, (target - source % 128 + 128) % 128, 1)
    return jnp.where(present, moved, jnp.zeros((CIN, 128), BF))


def put_corner(row, side, value):
    return jnp.where(lanes(CIN, 128) == (127 if side == 0 else EDGE), value, row)


def fill_columns(columns, buffer, centre, sides, rows):
    lane = lanes(CIN, PLANE)
    half_lane = lanes(CIN, 128)
    less = jnp.where(lane % EDGE == 0, sides[0], roll(centre, 1))
    more = jnp.where(lane % EDGE == EDGE - 1, sides[1], roll(centre, -1))
    for minor, value in enumerate((less, centre, more)):
        low, high = roll(rows[0], 1 - minor), roll(rows[1], 113 - minor)
        for major in range(3):
            start = (major * 3 + minor) * CIN
            at = slice(start, start + CIN)
            if major == 1:
                columns[buffer, at, :] = value
            elif major == 0:
                shifted = roll(value, EDGE)
                columns[buffer, at, :128] = jnp.where(half_lane < EDGE, low, shifted[:, :128])
                columns[buffer, at, 128:] = shifted[:, 128:]
            else:
                shifted = roll(value, -EDGE)
                columns[buffer, at, :128] = shifted[:, :128]
                columns[buffer, at, 128:] = jnp.where(half_lane >= 112, high, shifted[:, 128:])


def any_of(terms):
    result = terms[0]
    for term in terms[1:]:
        result = result | term
    return result


def near(links, slot, dx, dy, dz):
    present, code, _ = link(links, slot, dx, dy, dz)
    return present & (code < 4)


def add_rows(acc, sheet, side):
    half_o = lanes(COUT, 128)
    none = jnp.zeros((COUT, 128), F32)
    for x in range(EDGE):
        part = sheet[:, (x // 8) * 128 : (x // 8 + 1) * 128]
        if side == 0:
            moved = jnp.where(half_o < EDGE, roll(part, -(x % 8) * EDGE), none)
            at = slice(x * PLANE, x * PLANE + 128)
        else:
            moved = jnp.where(half_o >= 112, roll(part, 112 - (x % 8) * EDGE), none)
            at = slice(x * PLANE + 128, (x + 1) * PLANE)
        acc[:, at] = acc[:, at] + moved


def spread(sheet, side, x):
    lane_o = lanes(COUT, PLANE)
    moved = roll(sheet, last(1 - side) - x)
    return jnp.where(lane_o % EDGE == last(1 - side), moved, jnp.zeros((COUT, PLANE), F32))


def near_x(links, table, wall, columns, acc, slot, d):
    present, code, u = link(links, slot, sign(d), 0, 0)
    centre = whole(table, present, jnp.minimum(code, 1) * 4 + d * 2 + u)
    sides = []
    for f in range(2):
        present, code, u = link(links, slot, sign(d), 0, sign(f))
        index = jnp.minimum(code, 1) * 4 + d * 2 + u
        sides.append(column(table, present & (code < 4), index, last(f), f))
    rows = []
    for e in range(2):
        far = 112 if e == 0 else 0

        def index_of(code, u):
            return pick(
                code,
                (
                    (0, OWN_X + d * 2 + u),
                    (1, FAR_X + d * 2 + u),
                    (2, FAR_Y + u),
                    (3, EDGE_Y + d * 2 + u),
                ),
            )

        def start_of(code):
            return pick(
                code, ((0, last(e) * EDGE), (1, last(e) * EDGE), (2, last(d) * EDGE), (3, far))
            )

        present, code, u = link(links, slot, sign(d), sign(e), 0)
        row = short(table, present, index_of(code, u), start_of(code), 0)
        for f in range(2):
            present, code, u = link(links, slot, sign(d), sign(e), sign(f))
            target = 127 if f == 0 else EDGE
            source = start_of(code) + last(f)
            value = short(table, present & (code < 4), index_of(code, u), source, target)
            row = put_corner(row, f, value)
        rows.append(row)
    fill_columns(columns, d, centre, sides, rows)
    taps = wall[2 * d * COUT : (2 * d + 1) * COUT, :]
    x = last(1 - d)
    at = slice(x * PLANE, (x + 1) * PLANE)
    acc[:, at] = acc[:, at] + jnp.dot(taps, columns[d], preferred_element_type=F32)


def near_y(links, table, wall, columns, acc, slot, e):
    lane = lanes(CIN, PLANE)
    lane_o = lanes(COUT, PLANE)
    none = jnp.zeros((COUT, PLANE), F32)
    present, code, u = link(links, slot, 0, sign(e), 0)
    centre = whole(table, present, jnp.where(code == 0, OWN_Y + e * 2 + u, FAR_Y + u))
    sides = []
    for f in range(2):
        present, code, u = link(links, slot, 0, sign(e), sign(f))
        index = jnp.where(code == 0, OWN_Y + e * 2 + u, FAR_Y + u)
        sides.append(column(table, present & (code < 4), index, last(f), f))
    columns[e, :CIN, :] = jnp.where(lane % EDGE == 0, sides[0], roll(centre, 1))
    columns[e, CIN : 2 * CIN, :] = centre
    columns[e, 2 * CIN : 3 * CIN, :] = jnp.where(lane % EDGE == EDGE - 1, sides[1], roll(centre, -1))
    taps = wall[:, 2 * e * 3 * CIN : (2 * e + 1) * 3 * CIN]
    part = jnp.dot(taps, columns[e, : 3 * CIN, :], preferred_element_type=F32)
    sheet = part[COUT : 2 * COUT]
    sheet = sheet + jnp.where(lane_o < EDGE, none, roll(part[:COUT], EDGE))
    sheet = sheet + jnp.where(lane_o >= PLANE - EDGE, none, roll(part[2 * COUT :], -EDGE))
    add_rows(acc, sheet, e)


def near_z(links, faces_z, wall, columns, acc, slot, f):
    lane = lanes(CIN, PLANE)
    zero = jnp.zeros((CIN, PLANE), BF)
    lane_o = lanes(COUT, PLANE)
    none = jnp.zeros((COUT, PLANE), F32)
    _, _, u = link(links, slot, 0, 0, sign(f))
    centre = faces_z[f * 2 + u]
    columns[f, :CIN, :] = jnp.where(lane < EDGE, zero, roll(centre, EDGE))
    columns[f, CIN : 2 * CIN, :] = centre
    columns[f, 2 * CIN : 3 * CIN, :] = jnp.where(lane >= PLANE - EDGE, zero, roll(centre, -EDGE))
    taps = jnp.concatenate(
        [
            wall[:, (tap_y * 3 + 2 * f) * CIN : (tap_y * 3 + 2 * f + 1) * CIN]
            for tap_y in range(3)
        ],
        1,
    )
    part = jnp.dot(taps, columns[f, : 3 * CIN, :], preferred_element_type=F32)
    sheet = part[COUT : 2 * COUT]
    sheet = sheet + jnp.where(lane_o % EDGE == 0, none, roll(part[:COUT], 1))
    sheet = sheet + jnp.where(lane_o % EDGE == EDGE - 1, none, roll(part[2 * COUT :], -1))
    for x in range(EDGE):
        at = slice(x * PLANE, (x + 1) * PLANE)
        acc[:, at] = acc[:, at] + spread(sheet, f, x)


def finish_second(
    links_in, held, wall, tie, low_acc, high_acc, own_a, own_b, far_a, far_b, faces_y,
    far_y, faces_z, acc_a, acc_b, walls_z, columns, table, links, sem
):
    fetch = pltpu.make_async_copy(links_in, links, sem)
    fetch.start()
    parity_x, _, _ = place()
    odd_x = parity_x == 1
    for slot in range(SLOTS):
        a, b = own_a[slot], own_b[slot]
        table[OWN_X + slot] = jnp.where(odd_x, b, a)
        table[OWN_X + 2 + slot] = jnp.where(odd_x, a, b)
        a, b = far_a[slot], far_b[slot]
        table[FAR_X + slot] = jnp.where(odd_x, a, b)
        table[FAR_X + 2 + slot] = jnp.where(odd_x, b, a)
        table[FAR_Y + slot] = far_y[slot, :, :PLANE]
        for d in range(2):
            table[OWN_Y + d * 2 + slot] = faces_y[d * 2 + slot]
            table[EDGE_Y + d * 2 + slot, :, :128] = far_y[
                slot, :, PLANE + d * 128 : PLANE + (d + 1) * 128
            ]
            table[EDGE_Y + d * 2 + slot, :, 128:] = jnp.zeros((CIN, 128), BF)
    for x in range(EDGE):
        at = slice(x * PLANE, (x + 1) * PLANE)
        if x < SPLIT - 1:
            acc_a[:, at] = low_acc[:, at]
        else:
            source = x - (SPLIT - 1)
            acc_a[:, at] = high_acc[:, source * PLANE : (source + 1) * PLANE]
    interior(plane_of(held), wall, columns, write_plane(acc_b), 0, EDGE)
    for f in range(2):
        for tap_y in range(3):
            for tap_x in range(3):
                start = (tap_y * 3 + tap_x) * CIN
                source = (tap_y * 3 + 2 * f) * CIN
                walls_z[f, :, start : start + CIN] = wall[
                    tap_x * COUT : (tap_x + 1) * COUT, source : source + CIN
                ]
    fetch.wait()
    accs = (acc_a, acc_b)
    steps = (-1, 0, 1)
    for slot in range(SLOTS):
        acc = accs[slot]
        for d in range(2):
            wanted = any_of(
                [near(links, slot, sign(d), dy, dz) for dy in steps for dz in steps]
            )

            @pl.when(wanted)
            def _():
                near_x(links, table, wall, columns, acc, slot, d)

        for e in range(2):

            @pl.when(any_of([near(links, slot, 0, sign(e), dz) for dz in steps]))
            def _():
                near_y(links, table, wall, columns, acc, slot, e)

        for f in range(2):

            @pl.when(near(links, slot, 0, 0, sign(f)))
            def _():
                near_z(links, faces_z, wall, columns, acc, slot, f)


def far_z(links, table, walls_z, columns, slot, f):
    present, code, u = link(links, slot, 0, 0, sign(f))
    centre = whole(table, present & (code >= 4), FAR_Z + f * 2 + u)
    sides = []
    for d in range(2):
        present, code, u = link(links, slot, sign(d), 0, sign(f))
        index = jnp.where(code == 4, FAR_Z + f * 2 + u, EDGE_Z + f)
        source = jnp.where(code == 4, last(d), d * 2 + u)
        sides.append(column(table, present & (code >= 4), index, source, d))
    rows = []
    for e in range(2):
        present, code, u = link(links, slot, 0, sign(e), sign(f))
        index = jnp.where(code == 4, FAR_Z + f * 2 + u, TURN_Z + f)
        source = jnp.where(code == 4, last(e) * EDGE, (4 + u) * EDGE)
        row = short(table, present & (code >= 4), index, source, 0)
        for d in range(2):
            present, code, u = link(links, slot, sign(d), sign(e), sign(f))
            index = jnp.where(code == 4, FAR_Z + f * 2 + u, EDGE_Z + f)
            source = pick(
                code,
                (
                    (4, last(e) * EDGE + last(d)),
                    (5, last(e) * EDGE + d * 2 + u),
                    (6, last(d) * EDGE + 4 + u),
                    (7, d * EDGE + 6 + u),
                ),
            )
            target = 127 if d == 0 else EDGE
            value = short(table, present & (code >= 4), index, source, target)
            row = put_corner(row, d, value)
        rows.append(row)
    fill_columns(columns, f, centre, sides, rows)
    return jnp.dot(walls_z[f], columns[f], preferred_element_type=F32)


def upright(row):
    size = row.shape[1]
    across = lax.broadcasted_iota(jnp.int32, (size, size), 1)
    down = lax.broadcasted_iota(jnp.int32, (size, size), 0)
    wide = jnp.where(across == down, jnp.broadcast_to(row, (size, size)), 0.0)
    return jnp.sum(wide, axis=1, keepdims=True)


def finish(
    links_in, count_in, acc_a, acc_b, got_a, got_b, walls_z, bias_row, head, head_bias_row, turn,
    out_far, columns, table, sheets, out, links, count, sems, out_sems
):
    fetch_links = pltpu.make_async_copy(links_in, links, sems.at[0])
    fetch_count = pltpu.make_async_copy(count_in, count, sems.at[1])
    fetch_links.start()
    fetch_count.start()
    _, parity_z, _ = place()
    odd_z = parity_z == 1
    bias, head_bias = upright(bias_row[...]), upright(head_bias_row[...])
    weights = head[...]
    for slot in range(SLOTS):
        at = slice(slot * PLANE, (slot + 1) * PLANE)
        a, b = got_a[:, at], got_b[:, at]
        table[FAR_Z + slot] = jnp.where(odd_z, a, b)
        table[FAR_Z + 2 + slot] = jnp.where(odd_z, b, a)
    a, b = got_a[:, SLOTS * PLANE :], got_b[:, SLOTS * PLANE :]
    for f, value in enumerate((jnp.where(odd_z, a, b), jnp.where(odd_z, b, a))):
        table[EDGE_Z + f, :, :128] = value
        table[EDGE_Z + f, :, 128:] = roll(value, -8)
        table[TURN_Z + f] = jnp.dot(
            table[EDGE_Z + f], turn[...], preferred_element_type=F32
        ).astype(BF)
    fetch_links.wait()
    fetch_count.wait()
    accs = (acc_a, acc_b)
    steps = (-1, 0, 1)

    def emit(slot, total, x):
        hidden = jnp.maximum(total + bias, 0.0).astype(BF)
        mixed = jnp.dot(weights, hidden, preferred_element_type=F32) + head_bias
        out[slot, :, x * PLANE : (x + 1) * PLANE] = mixed.astype(BF)
        ship(slot, x)

    width = VOX // CHUNK

    def copy_out(slot, part):
        at = pl.ds(part * width, width)
        return pltpu.make_async_copy(
            out.at[slot, :, at], out_far.at[slot, :, at], out_sems.at[slot * CHUNK + part]
        )

    def ship(slot, x):
        if (x + 1) % (EDGE // CHUNK) == 0:
            copy_out(slot, x // (EDGE // CHUNK)).start()

    for slot in range(SLOTS):
        acc = accs[slot]
        wanted = []
        for f in range(2):
            terms = []
            for dx in steps:
                for dy in steps:
                    present, code, _ = link(links, slot, dx, dy, sign(f))
                    terms.append(present & (code >= 4))
            wanted.append(any_of(terms))
        used = slot < count[0, 0, 0]
        both = wanted[0] | wanted[1]

        @pl.when(used & both)
        def _():
            for f in range(2):

                @pl.when(wanted[f])
                def _():
                    sheets[f] = far_z(links, table, walls_z, columns, slot, f)

                @pl.when(jnp.logical_not(wanted[f]))
                def _():
                    sheets[f] = jnp.zeros((COUT, PLANE), F32)

            for x in range(EDGE):
                total = acc[:, x * PLANE : (x + 1) * PLANE]
                total = total + spread(sheets[0], 0, x) + spread(sheets[1], 1, x)
                emit(slot, total, x)

        @pl.when(used & jnp.logical_not(both))
        def _():
            for x in range(EDGE):
                emit(slot, acc[:, x * PLANE : (x + 1) * PLANE], x)

        @pl.when(jnp.logical_not(used))
        def _():
            for x in range(EDGE):
                out[slot, :, x * PLANE : (x + 1) * PLANE] = jnp.zeros((COUT, PLANE), BF)
                ship(slot, x)

    for slot in range(SLOTS):
        for part in range(CHUNK):
            copy_out(slot, part).wait()


VMEM = pl.BlockSpec(memory_space=pltpu.VMEM)
HBM = pl.BlockSpec(memory_space=pltpu.HBM)
ANY = pl.BlockSpec(memory_space=pl.ANY)


def shape(dims, kind=BF):
    return jax.ShapeDtypeStruct(dims, kind)


def in_hbm(value):
    return pltpu.with_memory_space_constraint(value, pltpu.HBM)


def swap(first, second, axis):
    length = lax.axis_size(axis)
    even = [(i, i ^ 1) for i in range(length)]
    odd = []
    for i in range(length):
        partner = ((i + 1) ^ 1) - 1
        for core in range(2):
            if 0 <= partner < length:
                odd.append((i * 2 + core, partner * 2 + core))
            else:
                odd.append((i * 2 + core, i * 2 + 1 - core))
    return lax.ppermute(first, axis, even), lax.ppermute(second, (axis, "gy"), odd)


def body(blocks, block_count, neighbours, conv_weight, conv_bias, head_weight, head_bias):
    volumes = blocks.reshape(SLOTS, CIN, VOX)
    links = neighbours.reshape(SLOTS, 26)
    odd_x = lax.axis_index("gx") % 2
    far_end = VOX - PLANE
    own_a = lax.dynamic_slice_in_dim(volumes, (1 - odd_x) * far_end, PLANE, 2)
    own_b = lax.dynamic_slice_in_dim(volumes, odd_x * far_end, PLANE, 2)
    far_a, far_b = swap(own_a, own_b, "gx")
    buffer = pltpu.VMEM((2, TAPS * CIN, PLANE), BF)
    block_flops = 2 * COUT * 27 * CIN * VOX
    held, faces_y, faces_z, low_acc, carry, rest, wall = pl.pallas_call(
        pack_and_convolve,
        out_shape=(
            shape((CIN, VOX)),
            shape((4, CIN, PLANE)),
            shape((4, CIN, PLANE)),
            shape((COUT, (SPLIT - 1) * PLANE), F32),
            shape((2, COUT, PLANE), F32),
            shape((CIN, (EDGE - SPLIT) * PLANE)),
            shape((3 * COUT, TAPS * CIN)),
        ),
        in_specs=[HBM, HBM],
        out_specs=(VMEM,) * 7,
        scratch_shapes=[
            buffer,
            pltpu.VMEM((CIN, VOX), BF),
            pltpu.VMEM((COUT, 27 * CIN), BF),
            pltpu.SemaphoreType.DMA((SLOTS * CHUNK,)),
            pltpu.SemaphoreType.DMA,
        ],
        compiler_params=params(16),
        cost_estimate=pl.CostEstimate(
            flops=2 * block_flops, bytes_accessed=4 * 2**20, transcendentals=0
        ),
    )(in_hbm(volumes), in_hbm(conv_weight))
    sent_y = pl.pallas_call(
        pack_for_y,
        out_shape=shape((SLOTS, CIN, 2 * PLANE)),
        in_specs=[VMEM, VMEM, VMEM],
        out_specs=VMEM,
        compiler_params=params(8),
    )(faces_y, far_a, far_b)
    far_y = lax.ppermute(sent_y, "gy", [(0, 1), (1, 0)])
    high_acc = pl.pallas_call(
        end_first,
        out_shape=shape((COUT, (EDGE - SPLIT + 1) * PLANE), F32),
        in_specs=[VMEM, VMEM, VMEM, ANY],
        out_specs=VMEM,
        scratch_shapes=[buffer],
        compiler_params=params(16),
        cost_estimate=pl.CostEstimate(
            flops=block_flops, bytes_accessed=2**20, transcendentals=0
        ),
    )(rest, wall, carry, sent_y)
    sent_a, sent_b = pl.pallas_call(
        pack_for_z,
        out_shape=(shape((CIN, Z_WIDTH)), shape((CIN, Z_WIDTH))),
        in_specs=[VMEM, VMEM, VMEM, VMEM],
        out_specs=(VMEM, VMEM),
        compiler_params=params(8),
    )(faces_z, far_a, far_b, far_y)
    got_a, got_b = swap(sent_a, sent_b, "gz")
    smem_links = pltpu.SMEM((SLOTS, 26), jnp.int32)
    acc_a, acc_b, walls_z = pl.pallas_call(
        finish_second,
        out_shape=(
            shape((COUT, VOX), F32), shape((COUT, VOX), F32), shape((2, COUT, TAPS * CIN))
        ),
        in_specs=[ANY, VMEM, VMEM, ANY] + [VMEM] * 9,
        out_specs=(VMEM,) * 3,
        scratch_shapes=[
            buffer,
            pltpu.VMEM((NEAR_SOURCES, CIN, PLANE), BF),
            smem_links,
            pltpu.SemaphoreType.DMA,
        ],
        compiler_params=params(16),
        cost_estimate=pl.CostEstimate(
            flops=2 * block_flops, bytes_accessed=2 * 2**20, transcendentals=0
        ),
    )(
        links, held, wall, sent_a, low_acc, high_acc, own_a, own_b, far_a, far_b, faces_y,
        far_y, faces_z,
    )
    index = jnp.arange(PLANE)
    turn = (index[:, None] == (index % EDGE * EDGE + index // EDGE)[None, :]).astype(BF)
    outputs = pl.pallas_call(
        finish,
        out_shape=shape((SLOTS, COUT, VOX)),
        in_specs=[ANY] * 2 + [VMEM] * 9,
        out_specs=HBM,
        scratch_shapes=[
            buffer,
            pltpu.VMEM((Z_SOURCES, CIN, PLANE), BF),
            pltpu.VMEM((2, COUT, PLANE), F32),
            pltpu.VMEM((SLOTS, COUT, VOX), BF),
            smem_links,
            pltpu.SMEM((1, 1, 1), jnp.int32),
            pltpu.SemaphoreType.DMA((2,)),
            pltpu.SemaphoreType.DMA((SLOTS * CHUNK,)),
        ],
        compiler_params=params(16),
    )(
        links, block_count, acc_a, acc_b, got_a, got_b, walls_z, conv_bias.reshape(1, COUT),
        head_weight, head_bias.reshape(1, COUT), turn,
    )
    return outputs.reshape(1, 1, SLOTS, COUT, VOX)


def solution(mesh):
    placed = (
        P("gx", "gz", "gy", None, None),
        P("gx", "gz", "gy"),
        P("gx", "gz", "gy", None),
        P(),
        P(),
        P(),
        P(),
    )
    return jax.shard_map(
        body, mesh=mesh, in_specs=placed, out_specs=P("gx", "gz", "gy", None, None), check_vma=False
    )
```

```python
import jax
import jax.numpy as jnp
from jax import lax
from jax.experimental import pallas as pl
from jax.experimental.pallas import tpu as pltpu
from jax.sharding import PartitionSpec as P

CIN = 96
COUT = 48
EDGE = 16
PLANE = 256
VOX = 4096
SLOTS = 2
BF = jnp.bfloat16
F32 = jnp.float32

OWN_X, FAR_X, FAR_Y, OWN_Y, EDGE_Y, NEAR_SOURCES = 0, 4, 8, 10, 14, 18
FAR_Z, EDGE_Z, TURN_Z, Z_SOURCES = 0, 4, 6, 8
Z_WIDTH = SLOTS * PLANE + 128
SPLIT = 12
CHUNK = 4


def params(mib):
    return pltpu.CompilerParams(vmem_limit_bytes=mib * 2**20)


def lanes(rows, width):
    return lax.broadcasted_iota(jnp.int32, (rows, width), 1)


def last(side):
    return EDGE - 1 if side == 0 else 0


def roll(value, shift):
    width = value.shape[1]
    if isinstance(shift, int):
        shift = shift % width
        if shift == 0:
            return value
    return pltpu.roll(value, shift, 1)


def place():
    return lax.axis_index("gx") % 2, lax.axis_index("gz") % 2, lax.axis_index("gy")


def interior(block, wall, write, first, stop, carry=None):
    lane = lanes(CIN, PLANE)
    z_of = lane % EDGE
    z_first, z_last = z_of == 0, z_of == EDGE - 1
    zero = jnp.zeros((CIN, PLANE), BF)
    lane_o = lanes(COUT, PLANE)
    y_first, y_last = lane_o < EDGE, lane_o >= PLANE - EDGE
    none = jnp.zeros((COUT, PLANE), F32)
    before, current = carry if carry is not None else (None, None)

    def join(parts):
        less = jnp.where(y_first, none, roll(parts[0], EDGE))
        more = jnp.where(y_last, none, roll(parts[2], -EDGE))
        return parts[1] + less + more

    for x in range(first, stop):
        centre = block(x)
        z_less = jnp.where(z_first, zero, roll(centre, 1))
        z_more = jnp.where(z_last, zero, roll(centre, -1))
        stack = jnp.concatenate([z_less, centre, z_more], 0)
        part = jnp.dot(wall[...], stack, preferred_element_type=F32)
        taps = [
            [part[(y * 3 + k) * COUT : (y * 3 + k + 1) * COUT] for k in range(3)] for y in range(3)
        ]
        if x > 0:
            write(x - 1, join([before[y] + taps[y][2] for y in range(3)]))
            before = [current[y] + taps[y][1] for y in range(3)]
        else:
            before = [taps[y][1] for y in range(3)]
        current = [taps[y][0] for y in range(3)]
    if stop == EDGE:
        write(EDGE - 1, join(before))
    return before, current


def write_plane(acc):
    def write(x, value):
        acc[:, x * PLANE : (x + 1) * PLANE] = value

    return write


def plane_of(block):
    return lambda x: block[:, x * PLANE : (x + 1) * PLANE]


def pack_and_convolve(blocks, weight, held, faces_y, faces_z, acc, carry, rest, wall, first, weights, sems, weight_sem):
    width = VOX // CHUNK
    copies = []
    for slot in range(SLOTS):
        for part in range(CHUNK):
            at = pl.ds(part * width, width)
            copies.append(
                pltpu.make_async_copy(
                    blocks.at[slot, :, at], (first, held)[slot].at[:, at], sems.at[slot * CHUNK + part]
                )
            )
    weight_copy = pltpu.make_async_copy(weight, weights, weight_sem)
    copies[0].start()
    weight_copy.start()
    for copy in copies[1:]:
        copy.start()
    lane = lanes(CIN, PLANE)
    half_lane = lanes(CIN, 128)
    for slot in range(SLOTS):
        planes_z = [jnp.zeros((CIN, PLANE), BF)] * 2
        halves = [[jnp.zeros((CIN, 128), BF)] * 2 for _ in range(2)]
        for x in range(EDGE):
            if x % (EDGE // CHUNK) == 0:
                copies[slot * CHUNK + x // (EDGE // CHUNK)].wait()
            centre = (first, held)[slot][:, x * PLANE : (x + 1) * PLANE]
            moved = roll(centre, x)
            planes_z[0] = jnp.where(lane % EDGE == (x + EDGE - 1) % EDGE, moved, planes_z[0])
            planes_z[1] = jnp.where(lane % EDGE == x, moved, planes_z[1])
            ends = jnp.where(half_lane < 64, centre[:, :128], centre[:, 128:])
            moved = roll(ends, (x % 8) * EDGE)
            part = x // 8
            halves[0][part] = jnp.where(half_lane // EDGE == (x + 7) % 8, moved, halves[0][part])
            halves[1][part] = jnp.where(half_lane // EDGE == x % 8, moved, halves[1][part])
        faces_z[slot] = roll(planes_z[0], 1 - EDGE)
        faces_z[2 + slot] = planes_z[1]
        for part in range(2):
            at = slice(part * 128, (part + 1) * 128)
            faces_y[slot, :, at] = roll(halves[0][part], EDGE)
            faces_y[2 + slot, :, at] = halves[1][part]
        if slot == 0:
            weight_copy.wait()
            for tap_y in range(3):
                for tap_x in range(3):
                    row = (tap_y * 3 + tap_x) * COUT
                    source = (tap_x * 3 + tap_y) * 3 * CIN
                    wall[row : row + COUT, :] = weights[:, source : source + 3 * CIN]
            before, current = interior(
                plane_of(first), wall, write_plane(acc), 0, SPLIT
            )
            for tap_y in range(3):
                carry[tap_y], carry[3 + tap_y] = before[tap_y], current[tap_y]
            rest[...] = first[:, SPLIT * PLANE :]


def end_first(rest, wall, carry, tie, acc):
    def block(x):
        return rest[:, (x - SPLIT) * PLANE : (x - SPLIT + 1) * PLANE]

    def write(x, value):
        x = x - (SPLIT - 1)
        acc[:, x * PLANE : (x + 1) * PLANE] = value

    before = [carry[k] for k in range(3)]
    current = [carry[3 + k] for k in range(3)]
    interior(block, wall, write, SPLIT, EDGE, (before, current))


def pack_for_y(faces_y, far_a, far_b, out):
    parity, _, at_y = place()
    odd_x = parity == 1
    for slot in range(SLOTS):
        out[slot, :, :PLANE] = faces_y[at_y * 2 + slot]
        start = pl.multiple_of((1 - at_y) * 128, 128)
        a = far_a[slot, :, pl.ds(start, 128)]
        b = far_b[slot, :, pl.ds(start, 128)]
        out[slot, :, PLANE : PLANE + 128] = jnp.where(odd_x, a, b)
        out[slot, :, PLANE + 128 :] = jnp.where(odd_x, b, a)


def corner_lane(k):
    return k // 2 * EDGE + 6 + k % 2


def pack_for_z(faces_z, far_a, far_b, far_y, out_a, out_b):
    parity_x, parity_z, at_y = place()
    odd_x, odd_z = parity_x == 1, parity_z == 1
    lane = lanes(CIN, PLANE)
    half_lane = lanes(CIN, 128)
    row = at_y * 112
    packs = []
    for side in range(2):
        z = last(side)
        pack = jnp.zeros((CIN, PLANE), BF)
        corner = jnp.zeros((CIN, 128), BF)
        for slot in range(SLOTS):
            a, b = far_a[slot], far_b[slot]
            pair = (jnp.where(odd_x, a, b), jnp.where(odd_x, b, a))
            for d in range(2):
                k = d * 2 + slot
                pack = jnp.where(lane % EDGE == k, roll(pair[d], k - z), pack)
                edge = far_y[slot, :, PLANE + d * 128 : PLANE + (d + 1) * 128]
                target = corner_lane(k)
                moved = pltpu.roll(edge, (target - z - row + 128) % 128, 1)
                corner = jnp.where(half_lane == target, moved, corner)
            k = 4 + slot
            pack = jnp.where(lane % EDGE == k, roll(far_y[slot, :, :PLANE], k - z), pack)
        slim = jnp.where(half_lane % EDGE < 8, pack[:, :128], roll(pack[:, 128:], 8))
        packs.append(jnp.where((half_lane % 8 >= 6) & (half_lane % EDGE < 8), corner, slim))
    first, second = packs
    out_a[:, SLOTS * PLANE :] = jnp.where(odd_z, second, first)
    out_b[:, SLOTS * PLANE :] = jnp.where(odd_z, first, second)
    for slot in range(SLOTS):
        at = slice(slot * PLANE, (slot + 1) * PLANE)
        out_a[:, at] = faces_z[parity_z * 2 + slot]
        out_b[:, at] = faces_z[(1 - parity_z) * 2 + slot]


def pick(code, choices):
    result = choices[-1][1]
    for known, value in reversed(choices[:-1]):
        result = jnp.where(code == known, value, result)
    return result


def sign(side):
    return -1 if side == 0 else 1


def link(links, slot, dx, dy, dz):
    index = (dx + 1) * 9 + (dy + 1) * 3 + dz + 1
    value = links[slot, index if index < 13 else index - 1]
    clean = jnp.maximum(value, 0)
    return value >= 0, clean // 2, clean % 2


def whole(table, present, index):
    return jnp.where(present, table[index], jnp.zeros((CIN, PLANE), BF))


def column(table, present, index, source, side):
    target = 0 if side == 0 else EDGE - 1
    moved = pltpu.roll(table[index], (target - source + PLANE) % PLANE, 1)
    return jnp.where(present, moved, jnp.zeros((CIN, PLANE), BF))


def short(table, present, index, source, target):
    start = pl.multiple_of((source // 128) * 128, 128)
    value = table[index, :, pl.ds(start, 128)]
    moved = pltpu.roll(value, (target - source % 128 + 128) % 128, 1)
    return jnp.where(present, moved, jnp.zeros((CIN, 128), BF))


def put_corner(row, side, value):
    return jnp.where(lanes(CIN, 128) == (127 if side == 0 else EDGE), value, row)


def shift_rows(part):
    lane_o = lanes(COUT, PLANE)
    none = jnp.zeros((COUT, PLANE), F32)
    less = jnp.where(lane_o < EDGE, none, roll(part[:COUT], EDGE))
    more = jnp.where(lane_o >= PLANE - EDGE, none, roll(part[2 * COUT :], -EDGE))
    return part[COUT : 2 * COUT] + less + more


def shift_lanes(part):
    lane_o = lanes(COUT, PLANE)
    none = jnp.zeros((COUT, PLANE), F32)
    less = jnp.where(lane_o % EDGE == 0, none, roll(part[:COUT], 1))
    more = jnp.where(lane_o % EDGE == EDGE - 1, none, roll(part[2 * COUT :], -1))
    return part[COUT : 2 * COUT] + less + more


def stack_lanes(centre, sides):
    lane = lanes(CIN, PLANE)
    less = jnp.where(lane % EDGE == 0, sides[0], roll(centre, 1))
    more = jnp.where(lane % EDGE == EDGE - 1, sides[1], roll(centre, -1))
    return jnp.concatenate([less, centre, more], 0)


def row_share(taps, row, side):
    stack = jnp.concatenate([roll(row, 1), row, roll(row, -1)], 0)
    share = jnp.dot(taps, stack, preferred_element_type=F32)
    half_o = lanes(COUT, 128)
    if side == 0:
        return jnp.where(half_o < EDGE, share, jnp.zeros((COUT, 128), F32))
    return jnp.where(half_o >= 112, roll(share, 112), jnp.zeros((COUT, 128), F32))


def any_of(terms):
    result = terms[0]
    for term in terms[1:]:
        result = result | term
    return result


def near(links, slot, dx, dy, dz):
    present, code, _ = link(links, slot, dx, dy, dz)
    return present & (code < 4)


def add_rows(acc, sheet, side):
    half_o = lanes(COUT, 128)
    none = jnp.zeros((COUT, 128), F32)
    for x in range(EDGE):
        part = sheet[:, (x // 8) * 128 : (x // 8 + 1) * 128]
        if side == 0:
            moved = jnp.where(half_o < EDGE, roll(part, -(x % 8) * EDGE), none)
            at = slice(x * PLANE, x * PLANE + 128)
        else:
            moved = jnp.where(half_o >= 112, roll(part, 112 - (x % 8) * EDGE), none)
            at = slice(x * PLANE + 128, (x + 1) * PLANE)
        acc[:, at] = acc[:, at] + moved


def spread(sheet, side, x):
    lane_o = lanes(COUT, PLANE)
    moved = roll(sheet, last(1 - side) - x)
    return jnp.where(lane_o % EDGE == last(1 - side), moved, jnp.zeros((COUT, PLANE), F32))


def near_x(links, table, wall, acc, slot, d):
    present, code, u = link(links, slot, sign(d), 0, 0)
    centre = whole(table, present, jnp.minimum(code, 1) * 4 + d * 2 + u)
    sides = []
    for f in range(2):
        present, code, u = link(links, slot, sign(d), 0, sign(f))
        index = jnp.minimum(code, 1) * 4 + d * 2 + u
        sides.append(column(table, present & (code < 4), index, last(f), f))
    blocks_of = [slice((y * 3 + 2 * d) * COUT, (y * 3 + 2 * d + 1) * COUT) for y in range(3)]
    taps = jnp.concatenate([wall[at, :] for at in blocks_of], 0)
    part = jnp.dot(taps, stack_lanes(centre, sides), preferred_element_type=F32)
    start = last(1 - d) * PLANE
    at = slice(start, start + PLANE)
    acc[:, at] = acc[:, at] + shift_rows(part)
    for e in range(2):
        far = 112 if e == 0 else 0

        def index_of(code, u):
            return pick(
                code,
                (
                    (0, OWN_X + d * 2 + u),
                    (1, FAR_X + d * 2 + u),
                    (2, FAR_Y + u),
                    (3, EDGE_Y + d * 2 + u),
                ),
            )

        def start_of(code):
            return pick(
                code, ((0, last(e) * EDGE), (1, last(e) * EDGE), (2, last(d) * EDGE), (3, far))
            )

        @pl.when(any_of([near(links, slot, sign(d), sign(e), dz) for dz in (-1, 0, 1)]))
        def _():
            present, code, u = link(links, slot, sign(d), sign(e), 0)
            row = short(table, present, index_of(code, u), start_of(code), 0)
            for f in range(2):
                present, code, u = link(links, slot, sign(d), sign(e), sign(f))
                target = 127 if f == 0 else EDGE
                source = start_of(code) + last(f)
                value = short(table, present & (code < 4), index_of(code, u), source, target)
                row = put_corner(row, f, value)
            half = slice(start + e * 128, start + (e + 1) * 128)
            acc[:, half] = acc[:, half] + row_share(wall[blocks_of[2 * e], :], row, e)


def near_y(links, table, wall, acc, slot, e):
    present, code, u = link(links, slot, 0, sign(e), 0)
    centre = whole(table, present, jnp.where(code == 0, OWN_Y + e * 2 + u, FAR_Y + u))
    sides = []
    for f in range(2):
        present, code, u = link(links, slot, 0, sign(e), sign(f))
        index = jnp.where(code == 0, OWN_Y + e * 2 + u, FAR_Y + u)
        sides.append(column(table, present & (code < 4), index, last(f), f))
    taps = wall[2 * e * 3 * COUT : (2 * e + 1) * 3 * COUT, :]
    part = jnp.dot(taps, stack_lanes(centre, sides), preferred_element_type=F32)
    add_rows(acc, shift_rows(part), e)


def near_z(links, faces_z, wall, acc, slot, f):
    lane = lanes(CIN, PLANE)
    zero = jnp.zeros((CIN, PLANE), BF)
    _, _, u = link(links, slot, 0, 0, sign(f))
    centre = faces_z[f * 2 + u]
    less = jnp.where(lane < EDGE, zero, roll(centre, EDGE))
    more = jnp.where(lane >= PLANE - EDGE, zero, roll(centre, -EDGE))
    taps = jnp.concatenate(
        [
            wall[tap_y * 3 * COUT : (tap_y + 1) * 3 * COUT, 2 * f * CIN : (2 * f + 1) * CIN]
            for tap_y in range(3)
        ],
        1,
    )
    stack = jnp.concatenate([less, centre, more], 0)
    sheet = shift_lanes(jnp.dot(taps, stack, preferred_element_type=F32))
    for x in range(EDGE):
        at = slice(x * PLANE, (x + 1) * PLANE)
        acc[:, at] = acc[:, at] + spread(sheet, f, x)


def finish_second(
    links_in, held, wall, tie, low_acc, high_acc, own_a, own_b, far_a, far_b, faces_y,
    far_y, faces_z, acc_a, acc_b, walls_z, table, links, sem
):
    fetch = pltpu.make_async_copy(links_in, links, sem)
    fetch.start()
    parity_x, _, _ = place()
    odd_x = parity_x == 1
    for slot in range(SLOTS):
        a, b = own_a[slot], own_b[slot]
        table[OWN_X + slot] = jnp.where(odd_x, b, a)
        table[OWN_X + 2 + slot] = jnp.where(odd_x, a, b)
        a, b = far_a[slot], far_b[slot]
        table[FAR_X + slot] = jnp.where(odd_x, a, b)
        table[FAR_X + 2 + slot] = jnp.where(odd_x, b, a)
        table[FAR_Y + slot] = far_y[slot, :, :PLANE]
        for d in range(2):
            table[OWN_Y + d * 2 + slot] = faces_y[d * 2 + slot]
            table[EDGE_Y + d * 2 + slot, :, :128] = far_y[
                slot, :, PLANE + d * 128 : PLANE + (d + 1) * 128
            ]
            table[EDGE_Y + d * 2 + slot, :, 128:] = jnp.zeros((CIN, 128), BF)
    for x in range(EDGE):
        at = slice(x * PLANE, (x + 1) * PLANE)
        if x < SPLIT - 1:
            acc_a[:, at] = low_acc[:, at]
        else:
            source = x - (SPLIT - 1)
            acc_a[:, at] = high_acc[:, source * PLANE : (source + 1) * PLANE]
    interior(plane_of(held), wall, write_plane(acc_b), 0, EDGE)
    for f in range(2):
        for tap_y in range(3):
            for tap_x in range(3):
                row = (tap_y * 3 + tap_x) * COUT
                walls_z[
                    f, tap_y * COUT : (tap_y + 1) * COUT, tap_x * CIN : (tap_x + 1) * CIN
                ] = wall[row : row + COUT, 2 * f * CIN : (2 * f + 1) * CIN]
    fetch.wait()
    accs = (acc_a, acc_b)
    steps = (-1, 0, 1)
    for slot in range(SLOTS):
        acc = accs[slot]
        for d in range(2):
            wanted = any_of(
                [near(links, slot, sign(d), dy, dz) for dy in steps for dz in steps]
            )

            @pl.when(wanted)
            def _():
                near_x(links, table, wall, acc, slot, d)

        for e in range(2):

            @pl.when(any_of([near(links, slot, 0, sign(e), dz) for dz in steps]))
            def _():
                near_y(links, table, wall, acc, slot, e)

        for f in range(2):

            @pl.when(near(links, slot, 0, 0, sign(f)))
            def _():
                near_z(links, faces_z, wall, acc, slot, f)


def far_z(links, table, walls_z, sheets, slot, f):
    present, code, u = link(links, slot, 0, 0, sign(f))
    centre = whole(table, present & (code >= 4), FAR_Z + f * 2 + u)
    sides = []
    for d in range(2):
        present, code, u = link(links, slot, sign(d), 0, sign(f))
        index = jnp.where(code == 4, FAR_Z + f * 2 + u, EDGE_Z + f)
        source = jnp.where(code == 4, last(d), d * 2 + u)
        sides.append(column(table, present & (code >= 4), index, source, d))
    part = jnp.dot(walls_z[f], stack_lanes(centre, sides), preferred_element_type=F32)
    sheets[f] = shift_rows(part)
    for e in range(2):
        terms = []
        for dx in (-1, 0, 1):
            present, code, _ = link(links, slot, dx, sign(e), sign(f))
            terms.append(present & (code >= 4))

        @pl.when(any_of(terms))
        def _():
            present, code, u = link(links, slot, 0, sign(e), sign(f))
            index = jnp.where(code == 4, FAR_Z + f * 2 + u, TURN_Z + f)
            source = jnp.where(code == 4, last(e) * EDGE, (4 + u) * EDGE)
            row = short(table, present & (code >= 4), index, source, 0)
            for d in range(2):
                present, code, u = link(links, slot, sign(d), sign(e), sign(f))
                index = jnp.where(code == 4, FAR_Z + f * 2 + u, EDGE_Z + f)
                source = pick(
                    code,
                    (
                        (4, last(e) * EDGE + last(d)),
                        (5, last(e) * EDGE + d * 2 + u),
                        (6, last(d) * EDGE + 4 + u),
                        (7, d * EDGE + 6 + u),
                    ),
                )
                target = 127 if d == 0 else EDGE
                value = short(table, present & (code >= 4), index, source, target)
                row = put_corner(row, d, value)
            half = slice(e * 128, (e + 1) * 128)
            taps = walls_z[f, 2 * e * COUT : (2 * e + 1) * COUT, :]
            sheets[f, :, half] = sheets[f, :, half] + row_share(taps, row, e)


def upright(row):
    size = row.shape[1]
    across = lax.broadcasted_iota(jnp.int32, (size, size), 1)
    down = lax.broadcasted_iota(jnp.int32, (size, size), 0)
    wide = jnp.where(across == down, jnp.broadcast_to(row, (size, size)), 0.0)
    return jnp.sum(wide, axis=1, keepdims=True)


def finish(
    links_in, count_in, acc_a, acc_b, got_a, got_b, walls_z, bias_row, head, head_bias_row, turn,
    out_far, table, sheets, out, links, count, sems, out_sems
):
    fetch_links = pltpu.make_async_copy(links_in, links, sems.at[0])
    fetch_count = pltpu.make_async_copy(count_in, count, sems.at[1])
    fetch_links.start()
    fetch_count.start()
    _, parity_z, _ = place()
    odd_z = parity_z == 1
    bias, head_bias = upright(bias_row[...]), upright(head_bias_row[...])
    weights = head[...]
    for slot in range(SLOTS):
        at = slice(slot * PLANE, (slot + 1) * PLANE)
        a, b = got_a[:, at], got_b[:, at]
        table[FAR_Z + slot] = jnp.where(odd_z, a, b)
        table[FAR_Z + 2 + slot] = jnp.where(odd_z, b, a)
    a, b = got_a[:, SLOTS * PLANE :], got_b[:, SLOTS * PLANE :]
    for f, value in enumerate((jnp.where(odd_z, a, b), jnp.where(odd_z, b, a))):
        table[EDGE_Z + f, :, :128] = value
        table[EDGE_Z + f, :, 128:] = roll(value, -8)
        table[TURN_Z + f] = jnp.dot(
            table[EDGE_Z + f], turn[...], preferred_element_type=F32
        ).astype(BF)
    fetch_links.wait()
    fetch_count.wait()
    accs = (acc_a, acc_b)
    steps = (-1, 0, 1)

    def emit(slot, total, x):
        hidden = jnp.maximum(total + bias, 0.0).astype(BF)
        mixed = jnp.dot(weights, hidden, preferred_element_type=F32) + head_bias
        out[slot, :, x * PLANE : (x + 1) * PLANE] = mixed.astype(BF)
        ship(slot, x)

    width = VOX // CHUNK

    def copy_out(slot, part):
        at = pl.ds(part * width, width)
        return pltpu.make_async_copy(
            out.at[slot, :, at], out_far.at[slot, :, at], out_sems.at[slot * CHUNK + part]
        )

    def ship(slot, x):
        if (x + 1) % (EDGE // CHUNK) == 0:
            copy_out(slot, x // (EDGE // CHUNK)).start()

    for slot in range(SLOTS):
        acc = accs[slot]
        wanted = []
        for f in range(2):
            terms = []
            for dx in steps:
                for dy in steps:
                    present, code, _ = link(links, slot, dx, dy, sign(f))
                    terms.append(present & (code >= 4))
            wanted.append(any_of(terms))
        used = slot < count[0, 0, 0]
        both = wanted[0] | wanted[1]

        @pl.when(used & both)
        def _():
            for f in range(2):

                @pl.when(wanted[f])
                def _():
                    far_z(links, table, walls_z, sheets, slot, f)

            for f in range(2):

                @pl.when(wanted[f] & jnp.logical_not(wanted[1 - f]))
                def _():
                    sheet = sheets[f]
                    for x in range(EDGE):
                        total = acc[:, x * PLANE : (x + 1) * PLANE]
                        emit(slot, total + spread(sheet, f, x), x)

            @pl.when(wanted[0] & wanted[1])
            def _():
                for x in range(EDGE):
                    total = acc[:, x * PLANE : (x + 1) * PLANE]
                    total = total + spread(sheets[0], 0, x) + spread(sheets[1], 1, x)
                    emit(slot, total, x)

        @pl.when(used & jnp.logical_not(both))
        def _():
            for x in range(EDGE):
                emit(slot, acc[:, x * PLANE : (x + 1) * PLANE], x)

        @pl.when(jnp.logical_not(used))
        def _():
            for x in range(EDGE):
                out[slot, :, x * PLANE : (x + 1) * PLANE] = jnp.zeros((COUT, PLANE), BF)
                ship(slot, x)

    for slot in range(SLOTS):
        for part in range(CHUNK):
            copy_out(slot, part).wait()


VMEM = pl.BlockSpec(memory_space=pltpu.VMEM)
HBM = pl.BlockSpec(memory_space=pltpu.HBM)
ANY = pl.BlockSpec(memory_space=pl.ANY)


def shape(dims, kind=BF):
    return jax.ShapeDtypeStruct(dims, kind)


def in_hbm(value):
    return pltpu.with_memory_space_constraint(value, pltpu.HBM)


def swap(first, second, axis):
    length = lax.axis_size(axis)
    even = [(i, i ^ 1) for i in range(length)]
    odd = []
    for i in range(length):
        partner = ((i + 1) ^ 1) - 1
        for core in range(2):
            if 0 <= partner < length:
                odd.append((i * 2 + core, partner * 2 + core))
            else:
                odd.append((i * 2 + core, i * 2 + 1 - core))
    return lax.ppermute(first, axis, even), lax.ppermute(second, (axis, "gy"), odd)


def body(blocks, block_count, neighbours, conv_weight, conv_bias, head_weight, head_bias):
    volumes = blocks.reshape(SLOTS, CIN, VOX)
    links = neighbours.reshape(SLOTS, 26)
    odd_x = lax.axis_index("gx") % 2
    far_end = VOX - PLANE
    own_a = lax.dynamic_slice_in_dim(volumes, (1 - odd_x) * far_end, PLANE, 2)
    own_b = lax.dynamic_slice_in_dim(volumes, odd_x * far_end, PLANE, 2)
    far_a, far_b = swap(own_a, own_b, "gx")
    block_flops = 2 * COUT * 27 * CIN * VOX
    held, faces_y, faces_z, low_acc, carry, rest, wall = pl.pallas_call(
        pack_and_convolve,
        out_shape=(
            shape((CIN, VOX)),
            shape((4, CIN, PLANE)),
            shape((4, CIN, PLANE)),
            shape((COUT, (SPLIT - 1) * PLANE), F32),
            shape((6, COUT, PLANE), F32),
            shape((CIN, (EDGE - SPLIT) * PLANE)),
            shape((9 * COUT, 3 * CIN)),
        ),
        in_specs=[HBM, HBM],
        out_specs=(VMEM,) * 7,
        scratch_shapes=[
            pltpu.VMEM((CIN, VOX), BF),
            pltpu.VMEM((COUT, 27 * CIN), BF),
            pltpu.SemaphoreType.DMA((SLOTS * CHUNK,)),
            pltpu.SemaphoreType.DMA,
        ],
        compiler_params=params(16),
        cost_estimate=pl.CostEstimate(
            flops=2 * block_flops, bytes_accessed=4 * 2**20, transcendentals=0
        ),
    )(in_hbm(volumes), in_hbm(conv_weight))
    sent_y = pl.pallas_call(
        pack_for_y,
        out_shape=shape((SLOTS, CIN, 2 * PLANE)),
        in_specs=[VMEM, VMEM, VMEM],
        out_specs=VMEM,
        compiler_params=params(8),
    )(faces_y, far_a, far_b)
    far_y = lax.ppermute(sent_y, "gy", [(0, 1), (1, 0)])
    high_acc = pl.pallas_call(
        end_first,
        out_shape=shape((COUT, (EDGE - SPLIT + 1) * PLANE), F32),
        in_specs=[VMEM, VMEM, VMEM, ANY],
        out_specs=VMEM,
        compiler_params=params(16),
        cost_estimate=pl.CostEstimate(
            flops=block_flops, bytes_accessed=2**20, transcendentals=0
        ),
    )(rest, wall, carry, sent_y)
    sent_a, sent_b = pl.pallas_call(
        pack_for_z,
        out_shape=(shape((CIN, Z_WIDTH)), shape((CIN, Z_WIDTH))),
        in_specs=[VMEM, VMEM, VMEM, VMEM],
        out_specs=(VMEM, VMEM),
        compiler_params=params(8),
    )(faces_z, far_a, far_b, far_y)
    got_a, got_b = swap(sent_a, sent_b, "gz")
    smem_links = pltpu.SMEM((SLOTS, 26), jnp.int32)
    acc_a, acc_b, walls_z = pl.pallas_call(
        finish_second,
        out_shape=(
            shape((COUT, VOX), F32), shape((COUT, VOX), F32), shape((2, 3 * COUT, 3 * CIN))
        ),
        in_specs=[ANY, VMEM, VMEM, ANY] + [VMEM] * 9,
        out_specs=(VMEM,) * 3,
        scratch_shapes=[
            pltpu.VMEM((NEAR_SOURCES, CIN, PLANE), BF),
            smem_links,
            pltpu.SemaphoreType.DMA,
        ],
        compiler_params=params(16),
        cost_estimate=pl.CostEstimate(
            flops=2 * block_flops, bytes_accessed=2 * 2**20, transcendentals=0
        ),
    )(
        links, held, wall, sent_a, low_acc, high_acc, own_a, own_b, far_a, far_b, faces_y,
        far_y, faces_z,
    )
    index = jnp.arange(PLANE)
    turn = (index[:, None] == (index % EDGE * EDGE + index // EDGE)[None, :]).astype(BF)
    outputs = pl.pallas_call(
        finish,
        out_shape=shape((SLOTS, COUT, VOX)),
        in_specs=[ANY] * 2 + [VMEM] * 9,
        out_specs=HBM,
        scratch_shapes=[
            pltpu.VMEM((Z_SOURCES, CIN, PLANE), BF),
            pltpu.VMEM((2, COUT, PLANE), F32),
            pltpu.VMEM((SLOTS, COUT, VOX), BF),
            smem_links,
            pltpu.SMEM((1, 1, 1), jnp.int32),
            pltpu.SemaphoreType.DMA((2,)),
            pltpu.SemaphoreType.DMA((SLOTS * CHUNK,)),
        ],
        compiler_params=params(16),
    )(
        links, block_count, acc_a, acc_b, got_a, got_b, walls_z, conv_bias.reshape(1, COUT),
        head_weight, head_bias.reshape(1, COUT), turn,
    )
    return outputs.reshape(1, 1, SLOTS, COUT, VOX)


def solution(mesh):
    placed = (
        P("gx", "gz", "gy", None, None),
        P("gx", "gz", "gy"),
        P("gx", "gz", "gy", None),
        P(),
        P(),
        P(),
        P(),
    )
    return jax.shard_map(
        body, mesh=mesh, in_specs=placed, out_specs=P("gx", "gz", "gy", None, None), check_vma=False
    )
```

```python
import jax
import jax.numpy as jnp
from jax import lax
from jax.experimental import pallas as pl
from jax.experimental.pallas import tpu as pltpu
from jax.sharding import PartitionSpec as P

CIN = 96
COUT = 48
EDGE = 16
PLANE = 256
VOX = 4096
SLOTS = 2
TAPS = 9
BF = jnp.bfloat16
F32 = jnp.float32

OWN_X, FAR_X, FAR_Y, OWN_Y, EDGE_Y, NEAR_SOURCES = 0, 4, 8, 10, 14, 18
FAR_Z, EDGE_Z, TURN_Z, Z_SOURCES = 0, 4, 6, 8
Z_WIDTH = SLOTS * PLANE + 128
SPLIT = 12
CHUNK = 4


def params(mib):
    return pltpu.CompilerParams(vmem_limit_bytes=mib * 2**20)


def lanes(rows, width):
    return lax.broadcasted_iota(jnp.int32, (rows, width), 1)


def last(side):
    return EDGE - 1 if side == 0 else 0


def roll(value, shift):
    width = value.shape[1]
    if isinstance(shift, int):
        shift = shift % width
        if shift == 0:
            return value
    return pltpu.roll(value, shift, 1)


def place():
    return lax.axis_index("gx") % 2, lax.axis_index("gz") % 2, lax.axis_index("gy")


def interior(block, wall, write, first, stop, carry=None):
    lane = lanes(CIN, PLANE)
    z_of = lane % EDGE
    z_first, z_last = z_of == 0, z_of == EDGE - 1
    zero = jnp.zeros((CIN, PLANE), BF)
    lane_o = lanes(COUT, PLANE)
    y_first, y_last = lane_o < EDGE, lane_o >= PLANE - EDGE
    none = jnp.zeros((COUT, PLANE), F32)
    before, current = carry if carry is not None else (None, None)

    def join(parts):
        less = jnp.where(y_first, none, roll(parts[0], EDGE))
        more = jnp.where(y_last, none, roll(parts[2], -EDGE))
        return parts[1] + less + more

    for x in range(first, stop):
        centre = block(x)
        z_less = jnp.where(z_first, zero, roll(centre, 1))
        z_more = jnp.where(z_last, zero, roll(centre, -1))
        stack = jnp.concatenate([z_less, centre, z_more], 0)
        part = jnp.dot(wall[...], stack, preferred_element_type=F32)
        taps = [
            [part[(y * 3 + k) * COUT : (y * 3 + k + 1) * COUT] for k in range(3)] for y in range(3)
        ]
        if x > 0:
            write(x - 1, join([before[y] + taps[y][2] for y in range(3)]))
            before = [current[y] + taps[y][1] for y in range(3)]
        else:
            before = [taps[y][1] for y in range(3)]
        current = [taps[y][0] for y in range(3)]
    if stop == EDGE:
        write(EDGE - 1, join(before))
    return before, current


def write_plane(acc):
    def write(x, value):
        acc[:, x * PLANE : (x + 1) * PLANE] = value

    return write


def plane_of(block):
    return lambda x: block[:, x * PLANE : (x + 1) * PLANE]


def pack_and_convolve(blocks, weight, held, faces_y, faces_z, acc, carry, rest, wall, weights, first, sems, weight_sem):
    width = VOX // CHUNK
    copies = []
    for slot in range(SLOTS):
        for part in range(CHUNK):
            at = pl.ds(part * width, width)
            copies.append(
                pltpu.make_async_copy(
                    blocks.at[slot, :, at], (first, held)[slot].at[:, at], sems.at[slot * CHUNK + part]
                )
            )
    weight_copy = pltpu.make_async_copy(weight, weights, weight_sem)
    copies[0].start()
    weight_copy.start()
    for copy in copies[1:]:
        copy.start()
    lane = lanes(CIN, PLANE)
    half_lane = lanes(CIN, 128)
    for slot in range(SLOTS):
        planes_z = [jnp.zeros((CIN, PLANE), BF)] * 2
        halves = [[jnp.zeros((CIN, 128), BF)] * 2 for _ in range(2)]
        for x in range(EDGE):
            if x % (EDGE // CHUNK) == 0:
                copies[slot * CHUNK + x // (EDGE // CHUNK)].wait()
            centre = (first, held)[slot][:, x * PLANE : (x + 1) * PLANE]
            moved = roll(centre, x)
            planes_z[0] = jnp.where(lane % EDGE == (x + EDGE - 1) % EDGE, moved, planes_z[0])
            planes_z[1] = jnp.where(lane % EDGE == x, moved, planes_z[1])
            ends = jnp.where(half_lane < 64, centre[:, :128], centre[:, 128:])
            moved = roll(ends, (x % 8) * EDGE)
            part = x // 8
            halves[0][part] = jnp.where(half_lane // EDGE == (x + 7) % 8, moved, halves[0][part])
            halves[1][part] = jnp.where(half_lane // EDGE == x % 8, moved, halves[1][part])
        faces_z[slot] = roll(planes_z[0], 1 - EDGE)
        faces_z[2 + slot] = planes_z[1]
        for part in range(2):
            at = slice(part * 128, (part + 1) * 128)
            faces_y[slot, :, at] = roll(halves[0][part], EDGE)
            faces_y[2 + slot, :, at] = halves[1][part]
        if slot == 0:
            weight_copy.wait()
            for tap_y in range(3):
                for tap_x in range(3):
                    row = (tap_y * 3 + tap_x) * COUT
                    source = (tap_x * 3 + tap_y) * 3 * CIN
                    wall[row : row + COUT, :] = weights[:, source : source + 3 * CIN]
            before, current = interior(
                plane_of(first), wall, write_plane(acc), 0, SPLIT
            )
            for tap_y in range(3):
                carry[tap_y], carry[3 + tap_y] = before[tap_y], current[tap_y]
            rest[...] = first[:, SPLIT * PLANE :]


def end_first(rest, wall, carry, tie, acc):
    def block(x):
        return rest[:, (x - SPLIT) * PLANE : (x - SPLIT + 1) * PLANE]

    def write(x, value):
        x = x - (SPLIT - 1)
        acc[:, x * PLANE : (x + 1) * PLANE] = value

    before = [carry[k] for k in range(3)]
    current = [carry[3 + k] for k in range(3)]
    interior(block, wall, write, SPLIT, EDGE, (before, current))


def pack_for_y(faces_y, far_a, far_b, out):
    parity, _, at_y = place()
    odd_x = parity == 1
    for slot in range(SLOTS):
        out[slot, :, :PLANE] = faces_y[at_y * 2 + slot]
        start = pl.multiple_of((1 - at_y) * 128, 128)
        a = far_a[slot, :, pl.ds(start, 128)]
        b = far_b[slot, :, pl.ds(start, 128)]
        out[slot, :, PLANE : PLANE + 128] = jnp.where(odd_x, a, b)
        out[slot, :, PLANE + 128 :] = jnp.where(odd_x, b, a)


def corner_lane(k):
    return k // 2 * EDGE + 6 + k % 2


def pack_for_z(faces_z, far_a, far_b, far_y, out_a, out_b):
    parity_x, parity_z, at_y = place()
    odd_x, odd_z = parity_x == 1, parity_z == 1
    lane = lanes(CIN, PLANE)
    half_lane = lanes(CIN, 128)
    row = at_y * 112
    packs = []
    for side in range(2):
        z = last(side)
        pack = jnp.zeros((CIN, PLANE), BF)
        corner = jnp.zeros((CIN, 128), BF)
        for slot in range(SLOTS):
            a, b = far_a[slot], far_b[slot]
            pair = (jnp.where(odd_x, a, b), jnp.where(odd_x, b, a))
            for d in range(2):
                k = d * 2 + slot
                pack = jnp.where(lane % EDGE == k, roll(pair[d], k - z), pack)
                edge = far_y[slot, :, PLANE + d * 128 : PLANE + (d + 1) * 128]
                target = corner_lane(k)
                moved = pltpu.roll(edge, (target - z - row + 128) % 128, 1)
                corner = jnp.where(half_lane == target, moved, corner)
            k = 4 + slot
            pack = jnp.where(lane % EDGE == k, roll(far_y[slot, :, :PLANE], k - z), pack)
        slim = jnp.where(half_lane % EDGE < 8, pack[:, :128], roll(pack[:, 128:], 8))
        packs.append(jnp.where((half_lane % 8 >= 6) & (half_lane % EDGE < 8), corner, slim))
    first, second = packs
    out_a[:, SLOTS * PLANE :] = jnp.where(odd_z, second, first)
    out_b[:, SLOTS * PLANE :] = jnp.where(odd_z, first, second)
    for slot in range(SLOTS):
        at = slice(slot * PLANE, (slot + 1) * PLANE)
        out_a[:, at] = faces_z[parity_z * 2 + slot]
        out_b[:, at] = faces_z[(1 - parity_z) * 2 + slot]


def pick(code, choices):
    result = choices[-1][1]
    for known, value in reversed(choices[:-1]):
        result = jnp.where(code == known, value, result)
    return result


def sign(side):
    return -1 if side == 0 else 1


def link(links, slot, dx, dy, dz):
    index = (dx + 1) * 9 + (dy + 1) * 3 + dz + 1
    value = links[slot, index if index < 13 else index - 1]
    clean = jnp.maximum(value, 0)
    return value >= 0, clean // 2, clean % 2


def whole(table, present, index):
    return jnp.where(present, table[index], jnp.zeros((CIN, PLANE), BF))


def column(table, present, index, source, side):
    target = 0 if side == 0 else EDGE - 1
    moved = pltpu.roll(table[index], (target - source + PLANE) % PLANE, 1)
    return jnp.where(present, moved, jnp.zeros((CIN, PLANE), BF))


def short(table, present, index, source, target):
    start = pl.multiple_of((source // 128) * 128, 128)
    value = table[index, :, pl.ds(start, 128)]
    moved = pltpu.roll(value, (target - source % 128 + 128) % 128, 1)
    return jnp.where(present, moved, jnp.zeros((CIN, 128), BF))


def put_corner(row, side, value):
    return jnp.where(lanes(CIN, 128) == (127 if side == 0 else EDGE), value, row)


def fill_columns(columns, buffer, centre, sides, rows):
    lane = lanes(CIN, PLANE)
    half_lane = lanes(CIN, 128)
    less = jnp.where(lane % EDGE == 0, sides[0], roll(centre, 1))
    more = jnp.where(lane % EDGE == EDGE - 1, sides[1], roll(centre, -1))
    for minor, value in enumerate((less, centre, more)):
        low, high = roll(rows[0], 1 - minor), roll(rows[1], 113 - minor)
        for major in range(3):
            start = (major * 3 + minor) * CIN
            at = slice(start, start + CIN)
            if major == 1:
                columns[buffer, at, :] = value
            elif major == 0:
                shifted = roll(value, EDGE)
                columns[buffer, at, :128] = jnp.where(half_lane < EDGE, low, shifted[:, :128])
                columns[buffer, at, 128:] = shifted[:, 128:]
            else:
                shifted = roll(value, -EDGE)
                columns[buffer, at, :128] = shifted[:, :128]
                columns[buffer, at, 128:] = jnp.where(half_lane >= 112, high, shifted[:, 128:])


def any_of(terms):
    result = terms[0]
    for term in terms[1:]:
        result = result | term
    return result


def near(links, slot, dx, dy, dz):
    present, code, _ = link(links, slot, dx, dy, dz)
    return present & (code < 4)


def add_rows(acc, sheet, side):
    half_o = lanes(COUT, 128)
    none = jnp.zeros((COUT, 128), F32)
    for x in range(EDGE):
        part = sheet[:, (x // 8) * 128 : (x // 8 + 1) * 128]
        if side == 0:
            moved = jnp.where(half_o < EDGE, roll(part, -(x % 8) * EDGE), none)
            at = slice(x * PLANE, x * PLANE + 128)
        else:
            moved = jnp.where(half_o >= 112, roll(part, 112 - (x % 8) * EDGE), none)
            at = slice(x * PLANE + 128, (x + 1) * PLANE)
        acc[:, at] = acc[:, at] + moved


def spread(sheet, side, x):
    lane_o = lanes(COUT, PLANE)
    moved = roll(sheet, last(1 - side) - x)
    return jnp.where(lane_o % EDGE == last(1 - side), moved, jnp.zeros((COUT, PLANE), F32))


def near_x(links, table, weights, columns, acc, slot, d):
    present, code, u = link(links, slot, sign(d), 0, 0)
    centre = whole(table, present, jnp.minimum(code, 1) * 4 + d * 2 + u)
    sides = []
    for f in range(2):
        present, code, u = link(links, slot, sign(d), 0, sign(f))
        index = jnp.minimum(code, 1) * 4 + d * 2 + u
        sides.append(column(table, present & (code < 4), index, last(f), f))
    rows = []
    for e in range(2):
        far = 112 if e == 0 else 0

        def index_of(code, u):
            return pick(
                code,
                (
                    (0, OWN_X + d * 2 + u),
                    (1, FAR_X + d * 2 + u),
                    (2, FAR_Y + u),
                    (3, EDGE_Y + d * 2 + u),
                ),
            )

        def start_of(code):
            return pick(
                code, ((0, last(e) * EDGE), (1, last(e) * EDGE), (2, last(d) * EDGE), (3, far))
            )

        present, code, u = link(links, slot, sign(d), sign(e), 0)
        row = short(table, present, index_of(code, u), start_of(code), 0)
        for f in range(2):
            present, code, u = link(links, slot, sign(d), sign(e), sign(f))
            target = 127 if f == 0 else EDGE
            source = start_of(code) + last(f)
            value = short(table, present & (code < 4), index_of(code, u), source, target)
            row = put_corner(row, f, value)
        rows.append(row)
    fill_columns(columns, d, centre, sides, rows)
    taps = weights[:, 2 * d * TAPS * CIN : (2 * d + 1) * TAPS * CIN]
    x = last(1 - d)
    at = slice(x * PLANE, (x + 1) * PLANE)
    acc[:, at] = acc[:, at] + jnp.dot(taps, columns[d], preferred_element_type=F32)


def near_y(links, table, wall, columns, acc, slot, e):
    lane = lanes(CIN, PLANE)
    lane_o = lanes(COUT, PLANE)
    none = jnp.zeros((COUT, PLANE), F32)
    present, code, u = link(links, slot, 0, sign(e), 0)
    centre = whole(table, present, jnp.where(code == 0, OWN_Y + e * 2 + u, FAR_Y + u))
    sides = []
    for f in range(2):
        present, code, u = link(links, slot, 0, sign(e), sign(f))
        index = jnp.where(code == 0, OWN_Y + e * 2 + u, FAR_Y + u)
        sides.append(column(table, present & (code < 4), index, last(f), f))
    columns[e, :CIN, :] = jnp.where(lane % EDGE == 0, sides[0], roll(centre, 1))
    columns[e, CIN : 2 * CIN, :] = centre
    columns[e, 2 * CIN : 3 * CIN, :] = jnp.where(lane % EDGE == EDGE - 1, sides[1], roll(centre, -1))
    taps = wall[2 * e * 3 * COUT : (2 * e + 1) * 3 * COUT, :]
    part = jnp.dot(taps, columns[e, : 3 * CIN, :], preferred_element_type=F32)
    sheet = part[COUT : 2 * COUT]
    sheet = sheet + jnp.where(lane_o < EDGE, none, roll(part[:COUT], EDGE))
    sheet = sheet + jnp.where(lane_o >= PLANE - EDGE, none, roll(part[2 * COUT :], -EDGE))
    add_rows(acc, sheet, e)


def near_z(links, faces_z, wall, columns, acc, slot, f):
    lane = lanes(CIN, PLANE)
    zero = jnp.zeros((CIN, PLANE), BF)
    lane_o = lanes(COUT, PLANE)
    none = jnp.zeros((COUT, PLANE), F32)
    _, _, u = link(links, slot, 0, 0, sign(f))
    centre = faces_z[f * 2 + u]
    columns[f, :CIN, :] = jnp.where(lane < EDGE, zero, roll(centre, EDGE))
    columns[f, CIN : 2 * CIN, :] = centre
    columns[f, 2 * CIN : 3 * CIN, :] = jnp.where(lane >= PLANE - EDGE, zero, roll(centre, -EDGE))
    taps = jnp.concatenate(
        [
            wall[tap_y * 3 * COUT : (tap_y + 1) * 3 * COUT, 2 * f * CIN : (2 * f + 1) * CIN]
            for tap_y in range(3)
        ],
        1,
    )
    part = jnp.dot(taps, columns[f, : 3 * CIN, :], preferred_element_type=F32)
    sheet = part[COUT : 2 * COUT]
    sheet = sheet + jnp.where(lane_o % EDGE == 0, none, roll(part[:COUT], 1))
    sheet = sheet + jnp.where(lane_o % EDGE == EDGE - 1, none, roll(part[2 * COUT :], -1))
    for x in range(EDGE):
        at = slice(x * PLANE, (x + 1) * PLANE)
        acc[:, at] = acc[:, at] + spread(sheet, f, x)


def finish_second(
    links_in, held, wall, weights, tie, low_acc, high_acc, own_a, own_b, far_a, far_b, faces_y,
    far_y, faces_z, acc_a, acc_b, walls_z, columns, table, links, sem
):
    fetch = pltpu.make_async_copy(links_in, links, sem)
    fetch.start()
    parity_x, _, _ = place()
    odd_x = parity_x == 1
    for slot in range(SLOTS):
        a, b = own_a[slot], own_b[slot]
        table[OWN_X + slot] = jnp.where(odd_x, b, a)
        table[OWN_X + 2 + slot] = jnp.where(odd_x, a, b)
        a, b = far_a[slot], far_b[slot]
        table[FAR_X + slot] = jnp.where(odd_x, a, b)
        table[FAR_X + 2 + slot] = jnp.where(odd_x, b, a)
        table[FAR_Y + slot] = far_y[slot, :, :PLANE]
        for d in range(2):
            table[OWN_Y + d * 2 + slot] = faces_y[d * 2 + slot]
            table[EDGE_Y + d * 2 + slot, :, :128] = far_y[
                slot, :, PLANE + d * 128 : PLANE + (d + 1) * 128
            ]
            table[EDGE_Y + d * 2 + slot, :, 128:] = jnp.zeros((CIN, 128), BF)
    for x in range(EDGE):
        at = slice(x * PLANE, (x + 1) * PLANE)
        if x < SPLIT - 1:
            acc_a[:, at] = low_acc[:, at]
        else:
            source = x - (SPLIT - 1)
            acc_a[:, at] = high_acc[:, source * PLANE : (source + 1) * PLANE]
    interior(plane_of(held), wall, write_plane(acc_b), 0, EDGE)
    for f in range(2):
        for tap_y in range(3):
            for tap_x in range(3):
                start = (tap_y * 3 + tap_x) * CIN
                row = (tap_y * 3 + tap_x) * COUT
                walls_z[f, :, start : start + CIN] = wall[
                    row : row + COUT, 2 * f * CIN : (2 * f + 1) * CIN
                ]
    fetch.wait()
    accs = (acc_a, acc_b)
    steps = (-1, 0, 1)
    for slot in range(SLOTS):
        acc = accs[slot]
        for d in range(2):
            wanted = any_of(
                [near(links, slot, sign(d), dy, dz) for dy in steps for dz in steps]
            )

            @pl.when(wanted)
            def _():
                near_x(links, table, weights, columns, acc, slot, d)

        for e in range(2):

            @pl.when(any_of([near(links, slot, 0, sign(e), dz) for dz in steps]))
            def _():
                near_y(links, table, wall, columns, acc, slot, e)

        for f in range(2):

            @pl.when(near(links, slot, 0, 0, sign(f)))
            def _():
                near_z(links, faces_z, wall, columns, acc, slot, f)


def far_z(links, table, walls_z, columns, slot, f):
    present, code, u = link(links, slot, 0, 0, sign(f))
    centre = whole(table, present & (code >= 4), FAR_Z + f * 2 + u)
    sides = []
    for d in range(2):
        present, code, u = link(links, slot, sign(d), 0, sign(f))
        index = jnp.where(code == 4, FAR_Z + f * 2 + u, EDGE_Z + f)
        source = jnp.where(code == 4, last(d), d * 2 + u)
        sides.append(column(table, present & (code >= 4), index, source, d))
    rows = []
    for e in range(2):
        present, code, u = link(links, slot, 0, sign(e), sign(f))
        index = jnp.where(code == 4, FAR_Z + f * 2 + u, TURN_Z + f)
        source = jnp.where(code == 4, last(e) * EDGE, (4 + u) * EDGE)
        row = short(table, present & (code >= 4), index, source, 0)
        for d in range(2):
            present, code, u = link(links, slot, sign(d), sign(e), sign(f))
            index = jnp.where(code == 4, FAR_Z + f * 2 + u, EDGE_Z + f)
            source = pick(
                code,
                (
                    (4, last(e) * EDGE + last(d)),
                    (5, last(e) * EDGE + d * 2 + u),
                    (6, last(d) * EDGE + 4 + u),
                    (7, d * EDGE + 6 + u),
                ),
            )
            target = 127 if d == 0 else EDGE
            value = short(table, present & (code >= 4), index, source, target)
            row = put_corner(row, d, value)
        rows.append(row)
    fill_columns(columns, f, centre, sides, rows)
    return jnp.dot(walls_z[f], columns[f], preferred_element_type=F32)


def upright(row):
    size = row.shape[1]
    across = lax.broadcasted_iota(jnp.int32, (size, size), 1)
    down = lax.broadcasted_iota(jnp.int32, (size, size), 0)
    wide = jnp.where(across == down, jnp.broadcast_to(row, (size, size)), 0.0)
    return jnp.sum(wide, axis=1, keepdims=True)


def finish(
    links_in, count_in, acc_a, acc_b, got_a, got_b, walls_z, bias_row, head, head_bias_row, turn,
    out_far, columns, table, sheets, out, links, count, sems, out_sems
):
    fetch_links = pltpu.make_async_copy(links_in, links, sems.at[0])
    fetch_count = pltpu.make_async_copy(count_in, count, sems.at[1])
    fetch_links.start()
    fetch_count.start()
    _, parity_z, _ = place()
    odd_z = parity_z == 1
    bias, head_bias = upright(bias_row[...]), upright(head_bias_row[...])
    weights = head[...]
    for slot in range(SLOTS):
        at = slice(slot * PLANE, (slot + 1) * PLANE)
        a, b = got_a[:, at], got_b[:, at]
        table[FAR_Z + slot] = jnp.where(odd_z, a, b)
        table[FAR_Z + 2 + slot] = jnp.where(odd_z, b, a)
    a, b = got_a[:, SLOTS * PLANE :], got_b[:, SLOTS * PLANE :]
    for f, value in enumerate((jnp.where(odd_z, a, b), jnp.where(odd_z, b, a))):
        table[EDGE_Z + f, :, :128] = value
        table[EDGE_Z + f, :, 128:] = roll(value, -8)
        table[TURN_Z + f] = jnp.dot(
            table[EDGE_Z + f], turn[...], preferred_element_type=F32
        ).astype(BF)
    fetch_links.wait()
    fetch_count.wait()
    accs = (acc_a, acc_b)
    steps = (-1, 0, 1)

    def emit(slot, total, x):
        hidden = jnp.maximum(total + bias, 0.0).astype(BF)
        mixed = jnp.dot(weights, hidden, preferred_element_type=F32) + head_bias
        out[slot, :, x * PLANE : (x + 1) * PLANE] = mixed.astype(BF)
        ship(slot, x)

    width = VOX // CHUNK

    def copy_out(slot, part):
        at = pl.ds(part * width, width)
        return pltpu.make_async_copy(
            out.at[slot, :, at], out_far.at[slot, :, at], out_sems.at[slot * CHUNK + part]
        )

    def ship(slot, x):
        if (x + 1) % (EDGE // CHUNK) == 0:
            copy_out(slot, x // (EDGE // CHUNK)).start()

    for slot in range(SLOTS):
        acc = accs[slot]
        wanted = []
        for f in range(2):
            terms = []
            for dx in steps:
                for dy in steps:
                    present, code, _ = link(links, slot, dx, dy, sign(f))
                    terms.append(present & (code >= 4))
            wanted.append(any_of(terms))
        used = slot < count[0, 0, 0]
        both = wanted[0] | wanted[1]

        @pl.when(used & both)
        def _():
            for f in range(2):

                @pl.when(wanted[f])
                def _():
                    sheets[f] = far_z(links, table, walls_z, columns, slot, f)

            for f in range(2):

                @pl.when(wanted[f] & jnp.logical_not(wanted[1 - f]))
                def _():
                    sheet = sheets[f]
                    for x in range(EDGE):
                        total = acc[:, x * PLANE : (x + 1) * PLANE]
                        emit(slot, total + spread(sheet, f, x), x)

            @pl.when(wanted[0] & wanted[1])
            def _():
                for x in range(EDGE):
                    total = acc[:, x * PLANE : (x + 1) * PLANE]
                    total = total + spread(sheets[0], 0, x) + spread(sheets[1], 1, x)
                    emit(slot, total, x)

        @pl.when(used & jnp.logical_not(both))
        def _():
            for x in range(EDGE):
                emit(slot, acc[:, x * PLANE : (x + 1) * PLANE], x)

        @pl.when(jnp.logical_not(used))
        def _():
            for x in range(EDGE):
                out[slot, :, x * PLANE : (x + 1) * PLANE] = jnp.zeros((COUT, PLANE), BF)
                ship(slot, x)

    for slot in range(SLOTS):
        for part in range(CHUNK):
            copy_out(slot, part).wait()


VMEM = pl.BlockSpec(memory_space=pltpu.VMEM)
HBM = pl.BlockSpec(memory_space=pltpu.HBM)
ANY = pl.BlockSpec(memory_space=pl.ANY)


def shape(dims, kind=BF):
    return jax.ShapeDtypeStruct(dims, kind)


def in_hbm(value):
    return pltpu.with_memory_space_constraint(value, pltpu.HBM)


def swap(first, second, axis):
    length = lax.axis_size(axis)
    even = [(i, i ^ 1) for i in range(length)]
    odd = []
    for i in range(length):
        partner = ((i + 1) ^ 1) - 1
        for core in range(2):
            if 0 <= partner < length:
                odd.append((i * 2 + core, partner * 2 + core))
            else:
                odd.append((i * 2 + core, i * 2 + 1 - core))
    return lax.ppermute(first, axis, even), lax.ppermute(second, (axis, "gy"), odd)


def body(blocks, block_count, neighbours, conv_weight, conv_bias, head_weight, head_bias):
    volumes = blocks.reshape(SLOTS, CIN, VOX)
    links = neighbours.reshape(SLOTS, 26)
    odd_x = lax.axis_index("gx") % 2
    far_end = VOX - PLANE
    own_a = lax.dynamic_slice_in_dim(volumes, (1 - odd_x) * far_end, PLANE, 2)
    own_b = lax.dynamic_slice_in_dim(volumes, odd_x * far_end, PLANE, 2)
    far_a, far_b = swap(own_a, own_b, "gx")
    buffer = pltpu.VMEM((2, TAPS * CIN, PLANE), BF)
    block_flops = 2 * COUT * 27 * CIN * VOX
    held, faces_y, faces_z, low_acc, carry, rest, wall, weights = pl.pallas_call(
        pack_and_convolve,
        out_shape=(
            shape((CIN, VOX)),
            shape((4, CIN, PLANE)),
            shape((4, CIN, PLANE)),
            shape((COUT, (SPLIT - 1) * PLANE), F32),
            shape((6, COUT, PLANE), F32),
            shape((CIN, (EDGE - SPLIT) * PLANE)),
            shape((9 * COUT, 3 * CIN)),
            shape((COUT, 27 * CIN)),
        ),
        in_specs=[HBM, HBM],
        out_specs=(VMEM,) * 8,
        scratch_shapes=[
            pltpu.VMEM((CIN, VOX), BF),
            pltpu.SemaphoreType.DMA((SLOTS * CHUNK,)),
            pltpu.SemaphoreType.DMA,
        ],
        compiler_params=params(16),
        cost_estimate=pl.CostEstimate(
            flops=2 * block_flops, bytes_accessed=4 * 2**20, transcendentals=0
        ),
    )(in_hbm(volumes), in_hbm(conv_weight))
    sent_y = pl.pallas_call(
        pack_for_y,
        out_shape=shape((SLOTS, CIN, 2 * PLANE)),
        in_specs=[VMEM, VMEM, VMEM],
        out_specs=VMEM,
        compiler_params=params(8),
    )(faces_y, far_a, far_b)
    far_y = lax.ppermute(sent_y, "gy", [(0, 1), (1, 0)])
    high_acc = pl.pallas_call(
        end_first,
        out_shape=shape((COUT, (EDGE - SPLIT + 1) * PLANE), F32),
        in_specs=[VMEM, VMEM, VMEM, ANY],
        out_specs=VMEM,
        compiler_params=params(16),
        cost_estimate=pl.CostEstimate(
            flops=block_flops, bytes_accessed=2**20, transcendentals=0
        ),
    )(rest, wall, carry, sent_y)
    sent_a, sent_b = pl.pallas_call(
        pack_for_z,
        out_shape=(shape((CIN, Z_WIDTH)), shape((CIN, Z_WIDTH))),
        in_specs=[VMEM, VMEM, VMEM, VMEM],
        out_specs=(VMEM, VMEM),
        compiler_params=params(8),
    )(faces_z, far_a, far_b, far_y)
    got_a, got_b = swap(sent_a, sent_b, "gz")
    smem_links = pltpu.SMEM((SLOTS, 26), jnp.int32)
    acc_a, acc_b, walls_z = pl.pallas_call(
        finish_second,
        out_shape=(
            shape((COUT, VOX), F32), shape((COUT, VOX), F32), shape((2, COUT, TAPS * CIN))
        ),
        in_specs=[ANY, VMEM, VMEM, VMEM, ANY] + [VMEM] * 9,
        out_specs=(VMEM,) * 3,
        scratch_shapes=[
            buffer,
            pltpu.VMEM((NEAR_SOURCES, CIN, PLANE), BF),
            smem_links,
            pltpu.SemaphoreType.DMA,
        ],
        compiler_params=params(16),
        cost_estimate=pl.CostEstimate(
            flops=2 * block_flops, bytes_accessed=2 * 2**20, transcendentals=0
        ),
    )(
        links, held, wall, weights, sent_a, low_acc, high_acc, own_a, own_b, far_a, far_b, faces_y,
        far_y, faces_z,
    )
    index = jnp.arange(PLANE)
    turn = (index[:, None] == (index % EDGE * EDGE + index // EDGE)[None, :]).astype(BF)
    outputs = pl.pallas_call(
        finish,
        out_shape=shape((SLOTS, COUT, VOX)),
        in_specs=[ANY] * 2 + [VMEM] * 9,
        out_specs=HBM,
        scratch_shapes=[
            buffer,
            pltpu.VMEM((Z_SOURCES, CIN, PLANE), BF),
            pltpu.VMEM((2, COUT, PLANE), F32),
            pltpu.VMEM((SLOTS, COUT, VOX), BF),
            smem_links,
            pltpu.SMEM((1, 1, 1), jnp.int32),
            pltpu.SemaphoreType.DMA((2,)),
            pltpu.SemaphoreType.DMA((SLOTS * CHUNK,)),
        ],
        compiler_params=params(16),
    )(
        links, block_count, acc_a, acc_b, got_a, got_b, walls_z, conv_bias.reshape(1, COUT),
        head_weight, head_bias.reshape(1, COUT), turn,
    )
    return outputs.reshape(1, 1, SLOTS, COUT, VOX)


def solution(mesh):
    placed = (
        P("gx", "gz", "gy", None, None),
        P("gx", "gz", "gy"),
        P("gx", "gz", "gy", None),
        P(),
        P(),
        P(),
        P(),
    )
    return jax.shard_map(
        body, mesh=mesh, in_specs=placed, out_specs=P("gx", "gz", "gy", None, None), check_vma=False
    )
```

```python
import jax
import jax.numpy as jnp
from jax import lax
from jax.experimental import pallas as pl
from jax.experimental.pallas import tpu as pltpu
from jax.sharding import PartitionSpec as P

CIN = 96
COUT = 48
EDGE = 16
PLANE = 256
VOX = 4096
SLOTS = 2
TAPS = 9
BF = jnp.bfloat16
F32 = jnp.float32

OWN_X, FAR_X, FAR_Y, OWN_Y, EDGE_Y, NEAR_SOURCES = 0, 4, 8, 10, 14, 18
FAR_Z, EDGE_Z, TURN_Z, Z_SOURCES = 0, 4, 6, 8
Z_WIDTH = SLOTS * PLANE + 128
SPLIT = 13
CHUNK = 4


def params(mib):
    return pltpu.CompilerParams(vmem_limit_bytes=mib * 2**20)


def lanes(rows, width):
    return lax.broadcasted_iota(jnp.int32, (rows, width), 1)


def last(side):
    return EDGE - 1 if side == 0 else 0


def roll(value, shift):
    width = value.shape[1]
    if isinstance(shift, int):
        shift = shift % width
        if shift == 0:
            return value
    return pltpu.roll(value, shift, 1)


def place():
    return lax.axis_index("gx") % 2, lax.axis_index("gz") % 2, lax.axis_index("gy")


def interior(block, wall, write, first, stop, carry=None):
    lane = lanes(CIN, PLANE)
    z_of = lane % EDGE
    z_first, z_last = z_of == 0, z_of == EDGE - 1
    zero = jnp.zeros((CIN, PLANE), BF)
    lane_o = lanes(COUT, PLANE)
    y_first, y_last = lane_o < EDGE, lane_o >= PLANE - EDGE
    none = jnp.zeros((COUT, PLANE), F32)
    before, current = carry if carry is not None else (None, None)

    def join(parts):
        less = jnp.where(y_first, none, roll(parts[0], EDGE))
        more = jnp.where(y_last, none, roll(parts[2], -EDGE))
        return parts[1] + less + more

    for x in range(first, stop):
        centre = block(x)
        z_less = jnp.where(z_first, zero, roll(centre, 1))
        z_more = jnp.where(z_last, zero, roll(centre, -1))
        stack = jnp.concatenate([z_less, centre, z_more], 0)
        part = jnp.dot(wall[...], stack, preferred_element_type=F32)
        taps = [
            [part[(y * 3 + k) * COUT : (y * 3 + k + 1) * COUT] for k in range(3)] for y in range(3)
        ]
        if x > 0:
            write(x - 1, join([before[y] + taps[y][2] for y in range(3)]))
            before = [current[y] + taps[y][1] for y in range(3)]
        else:
            before = [taps[y][1] for y in range(3)]
        current = [taps[y][0] for y in range(3)]
    if stop == EDGE:
        write(EDGE - 1, join(before))
    return before, current


def write_plane(acc):
    def write(x, value):
        acc[:, x * PLANE : (x + 1) * PLANE] = value

    return write


def plane_of(block):
    return lambda x: block[:, x * PLANE : (x + 1) * PLANE]


def pack_and_convolve(blocks, weight, held, faces_y, faces_z, acc, carry, rest, wall, weights, first, sems, weight_sem):
    width = VOX // CHUNK
    copies = []
    for slot in range(SLOTS):
        for part in range(CHUNK):
            at = pl.ds(part * width, width)
            copies.append(
                pltpu.make_async_copy(
                    blocks.at[slot, :, at], (first, held)[slot].at[:, at], sems.at[slot * CHUNK + part]
                )
            )
    weight_copy = pltpu.make_async_copy(weight, weights, weight_sem)
    copies[0].start()
    weight_copy.start()
    for copy in copies[1:]:
        copy.start()
    lane = lanes(CIN, PLANE)
    half_lane = lanes(CIN, 128)
    for slot in range(SLOTS):
        planes_z = [jnp.zeros((CIN, PLANE), BF)] * 2
        halves = [[jnp.zeros((CIN, 128), BF)] * 2 for _ in range(2)]
        for x in range(EDGE):
            if x % (EDGE // CHUNK) == 0:
                copies[slot * CHUNK + x // (EDGE // CHUNK)].wait()
            centre = (first, held)[slot][:, x * PLANE : (x + 1) * PLANE]
            moved = roll(centre, x)
            planes_z[0] = jnp.where(lane % EDGE == (x + EDGE - 1) % EDGE, moved, planes_z[0])
            planes_z[1] = jnp.where(lane % EDGE == x, moved, planes_z[1])
            ends = jnp.where(half_lane < 64, centre[:, :128], centre[:, 128:])
            moved = roll(ends, (x % 8) * EDGE)
            part = x // 8
            halves[0][part] = jnp.where(half_lane // EDGE == (x + 7) % 8, moved, halves[0][part])
            halves[1][part] = jnp.where(half_lane // EDGE == x % 8, moved, halves[1][part])
        faces_z[slot] = roll(planes_z[0], 1 - EDGE)
        faces_z[2 + slot] = planes_z[1]
        for part in range(2):
            at = slice(part * 128, (part + 1) * 128)
            faces_y[slot, :, at] = roll(halves[0][part], EDGE)
            faces_y[2 + slot, :, at] = halves[1][part]
        if slot == 0:
            weight_copy.wait()
            for tap_y in range(3):
                for tap_x in range(3):
                    row = (tap_y * 3 + tap_x) * COUT
                    source = (tap_x * 3 + tap_y) * 3 * CIN
                    wall[row : row + COUT, :] = weights[:, source : source + 3 * CIN]
            before, current = interior(
                plane_of(first), wall, write_plane(acc), 0, SPLIT
            )
            for tap_y in range(3):
                carry[tap_y], carry[3 + tap_y] = before[tap_y], current[tap_y]
            rest[...] = first[:, SPLIT * PLANE :]


def end_first(rest, wall, carry, tie, acc):
    def block(x):
        return rest[:, (x - SPLIT) * PLANE : (x - SPLIT + 1) * PLANE]

    def write(x, value):
        x = x - (SPLIT - 1)
        acc[:, x * PLANE : (x + 1) * PLANE] = value

    before = [carry[k] for k in range(3)]
    current = [carry[3 + k] for k in range(3)]
    interior(block, wall, write, SPLIT, EDGE, (before, current))


def pack_for_y(faces_y, far_a, far_b, out):
    parity, _, at_y = place()
    odd_x = parity == 1
    for slot in range(SLOTS):
        out[slot, :, :PLANE] = faces_y[at_y * 2 + slot]
        start = pl.multiple_of((1 - at_y) * 128, 128)
        a = far_a[slot, :, pl.ds(start, 128)]
        b = far_b[slot, :, pl.ds(start, 128)]
        out[slot, :, PLANE : PLANE + 128] = jnp.where(odd_x, a, b)
        out[slot, :, PLANE + 128 :] = jnp.where(odd_x, b, a)


def corner_lane(k):
    return k // 2 * EDGE + 6 + k % 2


def pack_for_z(faces_z, far_a, far_b, far_y, out_a, out_b):
    parity_x, parity_z, at_y = place()
    odd_x, odd_z = parity_x == 1, parity_z == 1
    lane = lanes(CIN, PLANE)
    half_lane = lanes(CIN, 128)
    row = at_y * 112
    packs = []
    for side in range(2):
        z = last(side)
        pack = jnp.zeros((CIN, PLANE), BF)
        corner = jnp.zeros((CIN, 128), BF)
        for slot in range(SLOTS):
            a, b = far_a[slot], far_b[slot]
            pair = (jnp.where(odd_x, a, b), jnp.where(odd_x, b, a))
            for d in range(2):
                k = d * 2 + slot
                pack = jnp.where(lane % EDGE == k, roll(pair[d], k - z), pack)
                edge = far_y[slot, :, PLANE + d * 128 : PLANE + (d + 1) * 128]
                target = corner_lane(k)
                moved = pltpu.roll(edge, (target - z - row + 128) % 128, 1)
                corner = jnp.where(half_lane == target, moved, corner)
            k = 4 + slot
            pack = jnp.where(lane % EDGE == k, roll(far_y[slot, :, :PLANE], k - z), pack)
        slim = jnp.where(half_lane % EDGE < 8, pack[:, :128], roll(pack[:, 128:], 8))
        packs.append(jnp.where((half_lane % 8 >= 6) & (half_lane % EDGE < 8), corner, slim))
    first, second = packs
    out_a[:, SLOTS * PLANE :] = jnp.where(odd_z, second, first)
    out_b[:, SLOTS * PLANE :] = jnp.where(odd_z, first, second)
    for slot in range(SLOTS):
        at = slice(slot * PLANE, (slot + 1) * PLANE)
        out_a[:, at] = faces_z[parity_z * 2 + slot]
        out_b[:, at] = faces_z[(1 - parity_z) * 2 + slot]


def pick(code, choices):
    result = choices[-1][1]
    for known, value in reversed(choices[:-1]):
        result = jnp.where(code == known, value, result)
    return result


def sign(side):
    return -1 if side == 0 else 1


def link(links, slot, dx, dy, dz):
    index = (dx + 1) * 9 + (dy + 1) * 3 + dz + 1
    value = links[slot, index if index < 13 else index - 1]
    clean = jnp.maximum(value, 0)
    return value >= 0, clean // 2, clean % 2


def whole(table, present, index):
    return jnp.where(present, table[index], jnp.zeros((CIN, PLANE), BF))


def column(table, present, index, source, side):
    target = 0 if side == 0 else EDGE - 1
    moved = pltpu.roll(table[index], (target - source + PLANE) % PLANE, 1)
    return jnp.where(present, moved, jnp.zeros((CIN, PLANE), BF))


def short(table, present, index, source, target):
    start = pl.multiple_of((source // 128) * 128, 128)
    value = table[index, :, pl.ds(start, 128)]
    moved = pltpu.roll(value, (target - source % 128 + 128) % 128, 1)
    return jnp.where(present, moved, jnp.zeros((CIN, 128), BF))


def put_corner(row, side, value):
    return jnp.where(lanes(CIN, 128) == (127 if side == 0 else EDGE), value, row)


def fill_columns(columns, buffer, centre, sides, rows):
    lane = lanes(CIN, PLANE)
    half_lane = lanes(CIN, 128)
    less = jnp.where(lane % EDGE == 0, sides[0], roll(centre, 1))
    more = jnp.where(lane % EDGE == EDGE - 1, sides[1], roll(centre, -1))
    for minor, value in enumerate((less, centre, more)):
        low, high = roll(rows[0], 1 - minor), roll(rows[1], 113 - minor)
        for major in range(3):
            start = (major * 3 + minor) * CIN
            at = slice(start, start + CIN)
            if major == 1:
                columns[buffer, at, :] = value
            elif major == 0:
                shifted = roll(value, EDGE)
                columns[buffer, at, :128] = jnp.where(half_lane < EDGE, low, shifted[:, :128])
                columns[buffer, at, 128:] = shifted[:, 128:]
            else:
                shifted = roll(value, -EDGE)
                columns[buffer, at, :128] = shifted[:, :128]
                columns[buffer, at, 128:] = jnp.where(half_lane >= 112, high, shifted[:, 128:])


def any_of(terms):
    result = terms[0]
    for term in terms[1:]:
        result = result | term
    return result


def near(links, slot, dx, dy, dz):
    present, code, _ = link(links, slot, dx, dy, dz)
    return present & (code < 4)


def add_rows(acc, sheet, side):
    half_o = lanes(COUT, 128)
    none = jnp.zeros((COUT, 128), F32)
    for x in range(EDGE):
        part = sheet[:, (x // 8) * 128 : (x // 8 + 1) * 128]
        if side == 0:
            moved = jnp.where(half_o < EDGE, roll(part, -(x % 8) * EDGE), none)
            at = slice(x * PLANE, x * PLANE + 128)
        else:
            moved = jnp.where(half_o >= 112, roll(part, 112 - (x % 8) * EDGE), none)
            at = slice(x * PLANE + 128, (x + 1) * PLANE)
        acc[:, at] = acc[:, at] + moved


def spread(sheet, side, x):
    lane_o = lanes(COUT, PLANE)
    moved = roll(sheet, last(1 - side) - x)
    return jnp.where(lane_o % EDGE == last(1 - side), moved, jnp.zeros((COUT, PLANE), F32))


def near_x(links, table, weights, columns, acc, slot, d):
    present, code, u = link(links, slot, sign(d), 0, 0)
    centre = whole(table, present, jnp.minimum(code, 1) * 4 + d * 2 + u)
    sides = []
    for f in range(2):
        present, code, u = link(links, slot, sign(d), 0, sign(f))
        index = jnp.minimum(code, 1) * 4 + d * 2 + u
        sides.append(column(table, present & (code < 4), index, last(f), f))
    rows = []
    for e in range(2):
        far = 112 if e == 0 else 0

        def index_of(code, u):
            return pick(
                code,
                (
                    (0, OWN_X + d * 2 + u),
                    (1, FAR_X + d * 2 + u),
                    (2, FAR_Y + u),
                    (3, EDGE_Y + d * 2 + u),
                ),
            )

        def start_of(code):
            return pick(
                code, ((0, last(e) * EDGE), (1, last(e) * EDGE), (2, last(d) * EDGE), (3, far))
            )

        present, code, u = link(links, slot, sign(d), sign(e), 0)
        row = short(table, present, index_of(code, u), start_of(code), 0)
        for f in range(2):
            present, code, u = link(links, slot, sign(d), sign(e), sign(f))
            target = 127 if f == 0 else EDGE
            source = start_of(code) + last(f)
            value = short(table, present & (code < 4), index_of(code, u), source, target)
            row = put_corner(row, f, value)
        rows.append(row)
    fill_columns(columns, d, centre, sides, rows)
    taps = weights[:, 2 * d * TAPS * CIN : (2 * d + 1) * TAPS * CIN]
    x = last(1 - d)
    at = slice(x * PLANE, (x + 1) * PLANE)
    acc[:, at] = acc[:, at] + jnp.dot(taps, columns[d], preferred_element_type=F32)


def near_y(links, table, wall, columns, acc, slot, e):
    lane = lanes(CIN, PLANE)
    lane_o = lanes(COUT, PLANE)
    none = jnp.zeros((COUT, PLANE), F32)
    present, code, u = link(links, slot, 0, sign(e), 0)
    centre = whole(table, present, jnp.where(code == 0, OWN_Y + e * 2 + u, FAR_Y + u))
    sides = []
    for f in range(2):
        present, code, u = link(links, slot, 0, sign(e), sign(f))
        index = jnp.where(code == 0, OWN_Y + e * 2 + u, FAR_Y + u)
        sides.append(column(table, present & (code < 4), index, last(f), f))
    columns[e, :CIN, :] = jnp.where(lane % EDGE == 0, sides[0], roll(centre, 1))
    columns[e, CIN : 2 * CIN, :] = centre
    columns[e, 2 * CIN : 3 * CIN, :] = jnp.where(lane % EDGE == EDGE - 1, sides[1], roll(centre, -1))
    taps = wall[2 * e * 3 * COUT : (2 * e + 1) * 3 * COUT, :]
    part = jnp.dot(taps, columns[e, : 3 * CIN, :], preferred_element_type=F32)
    sheet = part[COUT : 2 * COUT]
    sheet = sheet + jnp.where(lane_o < EDGE, none, roll(part[:COUT], EDGE))
    sheet = sheet + jnp.where(lane_o >= PLANE - EDGE, none, roll(part[2 * COUT :], -EDGE))
    add_rows(acc, sheet, e)


def near_z(links, faces_z, wall, columns, acc, slot, f):
    lane = lanes(CIN, PLANE)
    zero = jnp.zeros((CIN, PLANE), BF)
    lane_o = lanes(COUT, PLANE)
    none = jnp.zeros((COUT, PLANE), F32)
    _, _, u = link(links, slot, 0, 0, sign(f))
    centre = faces_z[f * 2 + u]
    columns[f, :CIN, :] = jnp.where(lane < EDGE, zero, roll(centre, EDGE))
    columns[f, CIN : 2 * CIN, :] = centre
    columns[f, 2 * CIN : 3 * CIN, :] = jnp.where(lane >= PLANE - EDGE, zero, roll(centre, -EDGE))
    taps = jnp.concatenate(
        [
            wall[tap_y * 3 * COUT : (tap_y + 1) * 3 * COUT, 2 * f * CIN : (2 * f + 1) * CIN]
            for tap_y in range(3)
        ],
        1,
    )
    part = jnp.dot(taps, columns[f, : 3 * CIN, :], preferred_element_type=F32)
    sheet = part[COUT : 2 * COUT]
    sheet = sheet + jnp.where(lane_o % EDGE == 0, none, roll(part[:COUT], 1))
    sheet = sheet + jnp.where(lane_o % EDGE == EDGE - 1, none, roll(part[2 * COUT :], -1))
    for x in range(EDGE):
        at = slice(x * PLANE, (x + 1) * PLANE)
        acc[:, at] = acc[:, at] + spread(sheet, f, x)


def finish_second(
    links_in, held, wall, weights, tie, low_acc, high_acc, own_a, own_b, far_a, far_b, faces_y,
    far_y, faces_z, acc_a, acc_b, walls_z, columns, table, links, sem
):
    fetch = pltpu.make_async_copy(links_in, links, sem)
    fetch.start()
    parity_x, _, _ = place()
    odd_x = parity_x == 1
    for slot in range(SLOTS):
        a, b = own_a[slot], own_b[slot]
        table[OWN_X + slot] = jnp.where(odd_x, b, a)
        table[OWN_X + 2 + slot] = jnp.where(odd_x, a, b)
        a, b = far_a[slot], far_b[slot]
        table[FAR_X + slot] = jnp.where(odd_x, a, b)
        table[FAR_X + 2 + slot] = jnp.where(odd_x, b, a)
        table[FAR_Y + slot] = far_y[slot, :, :PLANE]
        for d in range(2):
            table[OWN_Y + d * 2 + slot] = faces_y[d * 2 + slot]
            table[EDGE_Y + d * 2 + slot, :, :128] = far_y[
                slot, :, PLANE + d * 128 : PLANE + (d + 1) * 128
            ]
            table[EDGE_Y + d * 2 + slot, :, 128:] = jnp.zeros((CIN, 128), BF)
    for x in range(EDGE):
        at = slice(x * PLANE, (x + 1) * PLANE)
        if x < SPLIT - 1:
            acc_a[:, at] = low_acc[:, at]
        else:
            source = x - (SPLIT - 1)
            acc_a[:, at] = high_acc[:, source * PLANE : (source + 1) * PLANE]
    interior(plane_of(held), wall, write_plane(acc_b), 0, EDGE)
    for f in range(2):
        for tap_y in range(3):
            for tap_x in range(3):
                start = (tap_y * 3 + tap_x) * CIN
                row = (tap_y * 3 + tap_x) * COUT
                walls_z[f, :, start : start + CIN] = wall[
                    row : row + COUT, 2 * f * CIN : (2 * f + 1) * CIN
                ]
    fetch.wait()
    accs = (acc_a, acc_b)
    steps = (-1, 0, 1)
    for slot in range(SLOTS):
        acc = accs[slot]
        for d in range(2):
            wanted = any_of(
                [near(links, slot, sign(d), dy, dz) for dy in steps for dz in steps]
            )

            @pl.when(wanted)
            def _():
                near_x(links, table, weights, columns, acc, slot, d)

        for e in range(2):

            @pl.when(any_of([near(links, slot, 0, sign(e), dz) for dz in steps]))
            def _():
                near_y(links, table, wall, columns, acc, slot, e)

        for f in range(2):

            @pl.when(near(links, slot, 0, 0, sign(f)))
            def _():
                near_z(links, faces_z, wall, columns, acc, slot, f)


def far_z(links, table, walls_z, columns, slot, f):
    present, code, u = link(links, slot, 0, 0, sign(f))
    centre = whole(table, present & (code >= 4), FAR_Z + f * 2 + u)
    sides = []
    for d in range(2):
        present, code, u = link(links, slot, sign(d), 0, sign(f))
        index = jnp.where(code == 4, FAR_Z + f * 2 + u, EDGE_Z + f)
        source = jnp.where(code == 4, last(d), d * 2 + u)
        sides.append(column(table, present & (code >= 4), index, source, d))
    rows = []
    for e in range(2):
        present, code, u = link(links, slot, 0, sign(e), sign(f))
        index = jnp.where(code == 4, FAR_Z + f * 2 + u, TURN_Z + f)
        source = jnp.where(code == 4, last(e) * EDGE, (4 + u) * EDGE)
        row = short(table, present & (code >= 4), index, source, 0)
        for d in range(2):
            present, code, u = link(links, slot, sign(d), sign(e), sign(f))
            index = jnp.where(code == 4, FAR_Z + f * 2 + u, EDGE_Z + f)
            source = pick(
                code,
                (
                    (4, last(e) * EDGE + last(d)),
                    (5, last(e) * EDGE + d * 2 + u),
                    (6, last(d) * EDGE + 4 + u),
                    (7, d * EDGE + 6 + u),
                ),
            )
            target = 127 if d == 0 else EDGE
            value = short(table, present & (code >= 4), index, source, target)
            row = put_corner(row, d, value)
        rows.append(row)
    fill_columns(columns, f, centre, sides, rows)
    return jnp.dot(walls_z[f], columns[f], preferred_element_type=F32)


def upright(row):
    size = row.shape[1]
    across = lax.broadcasted_iota(jnp.int32, (size, size), 1)
    down = lax.broadcasted_iota(jnp.int32, (size, size), 0)
    wide = jnp.where(across == down, jnp.broadcast_to(row, (size, size)), 0.0)
    return jnp.sum(wide, axis=1, keepdims=True)


def finish(
    links_in, count_in, acc_a, acc_b, got_a, got_b, walls_z, bias_row, head, head_bias_row, turn,
    out_far, columns, table, sheets, out, links, count, sems, out_sems
):
    fetch_links = pltpu.make_async_copy(links_in, links, sems.at[0])
    fetch_count = pltpu.make_async_copy(count_in, count, sems.at[1])
    fetch_links.start()
    fetch_count.start()
    _, parity_z, _ = place()
    odd_z = parity_z == 1
    bias, head_bias = upright(bias_row[...]), upright(head_bias_row[...])
    weights = head[...]
    for slot in range(SLOTS):
        at = slice(slot * PLANE, (slot + 1) * PLANE)
        a, b = got_a[:, at], got_b[:, at]
        table[FAR_Z + slot] = jnp.where(odd_z, a, b)
        table[FAR_Z + 2 + slot] = jnp.where(odd_z, b, a)
    a, b = got_a[:, SLOTS * PLANE :], got_b[:, SLOTS * PLANE :]
    for f, value in enumerate((jnp.where(odd_z, a, b), jnp.where(odd_z, b, a))):
        table[EDGE_Z + f, :, :128] = value
        table[EDGE_Z + f, :, 128:] = roll(value, -8)
        table[TURN_Z + f] = jnp.dot(
            table[EDGE_Z + f], turn[...], preferred_element_type=F32
        ).astype(BF)
    fetch_links.wait()
    fetch_count.wait()
    accs = (acc_a, acc_b)
    steps = (-1, 0, 1)

    def emit(slot, total, x):
        hidden = jnp.maximum(total + bias, 0.0).astype(BF)
        mixed = jnp.dot(weights, hidden, preferred_element_type=F32) + head_bias
        out[slot, :, x * PLANE : (x + 1) * PLANE] = mixed.astype(BF)
        ship(slot, x)

    width = VOX // CHUNK

    def copy_out(slot, part):
        at = pl.ds(part * width, width)
        return pltpu.make_async_copy(
            out.at[slot, :, at], out_far.at[slot, :, at], out_sems.at[slot * CHUNK + part]
        )

    def ship(slot, x):
        if (x + 1) % (EDGE // CHUNK) == 0:
            copy_out(slot, x // (EDGE // CHUNK)).start()

    for slot in range(SLOTS):
        acc = accs[slot]
        wanted = []
        for f in range(2):
            terms = []
            for dx in steps:
                for dy in steps:
                    present, code, _ = link(links, slot, dx, dy, sign(f))
                    terms.append(present & (code >= 4))
            wanted.append(any_of(terms))
        used = slot < count[0, 0, 0]
        both = wanted[0] | wanted[1]

        @pl.when(used & both)
        def _():
            for f in range(2):

                @pl.when(wanted[f])
                def _():
                    sheets[f] = far_z(links, table, walls_z, columns, slot, f)

            for f in range(2):

                @pl.when(wanted[f] & jnp.logical_not(wanted[1 - f]))
                def _():
                    sheet = sheets[f]
                    for x in range(EDGE):
                        total = acc[:, x * PLANE : (x + 1) * PLANE]
                        emit(slot, total + spread(sheet, f, x), x)

            @pl.when(wanted[0] & wanted[1])
            def _():
                for x in range(EDGE):
                    total = acc[:, x * PLANE : (x + 1) * PLANE]
                    total = total + spread(sheets[0], 0, x) + spread(sheets[1], 1, x)
                    emit(slot, total, x)

        @pl.when(used & jnp.logical_not(both))
        def _():
            for x in range(EDGE):
                emit(slot, acc[:, x * PLANE : (x + 1) * PLANE], x)

        @pl.when(jnp.logical_not(used))
        def _():
            for x in range(EDGE):
                out[slot, :, x * PLANE : (x + 1) * PLANE] = jnp.zeros((COUT, PLANE), BF)
                ship(slot, x)

    for slot in range(SLOTS):
        for part in range(CHUNK):
            copy_out(slot, part).wait()


VMEM = pl.BlockSpec(memory_space=pltpu.VMEM)
HBM = pl.BlockSpec(memory_space=pltpu.HBM)
ANY = pl.BlockSpec(memory_space=pl.ANY)


def shape(dims, kind=BF):
    return jax.ShapeDtypeStruct(dims, kind)


def in_hbm(value):
    return pltpu.with_memory_space_constraint(value, pltpu.HBM)


def swap(first, second, axis):
    length = lax.axis_size(axis)
    even = [(i, i ^ 1) for i in range(length)]
    odd = []
    for i in range(length):
        partner = ((i + 1) ^ 1) - 1
        for core in range(2):
            if 0 <= partner < length:
                odd.append((i * 2 + core, partner * 2 + core))
            else:
                odd.append((i * 2 + core, i * 2 + 1 - core))
    return lax.ppermute(first, axis, even), lax.ppermute(second, (axis, "gy"), odd)


def body(blocks, block_count, neighbours, conv_weight, conv_bias, head_weight, head_bias):
    volumes = blocks.reshape(SLOTS, CIN, VOX)
    links = neighbours.reshape(SLOTS, 26)
    odd_x = lax.axis_index("gx") % 2
    far_end = VOX - PLANE
    own_a = lax.dynamic_slice_in_dim(volumes, (1 - odd_x) * far_end, PLANE, 2)
    own_b = lax.dynamic_slice_in_dim(volumes, odd_x * far_end, PLANE, 2)
    far_a, far_b = swap(own_a, own_b, "gx")
    buffer = pltpu.VMEM((2, TAPS * CIN, PLANE), BF)
    block_flops = 2 * COUT * 27 * CIN * VOX
    held, faces_y, faces_z, low_acc, carry, rest, wall, weights = pl.pallas_call(
        pack_and_convolve,
        out_shape=(
            shape((CIN, VOX)),
            shape((4, CIN, PLANE)),
            shape((4, CIN, PLANE)),
            shape((COUT, (SPLIT - 1) * PLANE), F32),
            shape((6, COUT, PLANE), F32),
            shape((CIN, (EDGE - SPLIT) * PLANE)),
            shape((9 * COUT, 3 * CIN)),
            shape((COUT, 27 * CIN)),
        ),
        in_specs=[HBM, HBM],
        out_specs=(VMEM,) * 8,
        scratch_shapes=[
            pltpu.VMEM((CIN, VOX), BF),
            pltpu.SemaphoreType.DMA((SLOTS * CHUNK,)),
            pltpu.SemaphoreType.DMA,
        ],
        compiler_params=params(16),
        cost_estimate=pl.CostEstimate(
            flops=2 * block_flops, bytes_accessed=4 * 2**20, transcendentals=0
        ),
    )(in_hbm(volumes), in_hbm(conv_weight))
    sent_y = pl.pallas_call(
        pack_for_y,
        out_shape=shape((SLOTS, CIN, 2 * PLANE)),
        in_specs=[VMEM, VMEM, VMEM],
        out_specs=VMEM,
        compiler_params=params(8),
    )(faces_y, far_a, far_b)
    far_y = lax.ppermute(sent_y, "gy", [(0, 1), (1, 0)])
    high_acc = pl.pallas_call(
        end_first,
        out_shape=shape((COUT, (EDGE - SPLIT + 1) * PLANE), F32),
        in_specs=[VMEM, VMEM, VMEM, ANY],
        out_specs=VMEM,
        compiler_params=params(16),
        cost_estimate=pl.CostEstimate(
            flops=block_flops, bytes_accessed=2**20, transcendentals=0
        ),
    )(rest, wall, carry, sent_y)
    sent_a, sent_b = pl.pallas_call(
        pack_for_z,
        out_shape=(shape((CIN, Z_WIDTH)), shape((CIN, Z_WIDTH))),
        in_specs=[VMEM, VMEM, VMEM, VMEM],
        out_specs=(VMEM, VMEM),
        compiler_params=params(8),
    )(faces_z, far_a, far_b, far_y)
    got_a, got_b = swap(sent_a, sent_b, "gz")
    smem_links = pltpu.SMEM((SLOTS, 26), jnp.int32)
    acc_a, acc_b, walls_z = pl.pallas_call(
        finish_second,
        out_shape=(
            shape((COUT, VOX), F32), shape((COUT, VOX), F32), shape((2, COUT, TAPS * CIN))
        ),
        in_specs=[ANY, VMEM, VMEM, VMEM, ANY] + [VMEM] * 9,
        out_specs=(VMEM,) * 3,
        scratch_shapes=[
            buffer,
            pltpu.VMEM((NEAR_SOURCES, CIN, PLANE), BF),
            smem_links,
            pltpu.SemaphoreType.DMA,
        ],
        compiler_params=params(16),
        cost_estimate=pl.CostEstimate(
            flops=2 * block_flops, bytes_accessed=2 * 2**20, transcendentals=0
        ),
    )(
        links, held, wall, weights, sent_a, low_acc, high_acc, own_a, own_b, far_a, far_b, faces_y,
        far_y, faces_z,
    )
    index = jnp.arange(PLANE)
    turn = (index[:, None] == (index % EDGE * EDGE + index // EDGE)[None, :]).astype(BF)
    outputs = pl.pallas_call(
        finish,
        out_shape=shape((SLOTS, COUT, VOX)),
        in_specs=[ANY] * 2 + [VMEM] * 9,
        out_specs=HBM,
        scratch_shapes=[
            buffer,
            pltpu.VMEM((Z_SOURCES, CIN, PLANE), BF),
            pltpu.VMEM((2, COUT, PLANE), F32),
            pltpu.VMEM((SLOTS, COUT, VOX), BF),
            smem_links,
            pltpu.SMEM((1, 1, 1), jnp.int32),
            pltpu.SemaphoreType.DMA((2,)),
            pltpu.SemaphoreType.DMA((SLOTS * CHUNK,)),
        ],
        compiler_params=params(16),
    )(
        links, block_count, acc_a, acc_b, got_a, got_b, walls_z, conv_bias.reshape(1, COUT),
        head_weight, head_bias.reshape(1, COUT), turn,
    )
    return outputs.reshape(1, 1, SLOTS, COUT, VOX)


def solution(mesh):
    placed = (
        P("gx", "gz", "gy", None, None),
        P("gx", "gz", "gy"),
        P("gx", "gz", "gy", None),
        P(),
        P(),
        P(),
        P(),
    )
    return jax.shard_map(
        body, mesh=mesh, in_specs=placed, out_specs=P("gx", "gz", "gy", None, None), check_vma=False
    )
```
